512 devices in a mesh: ctx: 32 (over x, z), tp: 16 (over y, core).
Axes of the slice: x: 4, y: 8, z: 8, core: 2. Of those that a mesh axis runs over, the one named last changes fastest.
Arguments:
- signal: bfloat16 [4096, 8192], P('tp', 'ctx'), may hold values from -6 to 6
- pre_gate: bfloat16 [4096, 8192], P('tp', 'ctx'), may hold values from -6 to 6
- post_gate: bfloat16 [4096, 8192], P('tp', 'ctx'), may hold values from -6 to 6
- filter_taps: float32 [4096, 8192], P('tp', 'ctx'), may hold values from -0.0625 to 0.0625
- skip_gain: float32 [4096], P('tp'), may hold values from -4 to 4
- out_weight: bfloat16 [4096, 4096], P('tp'), may hold values from -0.125 to 0.125
Outputs:
- projected: bfloat16 [4096, 8192], P('tp', 'ctx')
The draws below stay inside these ranges and needn't reach their ends.
All inputs are finite; a program needn't handle non-finite values.
Results may differ from the reference program's by a relative error of at most 0.027.
Values may be sent and summed in bfloat16 or wider, within the bound.
No kernel may reach another device: no remote copies, remote signals or barrier semaphores. Data moves between devices by JAX's collectives and lax.ppermute only.
A program may use at most 64 MiB of HBM per device.

```python
import jax
import jax.numpy as jnp
from jax import lax

C = 4096
D = 4096
SEQ = 8192
N_TP = 16


def strengthened(entries, key, source, target, parts, factor):
    owner, partner = [(jnp.arange(entries.shape[dim]) // (entries.shape[dim] // parts)).reshape([-1 if axis == dim else 1 for axis in range(entries.ndim)]) for dim in (source, target)]
    chosen = jax.random.permutation(key, parts)[partner]
    strong = (owner == chosen) | (owner == (partner + parts // 2) % parts)
    return jnp.where(strong, factor * entries, entries)


def levels(rng, extent, split, smallest, top_value):
    def one(position, shards_of):
        steps = jax.random.uniform(jax.random.fold_in(jax.random.fold_in(rng, 6), position), (shards_of,), jnp.float32, smallest / len(split), top_value / len(split))
        return jnp.repeat(jnp.exp(steps), extent[position] // shards_of).reshape((-1,) + (1,) * (len(extent) - position - 1))

    loudness = one(*split[0])
    for cut in split[1:]:
        loudness = loudness * one(*cut)
    return loudness


def gaussian(rng, dims, scale, reach, shards=(), held_as=jnp.bfloat16):
    gain = levels(rng, dims, shards, -0.22, 0.18) if shards else 1.0
    drawn = jax.random.normal(rng, dims, jnp.float32) * scale * gain
    return jnp.minimum(jnp.maximum(drawn, -reach), reach).astype(held_as)


def gaussian_with(rng, shape, scale, limit, shards, heavy, kind=jnp.bfloat16):
    entries = scale * jax.random.normal(rng, shape, jnp.float32)
    if shards:
        entries = entries * levels(rng, shape, shards, -0.22, 0.18)
    return jnp.clip(strengthened(entries, jax.random.fold_in(rng, 3), *heavy), -limit, limit).astype(kind)


def setup_inputs(seed: int = 0) -> dict:
    keys = jax.random.split(jax.random.key(seed), 7)
    return {
        "signal": gaussian(keys[0], (C, SEQ), 1.0, 6.0, ((0, 16), (1, 32))),
        "pre_gate": gaussian(keys[1], (C, SEQ), 1.0, 6.0, ((0, 16), (1, 32))),
        "post_gate": gaussian(keys[2], (C, SEQ), 1.0, 6.0, ((0, 16), (1, 32))),
        "filter_taps": gaussian(keys[3], (C, SEQ), SEQ ** -0.5, 0.0625, ((0, 16), (1, 32)), jnp.float32),
        "skip_gain": gaussian(keys[4], (C,), 1.0, 4.0, ((0, 16),), jnp.float32),
        "out_weight": gaussian_with(keys[5], (C, D), C ** -0.5, 0.125, ((0, 16),), (0, 1, 16, 2.0)),
    }


def reference(signal, pre_gate, post_gate, filter_taps, skip_gain, out_weight):
    gated_input = signal.astype(jnp.float32) * pre_gate.astype(jnp.float32)
    length = gated_input.shape[1]
    spectra = jnp.fft.rfft(gated_input, n=2 * length, axis=1) * jnp.fft.rfft(filter_taps, n=2 * length, axis=1)
    convolved = jnp.fft.irfft(spectra, n=2 * length, axis=1)[:, :length]
    mixed = (post_gate.astype(jnp.float32) * (convolved + skip_gain[:, None] * gated_input)).astype(jnp.bfloat16)
    width = C // N_TP

    def add_group(group, total):
        start = (group * width).astype(jnp.int32)
        weights = lax.dynamic_slice_in_dim(out_weight, start, width, 0)
        rows = lax.dynamic_slice_in_dim(mixed, start, width, 0)
        term = lax.dot_general(weights, rows, (((0,), (0,)), ((), ())), preferred_element_type=jnp.float32)
        return total + lax.optimization_barrier(term.astype(jnp.bfloat16)).astype(jnp.float32)

    summed = lax.fori_loop(0, N_TP, add_group, jnp.zeros((D, length), jnp.float32))
    return summed.astype(jnp.bfloat16)
```

```python
import math

import jax
import jax.numpy as jnp
import numpy as np
from jax import lax
from jax.sharding import Mesh
from jax.sharding import PartitionSpec as P

TP_AXES = ("quad", "pair", "core")
GROUP = ("pair", "core")


def dft_tables(blocks, tokens, channels):
    period = 2 * blocks
    total = period * tokens
    low = blocks + 1
    k1 = np.arange(low)
    i = np.arange(blocks)
    s = np.arange(tokens)
    first = 2 * np.pi * (np.outer(k1, i) % period) / period
    turn = 2 * np.pi * (np.outer(k1, s) % total) / total
    square = 2 * np.pi * (np.outer(s, s) % tokens) / tokens
    both = 2 * channels
    front = np.concatenate(
        [np.kron(np.cos(first), np.eye(both)), np.kron(-np.sin(first), np.eye(both))]
    )
    cos, sin = np.cos(square), np.sin(square)
    ahead = np.block([[cos, -sin], [sin, cos]])
    again = np.block([[cos, sin], [-sin, cos]])
    weight = np.where((k1 == 0) | (k1 == blocks), 1.0, 2.0)[:, None] / total
    back = np.concatenate(
        [
            np.kron((weight * np.cos(first)).T, np.eye(channels)),
            np.kron(-(weight * np.sin(first)).T, np.eye(channels)),
        ],
        axis=1,
    )
    matrices = [jnp.asarray(m, jnp.bfloat16) for m in (front, ahead, again, back)]
    turns = [jnp.asarray(m, jnp.float32)[:, None, :] for m in (np.cos(turn), np.sin(turn))]
    return matrices, turns


def matmul(left, right):
    return jnp.dot(left, right, preferred_element_type=jnp.float32)


def convolve(blocks_in, channels):
    blocks, both, tokens = blocks_in.shape
    (front, ahead, again, back), (turn_cos, turn_sin) = dft_tables(blocks, tokens, channels)
    low = blocks + 1
    spread = matmul(front, blocks_in.reshape(blocks * both, tokens)).reshape(2, low, both, tokens)
    real = spread[0] * turn_cos + spread[1] * turn_sin
    imag = spread[1] * turn_cos - spread[0] * turn_sin
    rows = jnp.concatenate([real, imag], axis=2).astype(jnp.bfloat16)
    spectrum = matmul(rows.reshape(low * both, 2 * tokens), ahead).reshape(
        low, 2, channels, 2, tokens
    )
    sig_real, sig_imag = spectrum[:, 0, :, 0], spectrum[:, 0, :, 1]
    tap_real, tap_imag = spectrum[:, 1, :, 0], spectrum[:, 1, :, 1]
    product = jnp.concatenate(
        [
            sig_real * tap_real - sig_imag * tap_imag,
            sig_real * tap_imag + sig_imag * tap_real,
        ],
        axis=2,
    ).astype(jnp.bfloat16)
    folded = matmul(product.reshape(low * channels, 2 * tokens), again).reshape(
        low, channels, 2, tokens
    )
    real = folded[:, :, 0] * turn_cos - folded[:, :, 1] * turn_sin
    imag = folded[:, :, 0] * turn_sin + folded[:, :, 1] * turn_cos
    rows = jnp.concatenate([real, imag], axis=0).astype(jnp.bfloat16)
    out = matmul(back, rows.reshape(2 * low * channels, tokens))
    return out.astype(jnp.bfloat16).reshape(blocks, channels, tokens)


def per_device(signal, pre_gate, post_gate, filter_taps, skip_gain, out_weight):
    channels_here, tokens_here = signal.shape
    devices = lax.axis_size("ctx")
    channels = channels_here // devices
    quads = lax.axis_size("quad")
    group = lax.axis_size("pair") * lax.axis_size("core")
    features = out_weight.shape[1]
    width = features // (quads * group)

    gated_input = signal.astype(jnp.float32) * pre_gate.astype(jnp.float32)
    send = jnp.concatenate(
        [
            gated_input.astype(jnp.bfloat16).reshape(devices, channels, tokens_here),
            filter_taps.astype(jnp.bfloat16).reshape(devices, channels, tokens_here),
        ],
        axis=1,
    )
    blocks = lax.all_to_all(send, "ctx", split_axis=0, concat_axis=0, tiled=True)

    place = lax.axis_index(GROUP)
    columns = [
        jnp.concatenate(
            [
                lax.slice_in_dim(out_weight, (q * group + t) * width, (q * group + t + 1) * width, axis=1)
                for q in range(quads)
            ],
            axis=1,
        )
        for t in range(group)
    ]

    def columns_of(target):
        chosen = columns[0]
        for t in range(1, group):
            chosen = jnp.where(target == t, columns[t], chosen)
        return chosen

    weights = [columns_of(place)] + [
        lax.ppermute(columns_of(place ^ r), GROUP, [(t, t ^ r) for t in range(group)])
        for r in range(1, group)
    ]

    convolved = lax.all_to_all(
        convolve(blocks, channels), "ctx", split_axis=0, concat_axis=0, tiled=True
    ).reshape(channels_here, tokens_here)
    mixed = (
        post_gate.astype(jnp.float32)
        * (convolved.astype(jnp.float32) + skip_gain[:, None] * gated_input)
    ).astype(jnp.bfloat16)
    gathered = lax.all_gather(mixed, GROUP, axis=0, tiled=False)
    partial = sum(
        lax.dot_general(
            weights[r],
            lax.dynamic_index_in_dim(gathered, place ^ r, 0, keepdims=False),
            (((0,), (0,)), ((), ())),
            preferred_element_type=jnp.float32,
        )
        for r in range(group)
    )
    shares = lax.all_to_all(
        partial.astype(jnp.bfloat16).reshape(quads, width, tokens_here),
        "quad",
        split_axis=0,
        concat_axis=0,
        tiled=True,
    )
    return jnp.sum(shares.astype(jnp.float32), axis=0).astype(jnp.bfloat16)


def solution(mesh):
    ctx, tp = mesh.devices.shape
    fine = Mesh(mesh.devices.reshape(ctx, tp // 4, 2, 2), ("ctx",) + TP_AXES)
    return jax.shard_map(
        per_device,
        mesh=fine,
        in_specs=(
            P(TP_AXES, "ctx"),
            P(TP_AXES, "ctx"),
            P(TP_AXES, "ctx"),
            P(TP_AXES, "ctx"),
            P(TP_AXES),
            P(TP_AXES, None),
        ),
        out_specs=P(TP_AXES, "ctx"),
        check_vma=False,
    )
```

```python
import math

import jax
import jax.numpy as jnp
import numpy as np
from jax import lax
from jax.experimental import pallas as pl
from jax.experimental.pallas import tpu as pltpu
from jax.sharding import Mesh
from jax.sharding import PartitionSpec as P

TP_AXES = ("quad", "pair", "core")
GROUP = ("pair", "core")
MIB = 1 << 20


def targets_of(quad, pair, core, quads):
    onward = jnp.where(pair == 1, 1, -1)
    chips = [
        ((quad + 2 * onward) % quads, 1 - pair),
        ((quad + onward) % quads, pair),
        ((quad + onward) % quads, 1 - pair),
        (quad, pair),
    ]
    return [(q * 2 + p) * 2 + core for q, p in chips]


def send_to_target(share, step, quads):
    pairs = []
    for quad in range(quads):
        for pair in range(2):
            onward = 1 if pair == 1 else -1
            q = (quad + (2 * onward if step == 0 else onward)) % quads
            p = pair if step == 1 else 1 - pair
            pairs += [((quad * 2 + pair) * 2 + c, (q * 2 + p) * 2 + c) for c in range(2)]
    return lax.ppermute(share, TP_AXES, pairs)


def arrange_kernel(group, width, order_ref, weight_ref, *out_refs):
    for r in range(group):
        for i in range(group):
            start = pl.multiple_of(order_ref[r * group + i] * width, width)
            out_refs[r][i * width : (i + 1) * width, :] = weight_ref[:, pl.ds(start, width)].T
    out_refs[group][0] = order_ref[0]


def arrange(out_weight, order, group, width):
    rows = out_weight.shape[0]
    piece = jax.ShapeDtypeStruct((group * width, rows), out_weight.dtype)
    return pl.pallas_call(
        lambda *refs: arrange_kernel(group, width, *refs),
        out_shape=[piece] * group + [jax.ShapeDtypeStruct((1,), jnp.int32)],
        in_specs=[
            pl.BlockSpec(memory_space=pltpu.SMEM),
            pl.BlockSpec(memory_space=pltpu.VMEM),
        ],
        out_specs=[pl.BlockSpec(memory_space=pltpu.VMEM)] * group
        + [pl.BlockSpec(memory_space=pltpu.SMEM)],
        compiler_params=pltpu.CompilerParams(vmem_limit_bytes=16 * MIB),
        cost_estimate=pl.CostEstimate(
            flops=0, bytes_accessed=4 * rows * group * group * width, transcendentals=0
        ),
    )(order, out_weight)


def project_kernel(group, place_ref, mixed_ref, *refs):
    weight_refs, out_refs = refs[:group], refs[group:]
    rows = mixed_ref.shape[0] // group
    width = out_refs[0].shape[0]
    mixed = [
        mixed_ref[pl.ds(pl.multiple_of((place_ref[0] ^ r) * rows, rows), rows), :]
        for r in range(group)
    ]
    for i in range(group):
        total = None
        for r in range(group):
            term = jnp.dot(
                weight_refs[r][i * width : (i + 1) * width, :],
                mixed[r],
                preferred_element_type=jnp.float32,
            )
            total = term if total is None else total + term
        out_refs[i][...] = total.astype(out_refs[i].dtype)


def project(place, mixed, weights, width):
    group = len(weights)
    tokens = mixed.shape[1]
    share = jax.ShapeDtypeStruct((width, tokens), mixed.dtype)
    return pl.pallas_call(
        lambda *refs: project_kernel(group, *refs),
        out_shape=[share] * group,
        in_specs=[pl.BlockSpec(memory_space=pltpu.SMEM)]
        + [pl.BlockSpec(memory_space=pltpu.VMEM)] * (1 + group),
        out_specs=[pl.BlockSpec(memory_space=pltpu.VMEM)] * group,
        compiler_params=pltpu.CompilerParams(vmem_limit_bytes=16 * MIB),
        cost_estimate=pl.CostEstimate(
            flops=2 * mixed.size * group * width,
            bytes_accessed=2 * (mixed.size + sum(w.size for w in weights) + group * share.size),
            transcendentals=0,
        ),
    )(place, mixed, *weights)


def dft_tables(blocks, tokens, channels):
    period = 2 * blocks
    total = period * tokens
    low = blocks + 1
    k1 = np.arange(low)
    i = np.arange(blocks)
    s = np.arange(tokens)
    first = 2 * np.pi * (np.outer(k1, i) % period) / period
    turn = 2 * np.pi * (np.outer(k1, s) % total) / total
    square = 2 * np.pi * (np.outer(s, s) % tokens) / tokens
    both = 2 * channels
    front = np.concatenate(
        [np.kron(np.cos(first), np.eye(both)), np.kron(-np.sin(first), np.eye(both))]
    )
    weight = np.where((k1 == 0) | (k1 == blocks), 1.0, 2.0)[:, None] / total
    back = np.concatenate(
        [
            np.kron((weight * np.cos(first)).T, np.eye(channels)),
            np.kron(-(weight * np.sin(first)).T, np.eye(channels)),
        ],
        axis=1,
    )
    matrices = [jnp.asarray(m, jnp.bfloat16) for m in (front, np.cos(square), np.sin(square), back)]
    turns = [jnp.asarray(m, jnp.float32) for m in (np.cos(turn), np.sin(turn))]
    return matrices, turns


def matmul(left, right):
    return jnp.dot(left, right, preferred_element_type=jnp.float32)


def convolve_kernel(
    channels, in_ref, front_ref, square_cos_ref, square_sin_ref, back_ref, cos_ref, sin_ref, after_ref, out_ref
):
    del after_ref
    low, tokens = cos_ref.shape
    both = 2 * channels
    turn_cos = cos_ref[...].reshape(low, 1, tokens)
    turn_sin = sin_ref[...].reshape(low, 1, tokens)
    spread = matmul(front_ref[...], in_ref[...])
    real = spread[: low * both].reshape(low, both, tokens)
    imag = spread[low * both :].reshape(low, both, tokens)
    turned_real = (real * turn_cos + imag * turn_sin).reshape(low * both, tokens).astype(jnp.bfloat16)
    turned_imag = (imag * turn_cos - real * turn_sin).reshape(low * both, tokens).astype(jnp.bfloat16)
    square_cos, square_sin = square_cos_ref[...], square_sin_ref[...]
    real = (matmul(turned_real, square_cos) + matmul(turned_imag, square_sin)).reshape(low, both, tokens)
    imag = (matmul(turned_imag, square_cos) - matmul(turned_real, square_sin)).reshape(low, both, tokens)
    sig_real, tap_real = real[:, :channels], real[:, channels:]
    sig_imag, tap_imag = imag[:, :channels], imag[:, channels:]
    prod_real = sig_real * tap_real - sig_imag * tap_imag
    prod_imag = sig_real * tap_imag + sig_imag * tap_real
    prod_real = prod_real.reshape(low * channels, tokens).astype(jnp.bfloat16)
    prod_imag = prod_imag.reshape(low * channels, tokens).astype(jnp.bfloat16)
    real = matmul(prod_real, square_cos) - matmul(prod_imag, square_sin)
    imag = matmul(prod_imag, square_cos) + matmul(prod_real, square_sin)
    real, imag = real.reshape(low, channels, tokens), imag.reshape(low, channels, tokens)
    rows = jnp.concatenate(
        [real * turn_cos - imag * turn_sin, real * turn_sin + imag * turn_cos], axis=0
    )
    out_ref[...] = matmul(
        back_ref[...], rows.reshape(2 * low * channels, tokens).astype(jnp.bfloat16)
    ).astype(out_ref.dtype)


def convolve(blocks_in, channels, after):
    blocks, both, tokens = blocks_in.shape
    matrices, turns = dft_tables(blocks, tokens, channels)
    out = pl.pallas_call(
        lambda *refs: convolve_kernel(channels, *refs),
        out_shape=jax.ShapeDtypeStruct((blocks * channels, tokens), jnp.bfloat16),
        in_specs=[pl.BlockSpec(memory_space=pltpu.VMEM)] * 7 + [pl.BlockSpec(memory_space=pltpu.SMEM)],
        out_specs=pl.BlockSpec(memory_space=pltpu.VMEM),
        compiler_params=pltpu.CompilerParams(vmem_limit_bytes=32 * MIB),
        cost_estimate=pl.CostEstimate(
            flops=800_000_000, bytes_accessed=3_000_000, transcendentals=0
        ),
    )(blocks_in.reshape(blocks * both, tokens), *matrices, *turns, after)
    return out.reshape(blocks, channels, tokens)


def outgoing_kernel(devices, signal_ref, gate_ref, taps_ref, out_ref):
    rows, tokens = signal_ref.shape
    gated = signal_ref[...].astype(jnp.float32) * gate_ref[...].astype(jnp.float32)
    both = jnp.concatenate(
        [
            gated.reshape(devices, rows // devices, tokens),
            taps_ref[...].reshape(devices, rows // devices, tokens),
        ],
        axis=1,
    )
    out_ref[...] = both.reshape(2 * rows, tokens).astype(out_ref.dtype)


def outgoing(signal, pre_gate, filter_taps, devices):
    rows, tokens = signal.shape
    out = pl.pallas_call(
        lambda *refs: outgoing_kernel(devices, *refs),
        out_shape=jax.ShapeDtypeStruct((2 * rows, tokens), jnp.bfloat16),
        in_specs=[pl.BlockSpec(memory_space=pltpu.VMEM)] * 3,
        out_specs=pl.BlockSpec(memory_space=pltpu.VMEM),
    )(signal, pre_gate, filter_taps)
    return out.reshape(devices, 2 * rows // devices, tokens)


def per_device(signal, pre_gate, post_gate, filter_taps, skip_gain, out_weight):
    channels_here, tokens_here = signal.shape
    devices = lax.axis_size("ctx")
    channels = channels_here // devices
    quads = lax.axis_size("quad")
    group = lax.axis_size("pair") * lax.axis_size("core")
    features = out_weight.shape[1]
    width = features // (quads * group)

    send = outgoing(signal, pre_gate, filter_taps, devices)
    blocks = lax.all_to_all(send, "ctx", split_axis=0, concat_axis=0, tiled=True)

    quad, pair, core = (lax.axis_index(axis) for axis in TP_AXES)
    place = pair * 2 + core
    order = [
        index
        for r in range(group)
        for index in targets_of(quad, pair ^ (r >> 1), core ^ (r & 1), quads)
    ]
    *weights, arranged = arrange(out_weight, jnp.stack(order).astype(jnp.int32), group, width)
    weights = [weights[0]] + [
        lax.ppermute(weights[r], GROUP, [(t, t ^ r) for t in range(group)])
        for r in range(1, group)
    ]

    convolved = lax.all_to_all(
        convolve(blocks, channels, arranged), "ctx", split_axis=0, concat_axis=0, tiled=True
    ).reshape(channels_here, tokens_here)
    gated_input = signal.astype(jnp.float32) * pre_gate.astype(jnp.float32)
    mixed = (
        post_gate.astype(jnp.float32)
        * (convolved.astype(jnp.float32) + skip_gain[:, None] * gated_input)
    ).astype(jnp.bfloat16)
    gathered = lax.all_gather(mixed, GROUP, axis=0, tiled=True)
    shares = project(place.astype(jnp.int32).reshape(1), gathered, weights, width)
    shares = [send_to_target(shares[step], step, quads) for step in range(3)] + [shares[3]]
    return sum(share.astype(jnp.float32) for share in shares).astype(jnp.bfloat16)


def solution(mesh):
    ctx, tp = mesh.devices.shape
    fine = Mesh(mesh.devices.reshape(ctx, tp // 4, 2, 2), ("ctx",) + TP_AXES)
    return jax.shard_map(
        per_device,
        mesh=fine,
        in_specs=(
            P(TP_AXES, "ctx"),
            P(TP_AXES, "ctx"),
            P(TP_AXES, "ctx"),
            P(TP_AXES, "ctx"),
            P(TP_AXES),
            P(TP_AXES, None),
        ),
        out_specs=P(TP_AXES, "ctx"),
        check_vma=False,
    )
```

```python
import math

import jax
import jax.numpy as jnp
import numpy as np
from jax import lax
from jax.experimental import pallas as pl
from jax.experimental.pallas import tpu as pltpu
from jax.sharding import Mesh
from jax.sharding import PartitionSpec as P

TP_AXES = ("quad", "pair", "core")
GROUP = ("pair", "core")
MIB = 1 << 20


def targets_of(quad, pair, core, quads):
    onward = jnp.where(pair == 1, 1, -1)
    chips = [
        ((quad + 2 * onward) % quads, 1 - pair),
        ((quad + onward) % quads, pair),
        ((quad + onward) % quads, 1 - pair),
        (quad, pair),
    ]
    return [(q * 2 + p) * 2 + core for q, p in chips]


def send_to_target(share, step, quads):
    pairs = []
    for quad in range(quads):
        for pair in range(2):
            onward = 1 if pair == 1 else -1
            q = (quad + (2 * onward if step == 0 else onward)) % quads
            p = pair if step == 1 else 1 - pair
            pairs += [((quad * 2 + pair) * 2 + c, (q * 2 + p) * 2 + c) for c in range(2)]
    return lax.ppermute(share, TP_AXES, pairs)


def arrange_kernel(group, width, order_ref, weight_ref, *refs):
    out_refs, done_ref, blocks, sems = refs[:group], refs[group], refs[group + 1], refs[group + 2]
    loads = []
    for n in range(group * group):
        start = pl.multiple_of(order_ref[n] * width, width)
        loads.append(
            pltpu.make_async_copy(
                weight_ref.at[:, pl.ds(start, width)], blocks.at[n], sems.at[n]
            )
        )
    for load in loads:
        load.start()
    for n, load in enumerate(loads):
        load.wait()
        r, i = divmod(n, group)
        out_refs[r][i * width : (i + 1) * width, :] = blocks[n].T
    done_ref[0] = order_ref[0]


def arrange(out_weight, order, group, width):
    rows = out_weight.shape[0]
    piece = jax.ShapeDtypeStruct((group * width, rows), out_weight.dtype)
    return pl.pallas_call(
        lambda *refs: arrange_kernel(group, width, *refs),
        out_shape=[piece] * group + [jax.ShapeDtypeStruct((1,), jnp.int32)],
        in_specs=[
            pl.BlockSpec(memory_space=pltpu.SMEM),
            pl.BlockSpec(memory_space=pltpu.HBM),
        ],
        out_specs=[pl.BlockSpec(memory_space=pltpu.VMEM)] * group
        + [pl.BlockSpec(memory_space=pltpu.SMEM)],
        scratch_shapes=[
            pltpu.VMEM((group * group, rows, width), out_weight.dtype),
            pltpu.SemaphoreType.DMA((group * group,)),
        ],
        compiler_params=pltpu.CompilerParams(vmem_limit_bytes=60 * MIB),
        cost_estimate=pl.CostEstimate(
            flops=0, bytes_accessed=4 * rows * group * group * width, transcendentals=0
        ),
    )(order, out_weight)


def project_kernel(group, place_ref, mixed_ref, *refs):
    weight_refs, out_refs = refs[:group], refs[group:]
    rows = mixed_ref.shape[0] // group
    width = out_refs[0].shape[0]
    mixed = [
        mixed_ref[pl.ds(pl.multiple_of((place_ref[0] ^ r) * rows, rows), rows), :]
        for r in range(group)
    ]
    for i in range(group):
        total = None
        for r in range(group):
            term = jnp.dot(
                weight_refs[r][i * width : (i + 1) * width, :],
                mixed[r],
                preferred_element_type=jnp.float32,
            )
            total = term if total is None else total + term
        out_refs[i][...] = total.astype(out_refs[i].dtype)


def project(place, mixed, weights, width):
    group = len(weights)
    tokens = mixed.shape[1]
    share = jax.ShapeDtypeStruct((width, tokens), mixed.dtype)
    return pl.pallas_call(
        lambda *refs: project_kernel(group, *refs),
        out_shape=[share] * group,
        in_specs=[pl.BlockSpec(memory_space=pltpu.SMEM)]
        + [pl.BlockSpec(memory_space=pltpu.VMEM)] * (1 + group),
        out_specs=[pl.BlockSpec(memory_space=pltpu.VMEM)] * group,
        compiler_params=pltpu.CompilerParams(vmem_limit_bytes=10 * MIB),
        cost_estimate=pl.CostEstimate(
            flops=2 * mixed.size * group * width,
            bytes_accessed=2 * (mixed.size + sum(w.size for w in weights) + group * share.size),
            transcendentals=0,
        ),
    )(place, mixed, *weights)


def dft_tables(blocks, tokens, channels):
    period = 2 * blocks
    total = period * tokens
    low = blocks + 1
    k1 = np.arange(low)
    i = np.arange(blocks)
    s = np.arange(tokens)
    first = 2 * np.pi * (np.outer(k1, i) % period) / period
    turn = 2 * np.pi * (np.outer(k1, s) % total) / total
    square = 2 * np.pi * (np.outer(s, s) % tokens) / tokens
    front = np.concatenate([np.cos(first), -np.sin(first)])
    weight = np.where((k1 == 0) | (k1 == blocks), 1.0, 2.0)[:, None] / total
    back = np.concatenate(
        [
            np.kron((weight * np.cos(first)).T, np.eye(channels)),
            np.kron(-(weight * np.sin(first)).T, np.eye(channels)),
        ],
        axis=1,
    )
    matrices = [jnp.asarray(m, jnp.bfloat16) for m in (front, np.cos(square), np.sin(square), back)]
    turns = [jnp.asarray(m, jnp.float32) for m in (np.cos(turn), np.sin(turn))]
    return matrices + turns


def matmul(left, right):
    return jnp.dot(left, right, preferred_element_type=jnp.float32)


def convolve_kernel(
    channels, in_ref, front_ref, square_cos_ref, square_sin_ref, back_ref, cos_ref, sin_ref, after_ref, out_ref
):
    del after_ref
    low, tokens = cos_ref.shape
    both = 2 * channels
    turn_cos = cos_ref[...].reshape(low, 1, tokens)
    turn_sin = sin_ref[...].reshape(low, 1, tokens)
    blocks = front_ref.shape[1]
    width = blocks * both
    repeat = lax.broadcasted_iota(jnp.int32, (blocks, width), 1) // both
    repeat = (repeat == lax.broadcasted_iota(jnp.int32, (blocks, width), 0)).astype(jnp.bfloat16)
    agree = lax.broadcasted_iota(jnp.int32, (both, width), 1) % both
    agree = agree == lax.broadcasted_iota(jnp.int32, (both, width), 0)
    entries = matmul(front_ref[...], repeat).reshape(2 * low, 1, width)
    front = jnp.where(agree[None], entries, 0.0).reshape(2 * low * both, width)
    spread = matmul(front.astype(jnp.bfloat16), in_ref[...])
    real = spread[: low * both].reshape(low, both, tokens)
    imag = spread[low * both :].reshape(low, both, tokens)
    turned_real = (real * turn_cos + imag * turn_sin).reshape(low * both, tokens).astype(jnp.bfloat16)
    turned_imag = (imag * turn_cos - real * turn_sin).reshape(low * both, tokens).astype(jnp.bfloat16)
    square_cos, square_sin = square_cos_ref[...], square_sin_ref[...]
    real = (matmul(turned_real, square_cos) + matmul(turned_imag, square_sin)).reshape(low, both, tokens)
    imag = (matmul(turned_imag, square_cos) - matmul(turned_real, square_sin)).reshape(low, both, tokens)
    sig_real, tap_real = real[:, :channels], real[:, channels:]
    sig_imag, tap_imag = imag[:, :channels], imag[:, channels:]
    prod_real = sig_real * tap_real - sig_imag * tap_imag
    prod_imag = sig_real * tap_imag + sig_imag * tap_real
    prod_real = prod_real.reshape(low * channels, tokens).astype(jnp.bfloat16)
    prod_imag = prod_imag.reshape(low * channels, tokens).astype(jnp.bfloat16)
    real = matmul(prod_real, square_cos) - matmul(prod_imag, square_sin)
    imag = matmul(prod_imag, square_cos) + matmul(prod_real, square_sin)
    real, imag = real.reshape(low, channels, tokens), imag.reshape(low, channels, tokens)
    rows = jnp.concatenate(
        [real * turn_cos - imag * turn_sin, real * turn_sin + imag * turn_cos], axis=0
    )
    out_ref[...] = matmul(
        back_ref[...], rows.reshape(2 * low * channels, tokens).astype(jnp.bfloat16)
    ).astype(out_ref.dtype)


def convolve(blocks_in, channels, tables, after):
    blocks, both, tokens = blocks_in.shape
    out = pl.pallas_call(
        lambda *refs: convolve_kernel(channels, *refs),
        out_shape=jax.ShapeDtypeStruct((blocks * channels, tokens), jnp.bfloat16),
        in_specs=[pl.BlockSpec(memory_space=pltpu.VMEM)] * (1 + len(tables))
        + [pl.BlockSpec(memory_space=pltpu.SMEM)],
        out_specs=pl.BlockSpec(memory_space=pltpu.VMEM),
        compiler_params=pltpu.CompilerParams(vmem_limit_bytes=32 * MIB),
        cost_estimate=pl.CostEstimate(
            flops=800_000_000, bytes_accessed=3_000_000, transcendentals=0
        ),
    )(blocks_in.reshape(blocks * both, tokens), *tables, after)
    return out.reshape(blocks, channels, tokens)


def outgoing_kernel(devices, signal_hbm, gate_hbm, taps_hbm, out_ref, signal_ref, gate_ref, taps_ref, sems):
    copies = [
        pltpu.make_async_copy(source, target, sems.at[n])
        for n, (source, target) in enumerate(
            [(signal_hbm, signal_ref), (gate_hbm, gate_ref), (taps_hbm, taps_ref)]
        )
    ]
    for copy in copies:
        copy.start()
    for copy in copies:
        copy.wait()
    rows, tokens = signal_ref.shape
    gated = signal_ref[...].astype(jnp.float32) * gate_ref[...].astype(jnp.float32)
    both = jnp.concatenate(
        [
            gated.reshape(devices, rows // devices, tokens),
            taps_ref[...].reshape(devices, rows // devices, tokens),
        ],
        axis=1,
    )
    out_ref[...] = both.reshape(2 * rows, tokens).astype(out_ref.dtype)


def outgoing(signal, pre_gate, filter_taps, devices):
    rows, tokens = signal.shape
    out = pl.pallas_call(
        lambda *refs: outgoing_kernel(devices, *refs),
        out_shape=jax.ShapeDtypeStruct((2 * rows, tokens), jnp.bfloat16),
        in_specs=[pl.BlockSpec(memory_space=pltpu.HBM)] * 3,
        out_specs=pl.BlockSpec(memory_space=pltpu.VMEM),
        scratch_shapes=[
            pltpu.VMEM(signal.shape, signal.dtype),
            pltpu.VMEM(pre_gate.shape, pre_gate.dtype),
            pltpu.VMEM(filter_taps.shape, filter_taps.dtype),
            pltpu.SemaphoreType.DMA((3,)),
        ],
        compiler_params=pltpu.CompilerParams(vmem_limit_bytes=60 * MIB),
    )(signal, pre_gate, filter_taps)
    return out.reshape(devices, 2 * rows // devices, tokens)


def gate_kernel(post_ref, signal_ref, pre_ref, convolved_ref, gain_ref, after_ref, out_ref):
    del after_ref
    gated = signal_ref[...].astype(jnp.float32) * pre_ref[...].astype(jnp.float32)
    inner = convolved_ref[...].astype(jnp.float32) + gain_ref[...] * gated
    out_ref[...] = (post_ref[...].astype(jnp.float32) * inner).astype(out_ref.dtype)


def gate(post_gate, signal, pre_gate, convolved, skip_gain, after):
    corners = jnp.concatenate([array[:16, :128] for array in after])
    return pl.pallas_call(
        gate_kernel,
        out_shape=jax.ShapeDtypeStruct(post_gate.shape, post_gate.dtype),
        in_specs=[pl.BlockSpec(memory_space=pltpu.VMEM)] * 6,
        out_specs=pl.BlockSpec(memory_space=pltpu.VMEM),
        compiler_params=pltpu.CompilerParams(vmem_limit_bytes=6 * MIB),
        cost_estimate=pl.CostEstimate(
            flops=5 * post_gate.size, bytes_accessed=10 * post_gate.size, transcendentals=0
        ),
    )(post_gate, signal, pre_gate, convolved, skip_gain[:, None], corners)


def per_device(signal, pre_gate, post_gate, filter_taps, skip_gain, out_weight):
    channels_here, tokens_here = signal.shape
    devices = lax.axis_size("ctx")
    channels = channels_here // devices
    quads = lax.axis_size("quad")
    group = lax.axis_size("pair") * lax.axis_size("core")
    features = out_weight.shape[1]
    width = features // (quads * group)

    send = outgoing(signal, pre_gate, filter_taps, devices)
    blocks = lax.all_to_all(send, "ctx", split_axis=0, concat_axis=0, tiled=True)

    quad, pair, core = (lax.axis_index(axis) for axis in TP_AXES)
    place = pair * 2 + core
    order = [
        index
        for r in range(group)
        for index in targets_of(quad, pair ^ (r >> 1), core ^ (r & 1), quads)
    ]
    tables = dft_tables(devices, tokens_here, channels)
    *weights, arranged = arrange(
        out_weight, jnp.stack(order).astype(jnp.int32), group, width
    )
    weights = [weights[0]] + [
        lax.ppermute(weights[r], GROUP, [(t, t ^ r) for t in range(group)])
        for r in range(1, group)
    ]

    convolved = lax.all_to_all(
        convolve(blocks, channels, tables, arranged), "ctx", split_axis=0, concat_axis=0, tiled=True
    ).reshape(channels_here, tokens_here)
    mixed = gate(post_gate, signal, pre_gate, convolved, skip_gain, weights[1:])
    gathered = lax.all_gather(mixed, GROUP, axis=0, tiled=True)
    shares = project(place.astype(jnp.int32).reshape(1), gathered, weights, width)
    shares = [send_to_target(shares[step], step, quads) for step in range(3)] + [shares[3]]
    return sum(share.astype(jnp.float32) for share in shares).astype(jnp.bfloat16)


def solution(mesh):
    ctx, tp = mesh.devices.shape
    fine = Mesh(mesh.devices.reshape(ctx, tp // 4, 2, 2), ("ctx",) + TP_AXES)
    return jax.shard_map(
        per_device,
        mesh=fine,
        in_specs=(
            P(TP_AXES, "ctx"),
            P(TP_AXES, "ctx"),
            P(TP_AXES, "ctx"),
            P(TP_AXES, "ctx"),
            P(TP_AXES),
            P(TP_AXES, None),
        ),
        out_specs=P(TP_AXES, "ctx"),
        check_vma=False,
    )
```

```python
import math

import jax
import jax.numpy as jnp
import numpy as np
from jax import lax
from jax.experimental import pallas as pl
from jax.experimental.pallas import tpu as pltpu
from jax.sharding import Mesh
from jax.sharding import PartitionSpec as P

TP_AXES = ("quad", "pair", "core")
GROUP = ("pair", "core")
MIB = 1 << 20


def targets_of(quad, pair, core, quads):
    onward = 2 * pair - 1
    far = lax.rem(quad + 2 * onward + quads, quads)
    near = lax.rem(quad + onward + quads, quads)
    chips = [(far, 1 - pair), (near, pair), (near, 1 - pair), (quad, pair)]
    return [(q * 2 + p) * 2 + core for q, p in chips]


def send_to_target(share, step, quads):
    pairs = []
    for quad in range(quads):
        for pair in range(2):
            onward = 1 if pair == 1 else -1
            q = (quad + (2 * onward if step == 0 else onward)) % quads
            p = pair if step == 1 else 1 - pair
            pairs += [((quad * 2 + pair) * 2 + c, (q * 2 + p) * 2 + c) for c in range(2)]
    return lax.ppermute(share, TP_AXES, pairs)


def arrange_kernel(group, quads, width, members, place_ref, weight_ref, *refs):
    out_refs, done_ref, sems = refs[: len(members)], refs[-2], refs[-1]
    tp = place_ref[0]
    quad, place = tp // group, lax.rem(tp, group)
    copies = []
    for n, r in enumerate(members):
        other = place ^ r
        for i, target in enumerate(targets_of(quad, other // 2, lax.rem(other, 2), quads)):
            start = pl.multiple_of(target * width, width)
            copies.append(
                pltpu.make_async_copy(
                    weight_ref.at[:, pl.ds(start, width)],
                    out_refs[n].at[:, pl.ds(i * width, width)],
                    sems.at[n * group + i],
                )
            )
    for copy in copies:
        copy.start()
    for copy in copies:
        copy.wait()
    done_ref[0] = tp


def arrange(out_weight, place, group, quads, width, members):
    rows = out_weight.shape[0]
    piece = jax.ShapeDtypeStruct((rows, group * width), out_weight.dtype)
    *pieces, done = pl.pallas_call(
        lambda *refs: arrange_kernel(group, quads, width, members, *refs),
        out_shape=[piece] * len(members) + [jax.ShapeDtypeStruct((1,), jnp.int32)],
        in_specs=[
            pl.BlockSpec(memory_space=pltpu.SMEM),
            pl.BlockSpec(memory_space=pltpu.HBM),
        ],
        out_specs=[pl.BlockSpec(memory_space=pltpu.HBM)] * len(members)
        + [pl.BlockSpec(memory_space=pltpu.SMEM)],
        scratch_shapes=[pltpu.SemaphoreType.DMA((len(members) * group,))],
        compiler_params=pltpu.CompilerParams(vmem_limit_bytes=60 * MIB),
        cost_estimate=pl.CostEstimate(
            flops=0,
            bytes_accessed=4 * rows * len(members) * group * width,
            transcendentals=0,
        ),
    )(place, out_weight)
    return pieces, done


def project_kernel(group, place_ref, mixed_ref, *refs):
    weight_refs, out_refs = refs[:group], refs[group:]
    tokens = mixed_ref.shape[0] // group
    width = out_refs[0].shape[1]
    place = lax.rem(place_ref[0], group)
    mixed = [
        mixed_ref[pl.ds(pl.multiple_of((place ^ r) * tokens, tokens), tokens), :]
        for r in range(group)
    ]
    for i in range(group):
        total = None
        for r in range(group):
            term = jnp.dot(
                mixed[r],
                weight_refs[r][:, i * width : (i + 1) * width],
                preferred_element_type=jnp.float32,
            )
            total = term if total is None else total + term
        out_refs[i][...] = total.astype(out_refs[i].dtype)


def project(place, mixed, weights, width):
    group = len(weights)
    share = jax.ShapeDtypeStruct((mixed.shape[0] // group, width), mixed.dtype)
    return pl.pallas_call(
        lambda *refs: project_kernel(group, *refs),
        out_shape=[share] * group,
        in_specs=[pl.BlockSpec(memory_space=pltpu.SMEM)]
        + [pl.BlockSpec(memory_space=pltpu.VMEM)] * (1 + group),
        out_specs=[pl.BlockSpec(memory_space=pltpu.VMEM)] * group,
        compiler_params=pltpu.CompilerParams(vmem_limit_bytes=10 * MIB),
        cost_estimate=pl.CostEstimate(
            flops=2 * mixed.size * group * width,
            bytes_accessed=2 * (mixed.size + sum(w.size for w in weights) + group * share.size),
            transcendentals=0,
        ),
    )(place, mixed, *weights)


def finish_kernel(*refs):
    total = refs[0][...].astype(jnp.float32)
    for ref in refs[1:-1]:
        total = total + ref[...].astype(jnp.float32)
    refs[-1][...] = total.astype(refs[-1].dtype).T


def finish(shares):
    tokens, width = shares[0].shape
    return pl.pallas_call(
        finish_kernel,
        out_shape=jax.ShapeDtypeStruct((width, tokens), shares[0].dtype),
        in_specs=[pl.BlockSpec(memory_space=pltpu.VMEM)] * len(shares),
        out_specs=pl.BlockSpec(memory_space=pltpu.VMEM),
        compiler_params=pltpu.CompilerParams(vmem_limit_bytes=6 * MIB),
    )(*shares)


def dft_tables(blocks, tokens, channels):
    period = 2 * blocks
    total = period * tokens
    low = blocks + 1
    k1 = np.arange(low)
    i = np.arange(blocks)
    s = np.arange(tokens)
    first = 2 * np.pi * (np.outer(k1, i) % period) / period
    turn = 2 * np.pi * (np.outer(k1, s) % total) / total
    square = 2 * np.pi * (np.outer(s, s) % tokens) / tokens
    front = np.concatenate([np.cos(first), -np.sin(first)])
    weight = np.where((k1 == 0) | (k1 == blocks), 1.0, 2.0)[:, None] / total
    back = np.concatenate(
        [
            np.kron((weight * np.cos(first)).T, np.eye(channels)),
            np.kron(-(weight * np.sin(first)).T, np.eye(channels)),
        ],
        axis=1,
    )
    matrices = [jnp.asarray(m, jnp.bfloat16) for m in (front, np.cos(square), np.sin(square), back)]
    turns = [jnp.asarray(m, jnp.float32) for m in (np.cos(turn), np.sin(turn))]
    return matrices + turns


def matmul(left, right):
    return jnp.dot(left, right, preferred_element_type=jnp.float32)


def convolve_kernel(
    channels, in_ref, front_ref, square_cos_ref, square_sin_ref, back_ref, cos_ref, sin_ref, after_ref, out_ref
):
    del after_ref
    low, tokens = cos_ref.shape
    both = 2 * channels
    turn_cos = cos_ref[...].reshape(low, 1, tokens)
    turn_sin = sin_ref[...].reshape(low, 1, tokens)
    blocks = front_ref.shape[1]
    width = blocks * both
    repeat = lax.broadcasted_iota(jnp.int32, (blocks, width), 1) // both
    repeat = (repeat == lax.broadcasted_iota(jnp.int32, (blocks, width), 0)).astype(jnp.bfloat16)
    agree = lax.broadcasted_iota(jnp.int32, (both, width), 1) % both
    agree = agree == lax.broadcasted_iota(jnp.int32, (both, width), 0)
    entries = matmul(front_ref[...], repeat).reshape(2 * low, 1, width)
    front = jnp.where(agree[None], entries, 0.0).reshape(2 * low * both, width)
    spread = matmul(front.astype(jnp.bfloat16), in_ref[...])
    real = spread[: low * both].reshape(low, both, tokens)
    imag = spread[low * both :].reshape(low, both, tokens)
    turned_real = (real * turn_cos + imag * turn_sin).reshape(low * both, tokens).astype(jnp.bfloat16)
    turned_imag = (imag * turn_cos - real * turn_sin).reshape(low * both, tokens).astype(jnp.bfloat16)
    square_cos, square_sin = square_cos_ref[...], square_sin_ref[...]
    real = (matmul(turned_real, square_cos) + matmul(turned_imag, square_sin)).reshape(low, both, tokens)
    imag = (matmul(turned_imag, square_cos) - matmul(turned_real, square_sin)).reshape(low, both, tokens)
    sig_real, tap_real = real[:, :channels], real[:, channels:]
    sig_imag, tap_imag = imag[:, :channels], imag[:, channels:]
    prod_real = sig_real * tap_real - sig_imag * tap_imag
    prod_imag = sig_real * tap_imag + sig_imag * tap_real
    prod_real = prod_real.reshape(low * channels, tokens).astype(jnp.bfloat16)
    prod_imag = prod_imag.reshape(low * channels, tokens).astype(jnp.bfloat16)
    real = matmul(prod_real, square_cos) - matmul(prod_imag, square_sin)
    imag = matmul(prod_imag, square_cos) + matmul(prod_real, square_sin)
    real, imag = real.reshape(low, channels, tokens), imag.reshape(low, channels, tokens)
    rows = jnp.concatenate(
        [real * turn_cos - imag * turn_sin, real * turn_sin + imag * turn_cos], axis=0
    )
    out_ref[...] = matmul(
        back_ref[...], rows.reshape(2 * low * channels, tokens).astype(jnp.bfloat16)
    ).astype(out_ref.dtype)


def convolve(blocks_in, channels, tables, after):
    blocks, both, tokens = blocks_in.shape
    out = pl.pallas_call(
        lambda *refs: convolve_kernel(channels, *refs),
        out_shape=jax.ShapeDtypeStruct((blocks * channels, tokens), jnp.bfloat16),
        in_specs=[pl.BlockSpec(memory_space=pltpu.VMEM)] * (1 + len(tables))
        + [pl.BlockSpec(memory_space=pltpu.SMEM)],
        out_specs=pl.BlockSpec(memory_space=pltpu.VMEM),
        compiler_params=pltpu.CompilerParams(vmem_limit_bytes=32 * MIB),
        cost_estimate=pl.CostEstimate(
            flops=800_000_000, bytes_accessed=3_000_000, transcendentals=0
        ),
    )(blocks_in.reshape(blocks * both, tokens), *tables, after)
    return out.reshape(blocks, channels, tokens)


def outgoing_kernel(devices, signal_hbm, gate_hbm, taps_hbm, out_ref, signal_ref, gate_ref, taps_ref, sems):
    copies = [
        pltpu.make_async_copy(source, target, sems.at[n])
        for n, (source, target) in enumerate(
            [(signal_hbm, signal_ref), (gate_hbm, gate_ref), (taps_hbm, taps_ref)]
        )
    ]
    for copy in copies:
        copy.start()
    for copy in copies:
        copy.wait()
    rows, tokens = signal_ref.shape
    gated = signal_ref[...].astype(jnp.float32) * gate_ref[...].astype(jnp.float32)
    both = jnp.concatenate(
        [
            gated.reshape(devices, rows // devices, tokens),
            taps_ref[...].reshape(devices, rows // devices, tokens),
        ],
        axis=1,
    )
    out_ref[...] = both.reshape(2 * rows, tokens).astype(out_ref.dtype)


def outgoing(signal, pre_gate, filter_taps, devices):
    rows, tokens = signal.shape
    out = pl.pallas_call(
        lambda *refs: outgoing_kernel(devices, *refs),
        out_shape=jax.ShapeDtypeStruct((2 * rows, tokens), jnp.bfloat16),
        in_specs=[pl.BlockSpec(memory_space=pltpu.HBM)] * 3,
        out_specs=pl.BlockSpec(memory_space=pltpu.VMEM),
        scratch_shapes=[
            pltpu.VMEM(signal.shape, signal.dtype),
            pltpu.VMEM(pre_gate.shape, pre_gate.dtype),
            pltpu.VMEM(filter_taps.shape, filter_taps.dtype),
            pltpu.SemaphoreType.DMA((3,)),
        ],
        compiler_params=pltpu.CompilerParams(vmem_limit_bytes=60 * MIB),
    )(signal, pre_gate, filter_taps)
    return out.reshape(devices, 2 * rows // devices, tokens)


def gate_kernel(post_ref, signal_ref, pre_ref, convolved_ref, gain_ref, after_ref, out_ref):
    del after_ref
    gated = signal_ref[...].astype(jnp.float32) * pre_ref[...].astype(jnp.float32)
    inner = convolved_ref[...].astype(jnp.float32) + gain_ref[...] * gated
    out_ref[...] = (post_ref[...].astype(jnp.float32) * inner).astype(out_ref.dtype).T


def gate(post_gate, signal, pre_gate, convolved, skip_gain, after):
    corners = jnp.concatenate([array[:16, :128] for array in after])
    return pl.pallas_call(
        gate_kernel,
        out_shape=jax.ShapeDtypeStruct(post_gate.shape[::-1], post_gate.dtype),
        in_specs=[pl.BlockSpec(memory_space=pltpu.VMEM)] * 6,
        out_specs=pl.BlockSpec(memory_space=pltpu.VMEM),
        compiler_params=pltpu.CompilerParams(vmem_limit_bytes=6 * MIB),
        cost_estimate=pl.CostEstimate(
            flops=5 * post_gate.size, bytes_accessed=10 * post_gate.size, transcendentals=0
        ),
    )(post_gate, signal, pre_gate, convolved, skip_gain[:, None], corners)


def per_device(signal, pre_gate, post_gate, filter_taps, skip_gain, out_weight):
    channels_here, tokens_here = signal.shape
    devices = lax.axis_size("ctx")
    channels = channels_here // devices
    quads = lax.axis_size("quad")
    group = lax.axis_size("pair") * lax.axis_size("core")
    features = out_weight.shape[1]
    width = features // (quads * group)

    send = outgoing(signal, pre_gate, filter_taps, devices)
    blocks = lax.all_to_all(send, "ctx", split_axis=0, concat_axis=0, tiled=True)

    place = lax.axis_index(TP_AXES).astype(jnp.int32).reshape(1)
    crossing = [r for r in range(group) if r >= 2]
    pieces, arranged = arrange(out_weight, place, group, quads, width, crossing)
    tables = dft_tables(devices, tokens_here, channels)
    convolved = convolve(blocks, channels, tables, arranged)
    inner, _ = arrange(out_weight, place, group, quads, width, [0, 1])
    weights = [inner[0]] + [
        lax.ppermute(piece, GROUP, [(t, t ^ r) for t in range(group)])
        for r, piece in zip(range(1, group), [inner[1]] + pieces)
    ]
    convolved = lax.all_to_all(convolved, "ctx", split_axis=0, concat_axis=0, tiled=True).reshape(
        channels_here, tokens_here
    )
    mixed = gate(post_gate, signal, pre_gate, convolved, skip_gain, weights[2:])
    gathered = lax.all_gather(mixed, GROUP, axis=0, tiled=True)
    shares = project(place, gathered, weights, width)
    return finish([send_to_target(shares[step], step, quads) for step in range(3)] + [shares[3]])


def solution(mesh):
    ctx, tp = mesh.devices.shape
    fine = Mesh(mesh.devices.reshape(ctx, tp // 4, 2, 2), ("ctx",) + TP_AXES)
    return jax.shard_map(
        per_device,
        mesh=fine,
        in_specs=(
            P(TP_AXES, "ctx"),
            P(TP_AXES, "ctx"),
            P(TP_AXES, "ctx"),
            P(TP_AXES, "ctx"),
            P(TP_AXES),
            P(TP_AXES, None),
        ),
        out_specs=P(TP_AXES, "ctx"),
        check_vma=False,
    )
```

```python
import math

import jax
import jax.numpy as jnp
import numpy as np
from jax import lax
from jax.experimental import pallas as pl
from jax.experimental.pallas import tpu as pltpu
from jax.sharding import Mesh
from jax.sharding import PartitionSpec as P

TP_AXES = ("quad", "pair", "core")
GROUP = ("pair", "core")
MIB = 1 << 20


def targets_of(quad, pair, core, quads):
    onward = 2 * pair - 1
    far = lax.rem(quad + 2 * onward + quads, quads)
    near = lax.rem(quad + onward + quads, quads)
    chips = [(far, 1 - pair), (near, pair), (near, 1 - pair), (quad, pair)]
    return [(q * 2 + p) * 2 + core for q, p in chips]


def send_to_target(share, step, quads):
    pairs = []
    for quad in range(quads):
        for pair in range(2):
            onward = 1 if pair == 1 else -1
            q = (quad + (2 * onward if step == 0 else onward)) % quads
            p = pair if step == 1 else 1 - pair
            pairs += [((quad * 2 + pair) * 2 + c, (q * 2 + p) * 2 + c) for c in range(2)]
    return lax.ppermute(share, TP_AXES, pairs)


def arrange_kernel(group, quads, width, members, place_ref, weight_ref, *refs):
    out_refs, done_ref, sems = refs[: len(members)], refs[-2], refs[-1]
    tp = place_ref[0]
    quad, place = tp // group, lax.rem(tp, group)
    copies = []
    for n, r in enumerate(members):
        other = place ^ r
        for i, target in enumerate(targets_of(quad, other // 2, lax.rem(other, 2), quads)):
            start = pl.multiple_of(target * width, width)
            copies.append(
                pltpu.make_async_copy(
                    weight_ref.at[:, pl.ds(start, width)],
                    out_refs[n].at[:, pl.ds(i * width, width)],
                    sems.at[n * group + i],
                )
            )
    for copy in copies:
        copy.start()
    for copy in copies:
        copy.wait()
    done_ref[0] = tp


def arrange(out_weight, place, group, quads, width, members):
    rows = out_weight.shape[0]
    piece = jax.ShapeDtypeStruct((rows, group * width), out_weight.dtype)
    *pieces, done = pl.pallas_call(
        lambda *refs: arrange_kernel(group, quads, width, members, *refs),
        out_shape=[piece] * len(members) + [jax.ShapeDtypeStruct((1,), jnp.int32)],
        in_specs=[
            pl.BlockSpec(memory_space=pltpu.SMEM),
            pl.BlockSpec(memory_space=pltpu.HBM),
        ],
        out_specs=[pl.BlockSpec(memory_space=pltpu.VMEM)] * len(members)
        + [pl.BlockSpec(memory_space=pltpu.SMEM)],
        scratch_shapes=[pltpu.SemaphoreType.DMA((len(members) * group,))],
        compiler_params=pltpu.CompilerParams(vmem_limit_bytes=60 * MIB),
        cost_estimate=pl.CostEstimate(
            flops=0,
            bytes_accessed=4 * rows * len(members) * group * width,
            transcendentals=0,
        ),
    )(place, out_weight)
    return pieces, done


def project_kernel(group, place_ref, mixed_ref, *refs):
    weight_refs, out_refs = refs[:group], refs[group:]
    tokens = mixed_ref.shape[0] // group
    width = out_refs[0].shape[1]
    place = lax.rem(place_ref[0], group)
    mixed = [
        mixed_ref[pl.ds(pl.multiple_of((place ^ r) * tokens, tokens), tokens), :]
        for r in range(group)
    ]
    for i in range(group):
        total = None
        for r in range(group):
            term = jnp.dot(
                mixed[r],
                weight_refs[r][:, i * width : (i + 1) * width],
                preferred_element_type=jnp.float32,
            )
            total = term if total is None else total + term
        out_refs[i][...] = total.astype(out_refs[i].dtype)


def project(place, mixed, weights, width):
    group = len(weights)
    share = jax.ShapeDtypeStruct((mixed.shape[0] // group, width), mixed.dtype)
    return pl.pallas_call(
        lambda *refs: project_kernel(group, *refs),
        out_shape=[share] * group,
        in_specs=[pl.BlockSpec(memory_space=pltpu.SMEM)]
        + [pl.BlockSpec(memory_space=pltpu.VMEM)] * (1 + group),
        out_specs=[pl.BlockSpec(memory_space=pltpu.VMEM)] * group,
        compiler_params=pltpu.CompilerParams(vmem_limit_bytes=10 * MIB),
        cost_estimate=pl.CostEstimate(
            flops=2 * mixed.size * group * width,
            bytes_accessed=2 * (mixed.size + sum(w.size for w in weights) + group * share.size),
            transcendentals=0,
        ),
    )(place, mixed, *weights)


def finish_kernel(*refs):
    total = refs[0][...].astype(jnp.float32)
    for ref in refs[1:-1]:
        total = total + ref[...].astype(jnp.float32)
    refs[-1][...] = total.astype(refs[-1].dtype).T


def finish(shares):
    tokens, width = shares[0].shape
    return pl.pallas_call(
        finish_kernel,
        out_shape=jax.ShapeDtypeStruct((width, tokens), shares[0].dtype),
        in_specs=[pl.BlockSpec(memory_space=pltpu.VMEM)] * len(shares),
        out_specs=pl.BlockSpec(memory_space=pltpu.VMEM),
        compiler_params=pltpu.CompilerParams(vmem_limit_bytes=6 * MIB),
    )(*shares)


def dft_tables(blocks, tokens, channels):
    period = 2 * blocks
    total = period * tokens
    low = blocks + 1
    k1 = np.arange(low)
    i = np.arange(blocks)
    s = np.arange(tokens)
    first = 2 * np.pi * (np.outer(k1, i) % period) / period
    turn = 2 * np.pi * (np.outer(k1, s) % total) / total
    square = 2 * np.pi * (np.outer(s, s) % tokens) / tokens
    front = np.concatenate([np.cos(first), -np.sin(first)])
    weight = np.where((k1 == 0) | (k1 == blocks), 1.0, 2.0)[:, None] / total
    back = np.concatenate(
        [
            np.kron((weight * np.cos(first)).T, np.eye(channels)),
            np.kron(-(weight * np.sin(first)).T, np.eye(channels)),
        ],
        axis=1,
    )
    matrices = [jnp.asarray(m, jnp.bfloat16) for m in (front, np.cos(square), np.sin(square), back)]
    turns = [jnp.asarray(m, jnp.float32) for m in (np.cos(turn), np.sin(turn))]
    return matrices + turns


def matmul(left, right):
    return jnp.dot(left, right, preferred_element_type=jnp.float32)


def convolve_kernel(
    channels, in_ref, front_ref, square_cos_ref, square_sin_ref, back_ref, cos_ref, sin_ref, after_ref, out_ref
):
    del after_ref
    low, tokens = cos_ref.shape
    both = 2 * channels
    turn_cos = cos_ref[...].reshape(low, 1, tokens)
    turn_sin = sin_ref[...].reshape(low, 1, tokens)
    blocks = front_ref.shape[1]
    width = blocks * both
    repeat = lax.broadcasted_iota(jnp.int32, (blocks, width), 1) // both
    repeat = (repeat == lax.broadcasted_iota(jnp.int32, (blocks, width), 0)).astype(jnp.bfloat16)
    agree = lax.broadcasted_iota(jnp.int32, (both, width), 1) % both
    agree = agree == lax.broadcasted_iota(jnp.int32, (both, width), 0)
    entries = matmul(front_ref[...], repeat).reshape(2 * low, 1, width)
    front = jnp.where(agree[None], entries, 0.0).reshape(2 * low * both, width)
    spread = matmul(front.astype(jnp.bfloat16), in_ref[...])
    real = spread[: low * both].reshape(low, both, tokens)
    imag = spread[low * both :].reshape(low, both, tokens)
    turned_real = (real * turn_cos + imag * turn_sin).reshape(low * both, tokens).astype(jnp.bfloat16)
    turned_imag = (imag * turn_cos - real * turn_sin).reshape(low * both, tokens).astype(jnp.bfloat16)
    square_cos, square_sin = square_cos_ref[...], square_sin_ref[...]
    real = (matmul(turned_real, square_cos) + matmul(turned_imag, square_sin)).reshape(low, both, tokens)
    imag = (matmul(turned_imag, square_cos) - matmul(turned_real, square_sin)).reshape(low, both, tokens)
    sig_real, tap_real = real[:, :channels], real[:, channels:]
    sig_imag, tap_imag = imag[:, :channels], imag[:, channels:]
    prod_real = sig_real * tap_real - sig_imag * tap_imag
    prod_imag = sig_real * tap_imag + sig_imag * tap_real
    prod_real = prod_real.reshape(low * channels, tokens).astype(jnp.bfloat16)
    prod_imag = prod_imag.reshape(low * channels, tokens).astype(jnp.bfloat16)
    real = matmul(prod_real, square_cos) - matmul(prod_imag, square_sin)
    imag = matmul(prod_imag, square_cos) + matmul(prod_real, square_sin)
    real, imag = real.reshape(low, channels, tokens), imag.reshape(low, channels, tokens)
    rows = jnp.concatenate(
        [real * turn_cos - imag * turn_sin, real * turn_sin + imag * turn_cos], axis=0
    )
    out_ref[...] = matmul(
        back_ref[...], rows.reshape(2 * low * channels, tokens).astype(jnp.bfloat16)
    ).astype(out_ref.dtype)


def convolve(blocks_in, channels, tables, after):
    blocks, both, tokens = blocks_in.shape
    out = pl.pallas_call(
        lambda *refs: convolve_kernel(channels, *refs),
        out_shape=jax.ShapeDtypeStruct((blocks * channels, tokens), jnp.bfloat16),
        in_specs=[pl.BlockSpec(memory_space=pltpu.VMEM)] * (1 + len(tables))
        + [pl.BlockSpec(memory_space=pltpu.SMEM)],
        out_specs=pl.BlockSpec(memory_space=pltpu.VMEM),
        compiler_params=pltpu.CompilerParams(vmem_limit_bytes=32 * MIB),
        cost_estimate=pl.CostEstimate(
            flops=800_000_000, bytes_accessed=3_000_000, transcendentals=0
        ),
    )(blocks_in.reshape(blocks * both, tokens), *tables, after)
    return out.reshape(blocks, channels, tokens)


def outgoing_kernel(devices, signal_hbm, gate_hbm, taps_hbm, out_ref, signal_ref, gate_ref, taps_ref, sems):
    copies = [
        pltpu.make_async_copy(source, target, sems.at[n])
        for n, (source, target) in enumerate(
            [(signal_hbm, signal_ref), (gate_hbm, gate_ref), (taps_hbm, taps_ref)]
        )
    ]
    for copy in copies:
        copy.start()
    for copy in copies:
        copy.wait()
    rows, tokens = signal_ref.shape
    gated = signal_ref[...].astype(jnp.float32) * gate_ref[...].astype(jnp.float32)
    both = jnp.concatenate(
        [
            gated.reshape(devices, rows // devices, tokens),
            taps_ref[...].reshape(devices, rows // devices, tokens),
        ],
        axis=1,
    )
    out_ref[...] = both.reshape(2 * rows, tokens).astype(out_ref.dtype)


def outgoing(signal, pre_gate, filter_taps, devices):
    rows, tokens = signal.shape
    out = pl.pallas_call(
        lambda *refs: outgoing_kernel(devices, *refs),
        out_shape=jax.ShapeDtypeStruct((2 * rows, tokens), jnp.bfloat16),
        in_specs=[pl.BlockSpec(memory_space=pltpu.HBM)] * 3,
        out_specs=pl.BlockSpec(memory_space=pltpu.VMEM),
        scratch_shapes=[
            pltpu.VMEM(signal.shape, signal.dtype),
            pltpu.VMEM(pre_gate.shape, pre_gate.dtype),
            pltpu.VMEM(filter_taps.shape, filter_taps.dtype),
            pltpu.SemaphoreType.DMA((3,)),
        ],
        compiler_params=pltpu.CompilerParams(vmem_limit_bytes=60 * MIB),
    )(signal, pre_gate, filter_taps)
    return out.reshape(devices, 2 * rows // devices, tokens)


def gate_kernel(post_ref, signal_ref, pre_ref, convolved_ref, gain_ref, after_ref, out_ref):
    del after_ref
    gated = signal_ref[...].astype(jnp.float32) * pre_ref[...].astype(jnp.float32)
    inner = convolved_ref[...].astype(jnp.float32) + gain_ref[...] * gated
    out_ref[...] = (post_ref[...].astype(jnp.float32) * inner).astype(out_ref.dtype).T


def gate(post_gate, signal, pre_gate, convolved, skip_gain, after):
    corners = jnp.concatenate([array[:16, :128] for array in after])
    return pl.pallas_call(
        gate_kernel,
        out_shape=jax.ShapeDtypeStruct(post_gate.shape[::-1], post_gate.dtype),
        in_specs=[pl.BlockSpec(memory_space=pltpu.VMEM)] * 6,
        out_specs=pl.BlockSpec(memory_space=pltpu.VMEM),
        compiler_params=pltpu.CompilerParams(vmem_limit_bytes=6 * MIB),
        cost_estimate=pl.CostEstimate(
            flops=5 * post_gate.size, bytes_accessed=10 * post_gate.size, transcendentals=0
        ),
    )(post_gate, signal, pre_gate, convolved, skip_gain[:, None], corners)


def per_device(signal, pre_gate, post_gate, filter_taps, skip_gain, out_weight):
    channels_here, tokens_here = signal.shape
    devices = lax.axis_size("ctx")
    channels = channels_here // devices
    quads = lax.axis_size("quad")
    group = lax.axis_size("pair") * lax.axis_size("core")
    features = out_weight.shape[1]
    width = features // (quads * group)

    send = outgoing(signal, pre_gate, filter_taps, devices)
    blocks = lax.all_to_all(send, "ctx", split_axis=0, concat_axis=0, tiled=True)

    place = lax.axis_index(TP_AXES).astype(jnp.int32).reshape(1)
    crossing = [r for r in range(group) if r >= 2]
    pieces, arranged = arrange(out_weight, place, group, quads, width, crossing)
    tables = dft_tables(devices, tokens_here, channels)
    convolved = convolve(blocks, channels, tables, arranged)
    inner, _ = arrange(out_weight, place, group, quads, width, [0, 1])
    weights = [inner[0]] + [
        lax.ppermute(piece, GROUP, [(t, t ^ r) for t in range(group)])
        for r, piece in zip(range(1, group), [inner[1]] + pieces)
    ]
    convolved = lax.all_to_all(convolved, "ctx", split_axis=0, concat_axis=0, tiled=True).reshape(
        channels_here, tokens_here
    )
    mixed = gate(post_gate, signal, pre_gate, convolved, skip_gain, weights[2:])
    gathered = lax.all_gather(mixed, GROUP, axis=0, tiled=True)
    shares = project(place, gathered, weights, width)
    return finish([send_to_target(shares[step], step, quads) for step in range(3)] + [shares[3]])


def solution(mesh):
    ctx, tp = mesh.devices.shape
    fine = Mesh(mesh.devices.reshape(ctx, tp // 4, 2, 2), ("ctx",) + TP_AXES)
    return jax.shard_map(
        per_device,
        mesh=fine,
        in_specs=(
            P(TP_AXES, "ctx"),
            P(TP_AXES, "ctx"),
            P(TP_AXES, "ctx"),
            P(TP_AXES, "ctx"),
            P(TP_AXES),
            P(TP_AXES, None),
        ),
        out_specs=P(TP_AXES, "ctx"),
        check_vma=False,
    )
```

```python
import math

import jax
import jax.numpy as jnp
import numpy as np
from jax import lax
from jax.experimental import pallas as pl
from jax.experimental.pallas import tpu as pltpu
from jax.sharding import Mesh
from jax.sharding import PartitionSpec as P

TP_AXES = ("quad", "pair", "core")
GROUP = ("pair", "core")
MIB = 1 << 20


def targets_of(quad, pair, core, quads):
    onward = 2 * pair - 1
    far = lax.rem(quad + 2 * onward + quads, quads)
    near = lax.rem(quad + onward + quads, quads)
    chips = [(far, 1 - pair), (near, pair), (near, 1 - pair), (quad, pair)]
    return [(q * 2 + p) * 2 + core for q, p in chips]


def send_to_target(share, step, quads):
    pairs = []
    for quad in range(quads):
        for pair in range(2):
            onward = 1 if pair == 1 else -1
            q = (quad + (2 * onward if step == 0 else onward)) % quads
            p = pair if step == 1 else 1 - pair
            pairs += [((quad * 2 + pair) * 2 + c, (q * 2 + p) * 2 + c) for c in range(2)]
    return lax.ppermute(share, TP_AXES, pairs)


def arrange_kernel(group, quads, width, members, place_ref, weight_ref, *refs):
    count = len(members) * group
    out_refs, done_ref, blocks, in_sems, out_sems = refs[: len(members)], *refs[-4:]
    tp = place_ref[0]
    quad, place = tp // group, lax.rem(tp, group)
    loads, stores = [], []
    for n, r in enumerate(members):
        other = place ^ r
        for i, target in enumerate(targets_of(quad, other // 2, lax.rem(other, 2), quads)):
            k = n * group + i
            start = pl.multiple_of(target * width, width)
            loads.append(
                pltpu.make_async_copy(
                    weight_ref.at[:, pl.ds(start, width)], blocks.at[k], in_sems.at[k]
                )
            )
            stores.append(
                pltpu.make_async_copy(
                    blocks.at[k], out_refs[n].at[:, pl.ds(i * width, width)], out_sems.at[k]
                )
            )
    for load in loads:
        load.start()
    for k in range(count):
        loads[k].wait()
        stores[k].start()
    for store in stores:
        store.wait()
    done_ref[0] = tp


def arrange(out_weight, place, group, quads, width, members):
    rows = out_weight.shape[0]
    count = len(members) * group
    piece = jax.ShapeDtypeStruct((rows, group * width), out_weight.dtype)
    *pieces, done = pl.pallas_call(
        lambda *refs: arrange_kernel(group, quads, width, members, *refs),
        out_shape=[piece] * len(members) + [jax.ShapeDtypeStruct((1,), jnp.int32)],
        in_specs=[
            pl.BlockSpec(memory_space=pltpu.SMEM),
            pl.BlockSpec(memory_space=pltpu.HBM),
        ],
        out_specs=[pl.BlockSpec(memory_space=pltpu.HBM)] * len(members)
        + [pl.BlockSpec(memory_space=pltpu.SMEM)],
        scratch_shapes=[
            pltpu.VMEM((count, rows, width), out_weight.dtype),
            pltpu.SemaphoreType.DMA((count,)),
            pltpu.SemaphoreType.DMA((count,)),
        ],
        compiler_params=pltpu.CompilerParams(vmem_limit_bytes=60 * MIB),
        cost_estimate=pl.CostEstimate(
            flops=0, bytes_accessed=4 * rows * count * width, transcendentals=0
        ),
    )(place, out_weight)
    return pieces, done


def project_kernel(
    group, quads, place_ref, mixed_ref, own_ref, *refs
):
    piece_refs, out_refs = refs[: group - 1], refs[group - 1 : 2 * group - 1]
    blocks, totals, sems = refs[-3:]
    tokens = mixed_ref.shape[0] // group
    width = out_refs[0].shape[1]
    tp = place_ref[0]
    quad, place = tp // group, lax.rem(tp, group)
    targets = targets_of(quad, place // 2, lax.rem(place, 2), quads)
    loads = []
    for i, target in enumerate(targets):
        start = pl.multiple_of(target * width, width)
        loads.append(
            pltpu.make_async_copy(own_ref.at[:, pl.ds(start, width)], blocks.at[i], sems.at[i])
        )
    for load in loads:
        load.start()
    mixed = [
        mixed_ref[pl.ds(pl.multiple_of((place ^ r) * tokens, tokens), tokens), :]
        for r in range(group)
    ]

    def product(r, weights):
        return jnp.dot(mixed[r], weights, preferred_element_type=jnp.float32)

    for i in range(group):
        columns = slice(i * width, (i + 1) * width)
        total = product(1, piece_refs[0][:, columns])
        for r in range(2, group):
            total = total + product(r, piece_refs[r - 1][:, columns])
        totals[i] = total
    for i in range(group):
        loads[i].wait()
        total = totals[i] + product(0, blocks[i])
        out_refs[i][...] = total.astype(out_refs[i].dtype)


def project(place, mixed, own, pieces, group, quads):
    rows = own.shape[0]
    width = pieces[0].shape[1] // group
    tokens = mixed.shape[0] // group
    share = jax.ShapeDtypeStruct((tokens, width), mixed.dtype)
    return pl.pallas_call(
        lambda *refs: project_kernel(group, quads, *refs),
        out_shape=[share] * group,
        in_specs=[
            pl.BlockSpec(memory_space=pltpu.SMEM),
            pl.BlockSpec(memory_space=pltpu.VMEM),
            pl.BlockSpec(memory_space=pltpu.HBM),
        ]
        + [pl.BlockSpec(memory_space=pltpu.VMEM)] * (group - 1),
        out_specs=[pl.BlockSpec(memory_space=pltpu.VMEM)] * group,
        scratch_shapes=[
            pltpu.VMEM((group, rows, width), own.dtype),
            pltpu.VMEM((group, tokens, width), jnp.float32),
            pltpu.SemaphoreType.DMA((group,)),
        ],
        compiler_params=pltpu.CompilerParams(vmem_limit_bytes=60 * MIB),
        cost_estimate=pl.CostEstimate(
            flops=2 * mixed.size * group * width,
            bytes_accessed=2 * (mixed.size + 4 * rows * group * width + group * share.size),
            transcendentals=0,
        ),
    )(place, mixed, own, *pieces)


def finish_kernel(*refs):
    total = refs[0][...].astype(jnp.float32)
    for ref in refs[1:-1]:
        total = total + ref[...].astype(jnp.float32)
    refs[-1][...] = total.astype(refs[-1].dtype).T


def finish(shares):
    tokens, width = shares[0].shape
    return pl.pallas_call(
        finish_kernel,
        out_shape=jax.ShapeDtypeStruct((width, tokens), shares[0].dtype),
        in_specs=[pl.BlockSpec(memory_space=pltpu.VMEM)] * len(shares),
        out_specs=pl.BlockSpec(memory_space=pltpu.VMEM),
        compiler_params=pltpu.CompilerParams(vmem_limit_bytes=6 * MIB),
    )(*shares)


def dft_tables(blocks, tokens, channels):
    period = 2 * blocks
    total = period * tokens
    low = blocks + 1
    k1 = np.arange(low)
    i = np.arange(blocks)
    s = np.arange(tokens)
    first = 2 * np.pi * (np.outer(k1, i) % period) / period
    turn = 2 * np.pi * (np.outer(k1, s) % total) / total
    square = 2 * np.pi * (np.outer(s, s) % tokens) / tokens
    front = np.concatenate([np.cos(first), -np.sin(first)])
    weight = np.where((k1 == 0) | (k1 == blocks), 1.0, 2.0)[:, None] / total
    back = np.concatenate(
        [
            np.kron((weight * np.cos(first)).T, np.eye(channels)),
            np.kron(-(weight * np.sin(first)).T, np.eye(channels)),
        ],
        axis=1,
    )
    matrices = [jnp.asarray(m, jnp.bfloat16) for m in (front, np.cos(square), np.sin(square), back)]
    turns = [jnp.asarray(m, jnp.float32) for m in (np.cos(turn), np.sin(turn))]
    return matrices + turns


def matmul(left, right):
    return jnp.dot(left, right, preferred_element_type=jnp.float32)


def convolve_kernel(
    channels, in_ref, front_ref, square_cos_ref, square_sin_ref, back_ref, cos_ref, sin_ref, after_ref, out_ref
):
    del after_ref
    low, tokens = cos_ref.shape
    both = 2 * channels
    turn_cos = cos_ref[...].reshape(low, 1, tokens)
    turn_sin = sin_ref[...].reshape(low, 1, tokens)
    blocks = front_ref.shape[1]
    width = blocks * both
    repeat = lax.broadcasted_iota(jnp.int32, (blocks, width), 1) // both
    repeat = (repeat == lax.broadcasted_iota(jnp.int32, (blocks, width), 0)).astype(jnp.bfloat16)
    agree = lax.broadcasted_iota(jnp.int32, (both, width), 1) % both
    agree = agree == lax.broadcasted_iota(jnp.int32, (both, width), 0)
    entries = matmul(front_ref[...], repeat).reshape(2 * low, 1, width)
    front = jnp.where(agree[None], entries, 0.0).reshape(2 * low * both, width)
    spread = matmul(front.astype(jnp.bfloat16), in_ref[...])
    real = spread[: low * both].reshape(low, both, tokens)
    imag = spread[low * both :].reshape(low, both, tokens)
    turned_real = (real * turn_cos + imag * turn_sin).reshape(low * both, tokens).astype(jnp.bfloat16)
    turned_imag = (imag * turn_cos - real * turn_sin).reshape(low * both, tokens).astype(jnp.bfloat16)
    square_cos, square_sin = square_cos_ref[...], square_sin_ref[...]
    real = (matmul(turned_real, square_cos) + matmul(turned_imag, square_sin)).reshape(low, both, tokens)
    imag = (matmul(turned_imag, square_cos) - matmul(turned_real, square_sin)).reshape(low, both, tokens)
    sig_real, tap_real = real[:, :channels], real[:, channels:]
    sig_imag, tap_imag = imag[:, :channels], imag[:, channels:]
    prod_real = sig_real * tap_real - sig_imag * tap_imag
    prod_imag = sig_real * tap_imag + sig_imag * tap_real
    prod_real = prod_real.reshape(low * channels, tokens).astype(jnp.bfloat16)
    prod_imag = prod_imag.reshape(low * channels, tokens).astype(jnp.bfloat16)
    real = matmul(prod_real, square_cos) - matmul(prod_imag, square_sin)
    imag = matmul(prod_imag, square_cos) + matmul(prod_real, square_sin)
    real, imag = real.reshape(low, channels, tokens), imag.reshape(low, channels, tokens)
    rows = jnp.concatenate(
        [real * turn_cos - imag * turn_sin, real * turn_sin + imag * turn_cos], axis=0
    )
    out_ref[...] = matmul(
        back_ref[...], rows.reshape(2 * low * channels, tokens).astype(jnp.bfloat16)
    ).astype(out_ref.dtype)


def convolve(blocks_in, channels, tables, after):
    blocks, both, tokens = blocks_in.shape
    out = pl.pallas_call(
        lambda *refs: convolve_kernel(channels, *refs),
        out_shape=jax.ShapeDtypeStruct((blocks * channels, tokens), jnp.bfloat16),
        in_specs=[pl.BlockSpec(memory_space=pltpu.VMEM)] * (1 + len(tables))
        + [pl.BlockSpec(memory_space=pltpu.SMEM)],
        out_specs=pl.BlockSpec(memory_space=pltpu.VMEM),
        compiler_params=pltpu.CompilerParams(vmem_limit_bytes=32 * MIB),
        cost_estimate=pl.CostEstimate(
            flops=800_000_000, bytes_accessed=3_000_000, transcendentals=0
        ),
    )(blocks_in.reshape(blocks * both, tokens), *tables, after)
    return out.reshape(blocks, channels, tokens)


def outgoing_kernel(devices, signal_hbm, gate_hbm, taps_hbm, out_ref, signal_ref, gate_ref, taps_ref, sems):
    copies = [
        pltpu.make_async_copy(source, target, sems.at[n])
        for n, (source, target) in enumerate(
            [(signal_hbm, signal_ref), (gate_hbm, gate_ref), (taps_hbm, taps_ref)]
        )
    ]
    for copy in copies:
        copy.start()
    for copy in copies:
        copy.wait()
    rows, tokens = signal_ref.shape
    gated = signal_ref[...].astype(jnp.float32) * gate_ref[...].astype(jnp.float32)
    both = jnp.concatenate(
        [
            gated.reshape(devices, rows // devices, tokens),
            taps_ref[...].reshape(devices, rows // devices, tokens),
        ],
        axis=1,
    )
    out_ref[...] = both.reshape(2 * rows, tokens).astype(out_ref.dtype)


def outgoing(signal, pre_gate, filter_taps, devices):
    rows, tokens = signal.shape
    out = pl.pallas_call(
        lambda *refs: outgoing_kernel(devices, *refs),
        out_shape=jax.ShapeDtypeStruct((2 * rows, tokens), jnp.bfloat16),
        in_specs=[pl.BlockSpec(memory_space=pltpu.HBM)] * 3,
        out_specs=pl.BlockSpec(memory_space=pltpu.VMEM),
        scratch_shapes=[
            pltpu.VMEM(signal.shape, signal.dtype),
            pltpu.VMEM(pre_gate.shape, pre_gate.dtype),
            pltpu.VMEM(filter_taps.shape, filter_taps.dtype),
            pltpu.SemaphoreType.DMA((3,)),
        ],
        compiler_params=pltpu.CompilerParams(vmem_limit_bytes=60 * MIB),
    )(signal, pre_gate, filter_taps)
    return out.reshape(devices, 2 * rows // devices, tokens)


def gate_kernel(post_ref, signal_ref, pre_ref, convolved_ref, gain_ref, after_ref, out_ref):
    del after_ref
    gated = signal_ref[...].astype(jnp.float32) * pre_ref[...].astype(jnp.float32)
    inner = convolved_ref[...].astype(jnp.float32) + gain_ref[...] * gated
    out_ref[...] = (post_ref[...].astype(jnp.float32) * inner).astype(out_ref.dtype).T


def gate(post_gate, signal, pre_gate, convolved, skip_gain, after):
    corners = jnp.concatenate([array[:16, :128] for array in after])
    return pl.pallas_call(
        gate_kernel,
        out_shape=jax.ShapeDtypeStruct(post_gate.shape[::-1], post_gate.dtype),
        in_specs=[pl.BlockSpec(memory_space=pltpu.VMEM)] * 6,
        out_specs=pl.BlockSpec(memory_space=pltpu.VMEM),
        compiler_params=pltpu.CompilerParams(vmem_limit_bytes=6 * MIB),
        cost_estimate=pl.CostEstimate(
            flops=5 * post_gate.size, bytes_accessed=10 * post_gate.size, transcendentals=0
        ),
    )(post_gate, signal, pre_gate, convolved, skip_gain[:, None], corners)


def per_device(signal, pre_gate, post_gate, filter_taps, skip_gain, out_weight):
    channels_here, tokens_here = signal.shape
    devices = lax.axis_size("ctx")
    channels = channels_here // devices
    quads = lax.axis_size("quad")
    group = lax.axis_size("pair") * lax.axis_size("core")
    features = out_weight.shape[1]
    width = features // (quads * group)

    send = outgoing(signal, pre_gate, filter_taps, devices)
    blocks = lax.all_to_all(send, "ctx", split_axis=0, concat_axis=0, tiled=True)

    place = lax.axis_index(TP_AXES).astype(jnp.int32).reshape(1)
    members = [2, 3, 1]
    pieces, arranged = arrange(out_weight, place, group, quads, width, members)
    pieces = {
        r: lax.ppermute(piece, GROUP, [(t, t ^ r) for t in range(group)])
        for r, piece in zip(members, pieces)
    }
    pieces = [pieces[r] for r in range(1, group)]
    tables = dft_tables(devices, tokens_here, channels)
    convolved = convolve(blocks, channels, tables, arranged)
    inner, _ = arrange(out_weight, place, group, quads, width, [0, 1])
    weights = [inner[0]] + [
        lax.ppermute(piece, GROUP, [(t, t ^ r) for t in range(group)])
        for r, piece in zip(range(1, group), [inner[1]] + pieces)
    ]
    convolved = lax.all_to_all(convolved, "ctx", split_axis=0, concat_axis=0, tiled=True).reshape(
        channels_here, tokens_here
    )
    mixed = gate(post_gate, signal, pre_gate, convolved, skip_gain, pieces)
    gathered = lax.all_gather(mixed, GROUP, axis=0, tiled=True)
    shares = project(place, gathered, out_weight, pieces, group, quads)
    return finish([send_to_target(shares[step], step, quads) for step in range(3)] + [shares[3]])


def solution(mesh):
    ctx, tp = mesh.devices.shape
    fine = Mesh(mesh.devices.reshape(ctx, tp // 4, 2, 2), ("ctx",) + TP_AXES)
    return jax.shard_map(
        per_device,
        mesh=fine,
        in_specs=(
            P(TP_AXES, "ctx"),
            P(TP_AXES, "ctx"),
            P(TP_AXES, "ctx"),
            P(TP_AXES, "ctx"),
            P(TP_AXES),
            P(TP_AXES, None),
        ),
        out_specs=P(TP_AXES, "ctx"),
        check_vma=False,
    )
```

```python
import math

import jax
import jax.numpy as jnp
import numpy as np
from jax import lax
from jax.experimental import pallas as pl
from jax.experimental.pallas import tpu as pltpu
from jax.sharding import Mesh
from jax.sharding import PartitionSpec as P

TP_AXES = ("quad", "pair", "core")
GROUP = ("pair", "core")
MIB = 1 << 20


def targets_of(quad, pair, core, quads):
    onward = 2 * pair - 1
    far = lax.rem(quad + 2 * onward + quads, quads)
    near = lax.rem(quad + onward + quads, quads)
    chips = [(far, 1 - pair), (near, pair), (near, 1 - pair), (quad, pair)]
    return [(q * 2 + p) * 2 + core for q, p in chips]


def send_to_target(share, step, quads):
    pairs = []
    for quad in range(quads):
        for pair in range(2):
            onward = 1 if pair == 1 else -1
            q = (quad + (2 * onward if step == 0 else onward)) % quads
            p = pair if step == 1 else 1 - pair
            pairs += [((quad * 2 + pair) * 2 + c, (q * 2 + p) * 2 + c) for c in range(2)]
    return lax.ppermute(share, TP_AXES, pairs)


def arrange_kernel(group, quads, width, members, place_ref, weight_ref, *refs):
    count = len(members) * group
    out_refs, done_ref, blocks, in_sems, out_sems = refs[: len(members)], *refs[-4:]
    tp = place_ref[0]
    quad, place = tp // group, lax.rem(tp, group)
    loads, stores = [], []
    for n, r in enumerate(members):
        other = place ^ r
        for i, target in enumerate(targets_of(quad, other // 2, lax.rem(other, 2), quads)):
            k = n * group + i
            start = pl.multiple_of(target * width, width)
            loads.append(
                pltpu.make_async_copy(
                    weight_ref.at[:, pl.ds(start, width)], blocks.at[k], in_sems.at[k]
                )
            )
            stores.append(
                pltpu.make_async_copy(
                    blocks.at[k], out_refs[n].at[:, pl.ds(i * width, width)], out_sems.at[k]
                )
            )
    for load in loads:
        load.start()
    for k in range(count):
        loads[k].wait()
        stores[k].start()
    for store in stores:
        store.wait()
    done_ref[0] = tp


def arrange(out_weight, place, group, quads, width, members):
    rows = out_weight.shape[0]
    count = len(members) * group
    piece = jax.ShapeDtypeStruct((rows, group * width), out_weight.dtype)
    *pieces, done = pl.pallas_call(
        lambda *refs: arrange_kernel(group, quads, width, members, *refs),
        out_shape=[piece] * len(members) + [jax.ShapeDtypeStruct((1,), jnp.int32)],
        in_specs=[
            pl.BlockSpec(memory_space=pltpu.SMEM),
            pl.BlockSpec(memory_space=pltpu.HBM),
        ],
        out_specs=[pl.BlockSpec(memory_space=pltpu.HBM)] * len(members)
        + [pl.BlockSpec(memory_space=pltpu.SMEM)],
        scratch_shapes=[
            pltpu.VMEM((count, rows, width), out_weight.dtype),
            pltpu.SemaphoreType.DMA((count,)),
            pltpu.SemaphoreType.DMA((count,)),
        ],
        compiler_params=pltpu.CompilerParams(vmem_limit_bytes=60 * MIB),
        cost_estimate=pl.CostEstimate(
            flops=0, bytes_accessed=4 * rows * count * width, transcendentals=0
        ),
    )(place, out_weight)
    return pieces, done


def own_columns_kernel(group, quads, width, place_ref, weight_ref, out_ref, sems):
    tp = place_ref[0]
    quad, place = tp // group, lax.rem(tp, group)
    copies = []
    for i, target in enumerate(targets_of(quad, place // 2, lax.rem(place, 2), quads)):
        start = pl.multiple_of(target * width, width)
        copies.append(
            pltpu.make_async_copy(
                weight_ref.at[:, pl.ds(start, width)],
                out_ref.at[:, pl.ds(i * width, width)],
                sems.at[i],
            )
        )
    for copy in copies:
        copy.start()
    for copy in copies:
        copy.wait()


def own_columns(out_weight, place, group, quads, width):
    rows = out_weight.shape[0]
    return pl.pallas_call(
        lambda *refs: own_columns_kernel(group, quads, width, *refs),
        out_shape=jax.ShapeDtypeStruct((rows, group * width), out_weight.dtype),
        in_specs=[
            pl.BlockSpec(memory_space=pltpu.SMEM),
            pl.BlockSpec(memory_space=pltpu.HBM),
        ],
        out_specs=pl.BlockSpec(memory_space=pltpu.VMEM),
        scratch_shapes=[pltpu.SemaphoreType.DMA((group,))],
        compiler_params=pltpu.CompilerParams(vmem_limit_bytes=60 * MIB),
        cost_estimate=pl.CostEstimate(
            flops=0, bytes_accessed=4 * rows * group * width, transcendentals=0
        ),
    )(place, out_weight)


def project_kernel(group, place_ref, mixed_ref, *refs):
    weight_refs, out_refs = refs[:group], refs[group:]
    tokens = mixed_ref.shape[0] // group
    width = out_refs[0].shape[1]
    place = lax.rem(place_ref[0], group)
    mixed = [
        mixed_ref[pl.ds(pl.multiple_of((place ^ r) * tokens, tokens), tokens), :]
        for r in range(group)
    ]
    for i in range(group):
        total = None
        for r in range(group):
            term = jnp.dot(
                mixed[r],
                weight_refs[r][:, i * width : (i + 1) * width],
                preferred_element_type=jnp.float32,
            )
            total = term if total is None else total + term
        out_refs[i][...] = total.astype(out_refs[i].dtype)


def project(place, mixed, weights, width):
    group = len(weights)
    share = jax.ShapeDtypeStruct((mixed.shape[0] // group, width), mixed.dtype)
    return pl.pallas_call(
        lambda *refs: project_kernel(group, *refs),
        out_shape=[share] * group,
        in_specs=[pl.BlockSpec(memory_space=pltpu.SMEM)]
        + [pl.BlockSpec(memory_space=pltpu.VMEM)] * (1 + group),
        out_specs=[pl.BlockSpec(memory_space=pltpu.VMEM)] * group,
        compiler_params=pltpu.CompilerParams(vmem_limit_bytes=10 * MIB),
        cost_estimate=pl.CostEstimate(
            flops=2 * mixed.size * group * width,
            bytes_accessed=2 * (mixed.size + sum(w.size for w in weights) + group * share.size),
            transcendentals=0,
        ),
    )(place, mixed, *weights)


def finish_kernel(*refs):
    total = refs[0][...].astype(jnp.float32)
    for ref in refs[1:-1]:
        total = total + ref[...].astype(jnp.float32)
    refs[-1][...] = total.astype(refs[-1].dtype).T


def finish(shares):
    tokens, width = shares[0].shape
    return pl.pallas_call(
        finish_kernel,
        out_shape=jax.ShapeDtypeStruct((width, tokens), shares[0].dtype),
        in_specs=[pl.BlockSpec(memory_space=pltpu.VMEM)] * len(shares),
        out_specs=pl.BlockSpec(memory_space=pltpu.VMEM),
        compiler_params=pltpu.CompilerParams(vmem_limit_bytes=6 * MIB),
    )(*shares)


def dft_tables(blocks, tokens, channels):
    period = 2 * blocks
    total = period * tokens
    low = blocks + 1
    k1 = np.arange(low)
    i = np.arange(blocks)
    s = np.arange(tokens)
    first = 2 * np.pi * (np.outer(k1, i) % period) / period
    turn = 2 * np.pi * (np.outer(k1, s) % total) / total
    square = 2 * np.pi * (np.outer(s, s) % tokens) / tokens
    front = np.concatenate([np.cos(first), -np.sin(first)])
    weight = np.where((k1 == 0) | (k1 == blocks), 1.0, 2.0)[:, None] / total
    back = np.concatenate(
        [
            np.kron((weight * np.cos(first)).T, np.eye(channels)),
            np.kron(-(weight * np.sin(first)).T, np.eye(channels)),
        ],
        axis=1,
    )
    matrices = [jnp.asarray(m, jnp.bfloat16) for m in (front, np.cos(square), np.sin(square), back)]
    turns = [jnp.asarray(m, jnp.float32) for m in (np.cos(turn), np.sin(turn))]
    return matrices + turns


def matmul(left, right):
    return jnp.dot(left, right, preferred_element_type=jnp.float32)


def convolve_kernel(
    channels, in_ref, front_ref, square_cos_ref, square_sin_ref, back_ref, cos_ref, sin_ref, after_ref, out_ref
):
    del after_ref
    low, tokens = cos_ref.shape
    both = 2 * channels
    turn_cos = cos_ref[...].reshape(low, 1, tokens)
    turn_sin = sin_ref[...].reshape(low, 1, tokens)
    blocks = front_ref.shape[1]
    width = blocks * both
    repeat = lax.broadcasted_iota(jnp.int32, (blocks, width), 1) // both
    repeat = (repeat == lax.broadcasted_iota(jnp.int32, (blocks, width), 0)).astype(jnp.bfloat16)
    agree = lax.broadcasted_iota(jnp.int32, (both, width), 1) % both
    agree = agree == lax.broadcasted_iota(jnp.int32, (both, width), 0)
    entries = matmul(front_ref[...], repeat).reshape(2 * low, 1, width)
    front = jnp.where(agree[None], entries, 0.0).reshape(2 * low * both, width)
    spread = matmul(front.astype(jnp.bfloat16), in_ref[...])
    real = spread[: low * both].reshape(low, both, tokens)
    imag = spread[low * both :].reshape(low, both, tokens)
    turned_real = (real * turn_cos + imag * turn_sin).reshape(low * both, tokens).astype(jnp.bfloat16)
    turned_imag = (imag * turn_cos - real * turn_sin).reshape(low * both, tokens).astype(jnp.bfloat16)
    square_cos, square_sin = square_cos_ref[...], square_sin_ref[...]
    real = (matmul(turned_real, square_cos) + matmul(turned_imag, square_sin)).reshape(low, both, tokens)
    imag = (matmul(turned_imag, square_cos) - matmul(turned_real, square_sin)).reshape(low, both, tokens)
    sig_real, tap_real = real[:, :channels], real[:, channels:]
    sig_imag, tap_imag = imag[:, :channels], imag[:, channels:]
    prod_real = sig_real * tap_real - sig_imag * tap_imag
    prod_imag = sig_real * tap_imag + sig_imag * tap_real
    prod_real = prod_real.reshape(low * channels, tokens).astype(jnp.bfloat16)
    prod_imag = prod_imag.reshape(low * channels, tokens).astype(jnp.bfloat16)
    real = matmul(prod_real, square_cos) - matmul(prod_imag, square_sin)
    imag = matmul(prod_imag, square_cos) + matmul(prod_real, square_sin)
    real, imag = real.reshape(low, channels, tokens), imag.reshape(low, channels, tokens)
    rows = jnp.concatenate(
        [real * turn_cos - imag * turn_sin, real * turn_sin + imag * turn_cos], axis=0
    )
    out_ref[...] = matmul(
        back_ref[...], rows.reshape(2 * low * channels, tokens).astype(jnp.bfloat16)
    ).astype(out_ref.dtype)


def convolve(blocks_in, channels, tables, after):
    blocks, both, tokens = blocks_in.shape
    out = pl.pallas_call(
        lambda *refs: convolve_kernel(channels, *refs),
        out_shape=jax.ShapeDtypeStruct((blocks * channels, tokens), jnp.bfloat16),
        in_specs=[pl.BlockSpec(memory_space=pltpu.VMEM)] * (1 + len(tables))
        + [pl.BlockSpec(memory_space=pltpu.SMEM)],
        out_specs=pl.BlockSpec(memory_space=pltpu.VMEM),
        compiler_params=pltpu.CompilerParams(vmem_limit_bytes=32 * MIB),
        cost_estimate=pl.CostEstimate(
            flops=800_000_000, bytes_accessed=3_000_000, transcendentals=0
        ),
    )(blocks_in.reshape(blocks * both, tokens), *tables, after)
    return out.reshape(blocks, channels, tokens)


def outgoing_kernel(devices, signal_hbm, gate_hbm, taps_hbm, out_ref, signal_ref, gate_ref, taps_ref, sems):
    copies = [
        pltpu.make_async_copy(source, target, sems.at[n])
        for n, (source, target) in enumerate(
            [(signal_hbm, signal_ref), (gate_hbm, gate_ref), (taps_hbm, taps_ref)]
        )
    ]
    for copy in copies:
        copy.start()
    for copy in copies:
        copy.wait()
    rows, tokens = signal_ref.shape
    gated = signal_ref[...].astype(jnp.float32) * gate_ref[...].astype(jnp.float32)
    both = jnp.concatenate(
        [
            gated.reshape(devices, rows // devices, tokens),
            taps_ref[...].reshape(devices, rows // devices, tokens),
        ],
        axis=1,
    )
    out_ref[...] = both.reshape(2 * rows, tokens).astype(out_ref.dtype)


def outgoing(signal, pre_gate, filter_taps, devices):
    rows, tokens = signal.shape
    out = pl.pallas_call(
        lambda *refs: outgoing_kernel(devices, *refs),
        out_shape=jax.ShapeDtypeStruct((2 * rows, tokens), jnp.bfloat16),
        in_specs=[pl.BlockSpec(memory_space=pltpu.HBM)] * 3,
        out_specs=pl.BlockSpec(memory_space=pltpu.VMEM),
        scratch_shapes=[
            pltpu.VMEM(signal.shape, signal.dtype),
            pltpu.VMEM(pre_gate.shape, pre_gate.dtype),
            pltpu.VMEM(filter_taps.shape, filter_taps.dtype),
            pltpu.SemaphoreType.DMA((3,)),
        ],
        compiler_params=pltpu.CompilerParams(vmem_limit_bytes=60 * MIB),
    )(signal, pre_gate, filter_taps)
    return out.reshape(devices, 2 * rows // devices, tokens)


def gate_kernel(post_ref, signal_ref, pre_ref, convolved_ref, gain_ref, after_ref, out_ref):
    del after_ref
    gated = signal_ref[...].astype(jnp.float32) * pre_ref[...].astype(jnp.float32)
    inner = convolved_ref[...].astype(jnp.float32) + gain_ref[...] * gated
    out_ref[...] = (post_ref[...].astype(jnp.float32) * inner).astype(out_ref.dtype).T


def gate(post_gate, signal, pre_gate, convolved, skip_gain, after):
    corners = jnp.concatenate([array[:16, :128] for array in after])
    return pl.pallas_call(
        gate_kernel,
        out_shape=jax.ShapeDtypeStruct(post_gate.shape[::-1], post_gate.dtype),
        in_specs=[pl.BlockSpec(memory_space=pltpu.VMEM)] * 6,
        out_specs=pl.BlockSpec(memory_space=pltpu.VMEM),
        compiler_params=pltpu.CompilerParams(vmem_limit_bytes=6 * MIB),
        cost_estimate=pl.CostEstimate(
            flops=5 * post_gate.size, bytes_accessed=10 * post_gate.size, transcendentals=0
        ),
    )(post_gate, signal, pre_gate, convolved, skip_gain[:, None], corners)


def per_device(signal, pre_gate, post_gate, filter_taps, skip_gain, out_weight):
    channels_here, tokens_here = signal.shape
    devices = lax.axis_size("ctx")
    channels = channels_here // devices
    quads = lax.axis_size("quad")
    group = lax.axis_size("pair") * lax.axis_size("core")
    features = out_weight.shape[1]
    width = features // (quads * group)

    send = outgoing(signal, pre_gate, filter_taps, devices)
    blocks = lax.all_to_all(send, "ctx", split_axis=0, concat_axis=0, tiled=True)

    place = lax.axis_index(TP_AXES).astype(jnp.int32).reshape(1)
    members = [2, 3, 1]
    pieces, arranged = arrange(out_weight, place, group, quads, width, members)
    pieces = {
        r: lax.ppermute(piece, GROUP, [(t, t ^ r) for t in range(group)])
        for r, piece in zip(members, pieces)
    }
    pieces = [pieces[r] for r in range(1, group)]
    own = own_columns(out_weight, place, group, quads, width)
    tables = dft_tables(devices, tokens_here, channels)
    convolved = convolve(blocks, channels, tables, arranged)
    inner, _ = arrange(out_weight, place, group, quads, width, [0, 1])
    weights = [inner[0]] + [
        lax.ppermute(piece, GROUP, [(t, t ^ r) for t in range(group)])
        for r, piece in zip(range(1, group), [inner[1]] + pieces)
    ]
    convolved = lax.all_to_all(convolved, "ctx", split_axis=0, concat_axis=0, tiled=True).reshape(
        channels_here, tokens_here
    )
    mixed = gate(post_gate, signal, pre_gate, convolved, skip_gain, pieces)
    gathered = lax.all_gather(mixed, GROUP, axis=0, tiled=True)
    shares = project(place, gathered, [own] + pieces, width)
    return finish([send_to_target(shares[step], step, quads) for step in range(3)] + [shares[3]])


def solution(mesh):
    ctx, tp = mesh.devices.shape
    fine = Mesh(mesh.devices.reshape(ctx, tp // 4, 2, 2), ("ctx",) + TP_AXES)
    return jax.shard_map(
        per_device,
        mesh=fine,
        in_specs=(
            P(TP_AXES, "ctx"),
            P(TP_AXES, "ctx"),
            P(TP_AXES, "ctx"),
            P(TP_AXES, "ctx"),
            P(TP_AXES),
            P(TP_AXES, None),
        ),
        out_specs=P(TP_AXES, "ctx"),
        check_vma=False,
    )
```

```python
import math

import jax
import jax.numpy as jnp
import numpy as np
from jax import lax
from jax.experimental import pallas as pl
from jax.experimental.pallas import tpu as pltpu
from jax.sharding import Mesh
from jax.sharding import PartitionSpec as P

TP_AXES = ("quad", "pair", "core")
REMOTE = 3
TARGETS = 5
GROUP = ("pair", "core")
MIB = 1 << 20


def targets_of(quad, pair, core, quads):
    onward = 2 * pair - 1
    far = lax.rem(quad + 2 * onward + quads, quads)
    near = lax.rem(quad + onward + quads, quads)
    chips = [(far, 1 - pair), (near, pair), (near, 1 - pair), (quad, 1 - pair), (quad, pair)]
    return [(q * 2 + p) * 2 + core for q, p in chips]


def send_to_target(share, step, quads):
    pairs = []
    for quad in range(quads):
        for pair in range(2):
            onward = 1 if pair == 1 else -1
            q = (quad + (2 * onward, onward, onward, 0)[step]) % quads
            p = pair if step == 1 else 1 - pair
            pairs += [((quad * 2 + pair) * 2 + c, (q * 2 + p) * 2 + c) for c in range(2)]
    return lax.ppermute(share, TP_AXES, pairs)


def arrange_kernel(group, quads, width, members, place_ref, weight_ref, *refs):
    out_refs, done_ref, blocks, in_sems, out_sems = refs[: len(members)], *refs[-4:]
    tp = place_ref[0]
    quad, place = tp // group, lax.rem(tp, group)
    loads, stores = [], []
    for n, r in enumerate(members):
        other = place ^ r
        targets = targets_of(quad, other // 2, lax.rem(other, 2), quads)
        for i, target in enumerate(targets[: out_refs[n].shape[1] // width]):
            k = len(loads)
            start = pl.multiple_of(target * width, width)
            loads.append(
                pltpu.make_async_copy(
                    weight_ref.at[:, pl.ds(start, width)], blocks.at[k], in_sems.at[k]
                )
            )
            stores.append(
                pltpu.make_async_copy(
                    blocks.at[k], out_refs[n].at[:, pl.ds(i * width, width)], out_sems.at[k]
                )
            )
    for load in loads:
        load.start()
    for load, store in zip(loads, stores):
        load.wait()
        store.start()
    for store in stores:
        store.wait()
    done_ref[0] = tp


def arrange(out_weight, place, group, quads, width, members):
    rows = out_weight.shape[0]
    counts = [TARGETS if r < 2 else REMOTE for r in members]
    *pieces, done = pl.pallas_call(
        lambda *refs: arrange_kernel(group, quads, width, members, *refs),
        out_shape=[jax.ShapeDtypeStruct((rows, n * width), out_weight.dtype) for n in counts]
        + [jax.ShapeDtypeStruct((1,), jnp.int32)],
        in_specs=[
            pl.BlockSpec(memory_space=pltpu.SMEM),
            pl.BlockSpec(memory_space=pltpu.HBM),
        ],
        out_specs=[pl.BlockSpec(memory_space=pltpu.HBM)] * len(members)
        + [pl.BlockSpec(memory_space=pltpu.SMEM)],
        scratch_shapes=[
            pltpu.VMEM((sum(counts), rows, width), out_weight.dtype),
            pltpu.SemaphoreType.DMA((sum(counts),)),
            pltpu.SemaphoreType.DMA((sum(counts),)),
        ],
        compiler_params=pltpu.CompilerParams(vmem_limit_bytes=60 * MIB),
        cost_estimate=pl.CostEstimate(
            flops=0, bytes_accessed=4 * rows * sum(counts) * width, transcendentals=0
        ),
    )(place, out_weight)
    return pieces, done


def own_columns_kernel(group, quads, width, place_ref, weight_ref, out_ref, sems):
    tp = place_ref[0]
    quad, place = tp // group, lax.rem(tp, group)
    copies = []
    for i, target in enumerate(targets_of(quad, place // 2, lax.rem(place, 2), quads)):
        start = pl.multiple_of(target * width, width)
        copies.append(
            pltpu.make_async_copy(
                weight_ref.at[:, pl.ds(start, width)],
                out_ref.at[:, pl.ds(i * width, width)],
                sems.at[i],
            )
        )
    for copy in copies:
        copy.start()
    for copy in copies:
        copy.wait()


def own_columns(out_weight, place, group, quads, width):
    rows = out_weight.shape[0]
    return pl.pallas_call(
        lambda *refs: own_columns_kernel(group, quads, width, *refs),
        out_shape=jax.ShapeDtypeStruct((rows, TARGETS * width), out_weight.dtype),
        in_specs=[
            pl.BlockSpec(memory_space=pltpu.SMEM),
            pl.BlockSpec(memory_space=pltpu.HBM),
        ],
        out_specs=pl.BlockSpec(memory_space=pltpu.VMEM),
        scratch_shapes=[pltpu.SemaphoreType.DMA((TARGETS,))],
        compiler_params=pltpu.CompilerParams(vmem_limit_bytes=60 * MIB),
        cost_estimate=pl.CostEstimate(
            flops=0, bytes_accessed=4 * rows * TARGETS * width, transcendentals=0
        ),
    )(place, out_weight)


def project_kernel(group, place_ref, mixed_ref, *refs):
    weight_refs, out_refs = refs[:group], refs[group:]
    tokens = mixed_ref.shape[0] // group
    width = out_refs[0].shape[1]
    place = lax.rem(place_ref[0], group)
    mixed = [
        mixed_ref[pl.ds(pl.multiple_of((place ^ r) * tokens, tokens), tokens), :]
        for r in range(group)
    ]
    for i in range(TARGETS):
        total = None
        for r in range(group if i < REMOTE else 2):
            term = jnp.dot(
                mixed[r],
                weight_refs[r][:, i * width : (i + 1) * width],
                preferred_element_type=jnp.float32,
            )
            total = term if total is None else total + term
        out_refs[i][...] = total.astype(out_refs[i].dtype)


def project(place, mixed, weights, width):
    group = len(weights)
    share = jax.ShapeDtypeStruct((mixed.shape[0] // group, width), mixed.dtype)
    return pl.pallas_call(
        lambda *refs: project_kernel(group, *refs),
        out_shape=[share] * TARGETS,
        in_specs=[pl.BlockSpec(memory_space=pltpu.SMEM)]
        + [pl.BlockSpec(memory_space=pltpu.VMEM)] * (1 + group),
        out_specs=[pl.BlockSpec(memory_space=pltpu.VMEM)] * TARGETS,
        compiler_params=pltpu.CompilerParams(vmem_limit_bytes=10 * MIB),
        cost_estimate=pl.CostEstimate(
            flops=2 * mixed.size * 4 * width,
            bytes_accessed=2 * (mixed.size + sum(w.size for w in weights) + TARGETS * share.size),
            transcendentals=0,
        ),
    )(place, mixed, *weights)


def finish_kernel(*refs):
    total = refs[0][...].astype(jnp.float32)
    for ref in refs[1:-1]:
        total = total + ref[...].astype(jnp.float32)
    refs[-1][...] = total.astype(refs[-1].dtype).T


def finish(shares):
    tokens, width = shares[0].shape
    return pl.pallas_call(
        finish_kernel,
        out_shape=jax.ShapeDtypeStruct((width, tokens), shares[0].dtype),
        in_specs=[pl.BlockSpec(memory_space=pltpu.VMEM)] * len(shares),
        out_specs=pl.BlockSpec(memory_space=pltpu.VMEM),
        compiler_params=pltpu.CompilerParams(vmem_limit_bytes=6 * MIB),
    )(*shares)


def dft_tables(blocks, tokens, channels):
    period = 2 * blocks
    total = period * tokens
    low = blocks + 1
    k1 = np.arange(low)
    i = np.arange(blocks)
    s = np.arange(tokens)
    first = 2 * np.pi * (np.outer(k1, i) % period) / period
    turn = 2 * np.pi * (np.outer(k1, s) % total) / total
    square = 2 * np.pi * (np.outer(s, s) % tokens) / tokens
    front = np.concatenate([np.cos(first), -np.sin(first)])
    weight = np.where((k1 == 0) | (k1 == blocks), 1.0, 2.0)[:, None] / total
    back = np.concatenate(
        [
            np.kron((weight * np.cos(first)).T, np.eye(channels)),
            np.kron(-(weight * np.sin(first)).T, np.eye(channels)),
        ],
        axis=1,
    )
    matrices = [jnp.asarray(m, jnp.bfloat16) for m in (front, np.cos(square), np.sin(square), back)]
    turns = [jnp.asarray(m, jnp.float32) for m in (np.cos(turn), np.sin(turn))]
    return matrices + turns


def matmul(left, right):
    return jnp.dot(left, right, preferred_element_type=jnp.float32)


def convolve_kernel(
    channels, in_ref, front_ref, square_cos_ref, square_sin_ref, back_ref, cos_ref, sin_ref, after_ref, out_ref
):
    del after_ref
    low, tokens = cos_ref.shape
    both = 2 * channels
    turn_cos = cos_ref[...].reshape(low, 1, tokens)
    turn_sin = sin_ref[...].reshape(low, 1, tokens)
    blocks = front_ref.shape[1]
    width = blocks * both
    repeat = lax.broadcasted_iota(jnp.int32, (blocks, width), 1) // both
    repeat = (repeat == lax.broadcasted_iota(jnp.int32, (blocks, width), 0)).astype(jnp.bfloat16)
    agree = lax.broadcasted_iota(jnp.int32, (both, width), 1) % both
    agree = agree == lax.broadcasted_iota(jnp.int32, (both, width), 0)
    entries = matmul(front_ref[...], repeat).reshape(2 * low, 1, width)
    front = jnp.where(agree[None], entries, 0.0).reshape(2 * low * both, width)
    spread = matmul(front.astype(jnp.bfloat16), in_ref[...])
    real = spread[: low * both].reshape(low, both, tokens)
    imag = spread[low * both :].reshape(low, both, tokens)
    turned_real = (real * turn_cos + imag * turn_sin).reshape(low * both, tokens).astype(jnp.bfloat16)
    turned_imag = (imag * turn_cos - real * turn_sin).reshape(low * both, tokens).astype(jnp.bfloat16)
    square_cos, square_sin = square_cos_ref[...], square_sin_ref[...]
    real = (matmul(turned_real, square_cos) + matmul(turned_imag, square_sin)).reshape(low, both, tokens)
    imag = (matmul(turned_imag, square_cos) - matmul(turned_real, square_sin)).reshape(low, both, tokens)
    sig_real, tap_real = real[:, :channels], real[:, channels:]
    sig_imag, tap_imag = imag[:, :channels], imag[:, channels:]
    prod_real = sig_real * tap_real - sig_imag * tap_imag
    prod_imag = sig_real * tap_imag + sig_imag * tap_real
    prod_real = prod_real.reshape(low * channels, tokens).astype(jnp.bfloat16)
    prod_imag = prod_imag.reshape(low * channels, tokens).astype(jnp.bfloat16)
    real = matmul(prod_real, square_cos) - matmul(prod_imag, square_sin)
    imag = matmul(prod_imag, square_cos) + matmul(prod_real, square_sin)
    real, imag = real.reshape(low, channels, tokens), imag.reshape(low, channels, tokens)
    rows = jnp.concatenate(
        [real * turn_cos - imag * turn_sin, real * turn_sin + imag * turn_cos], axis=0
    )
    out_ref[...] = matmul(
        back_ref[...], rows.reshape(2 * low * channels, tokens).astype(jnp.bfloat16)
    ).astype(out_ref.dtype)


def convolve(blocks_in, channels, tables, after):
    blocks, both, tokens = blocks_in.shape
    out = pl.pallas_call(
        lambda *refs: convolve_kernel(channels, *refs),
        out_shape=jax.ShapeDtypeStruct((blocks * channels, tokens), jnp.bfloat16),
        in_specs=[pl.BlockSpec(memory_space=pltpu.VMEM)] * (1 + len(tables))
        + [pl.BlockSpec(memory_space=pltpu.SMEM)],
        out_specs=pl.BlockSpec(memory_space=pltpu.VMEM),
        compiler_params=pltpu.CompilerParams(vmem_limit_bytes=32 * MIB),
        cost_estimate=pl.CostEstimate(
            flops=800_000_000, bytes_accessed=3_000_000, transcendentals=0
        ),
    )(blocks_in.reshape(blocks * both, tokens), *tables, after)
    return out.reshape(blocks, channels, tokens)


def outgoing_kernel(devices, signal_hbm, gate_hbm, taps_hbm, out_ref, signal_ref, gate_ref, taps_ref, sems):
    copies = [
        pltpu.make_async_copy(source, target, sems.at[n])
        for n, (source, target) in enumerate(
            [(signal_hbm, signal_ref), (gate_hbm, gate_ref), (taps_hbm, taps_ref)]
        )
    ]
    for copy in copies:
        copy.start()
    for copy in copies:
        copy.wait()
    rows, tokens = signal_ref.shape
    gated = signal_ref[...].astype(jnp.float32) * gate_ref[...].astype(jnp.float32)
    both = jnp.concatenate(
        [
            gated.reshape(devices, rows // devices, tokens),
            taps_ref[...].reshape(devices, rows // devices, tokens),
        ],
        axis=1,
    )
    out_ref[...] = both.reshape(2 * rows, tokens).astype(out_ref.dtype)


def outgoing(signal, pre_gate, filter_taps, devices):
    rows, tokens = signal.shape
    out = pl.pallas_call(
        lambda *refs: outgoing_kernel(devices, *refs),
        out_shape=jax.ShapeDtypeStruct((2 * rows, tokens), jnp.bfloat16),
        in_specs=[pl.BlockSpec(memory_space=pltpu.HBM)] * 3,
        out_specs=pl.BlockSpec(memory_space=pltpu.VMEM),
        scratch_shapes=[
            pltpu.VMEM(signal.shape, signal.dtype),
            pltpu.VMEM(pre_gate.shape, pre_gate.dtype),
            pltpu.VMEM(filter_taps.shape, filter_taps.dtype),
            pltpu.SemaphoreType.DMA((3,)),
        ],
        compiler_params=pltpu.CompilerParams(vmem_limit_bytes=60 * MIB),
    )(signal, pre_gate, filter_taps)
    return out.reshape(devices, 2 * rows // devices, tokens)


def gate_kernel(post_ref, signal_ref, pre_ref, convolved_ref, gain_ref, after_ref, out_ref):
    del after_ref
    gated = signal_ref[...].astype(jnp.float32) * pre_ref[...].astype(jnp.float32)
    inner = convolved_ref[...].astype(jnp.float32) + gain_ref[...] * gated
    out_ref[...] = (post_ref[...].astype(jnp.float32) * inner).astype(out_ref.dtype).T


def gate(post_gate, signal, pre_gate, convolved, skip_gain, after):
    corners = jnp.concatenate([array[:16, :128] for array in after])
    return pl.pallas_call(
        gate_kernel,
        out_shape=jax.ShapeDtypeStruct(post_gate.shape[::-1], post_gate.dtype),
        in_specs=[pl.BlockSpec(memory_space=pltpu.VMEM)] * 6,
        out_specs=pl.BlockSpec(memory_space=pltpu.VMEM),
        compiler_params=pltpu.CompilerParams(vmem_limit_bytes=6 * MIB),
        cost_estimate=pl.CostEstimate(
            flops=5 * post_gate.size, bytes_accessed=10 * post_gate.size, transcendentals=0
        ),
    )(post_gate, signal, pre_gate, convolved, skip_gain[:, None], corners)


def per_device(signal, pre_gate, post_gate, filter_taps, skip_gain, out_weight):
    channels_here, tokens_here = signal.shape
    devices = lax.axis_size("ctx")
    channels = channels_here // devices
    quads = lax.axis_size("quad")
    group = lax.axis_size("pair") * lax.axis_size("core")
    features = out_weight.shape[1]
    width = features // (quads * group)

    send = outgoing(signal, pre_gate, filter_taps, devices)
    blocks = lax.all_to_all(send, "ctx", split_axis=0, concat_axis=0, tiled=True)

    place = lax.axis_index(TP_AXES).astype(jnp.int32).reshape(1)
    members = [2, 3, 1]
    pieces, arranged = arrange(out_weight, place, group, quads, width, members)
    pieces = {
        r: lax.ppermute(piece, GROUP, [(t, t ^ r) for t in range(group)])
        for r, piece in zip(members, pieces)
    }
    pieces = [pieces[r] for r in range(1, group)]
    own = own_columns(out_weight, place, group, quads, width)
    tables = dft_tables(devices, tokens_here, channels)
    convolved = convolve(blocks, channels, tables, arranged)
    inner, _ = arrange(out_weight, place, group, quads, width, [0, 1])
    weights = [inner[0]] + [
        lax.ppermute(piece, GROUP, [(t, t ^ r) for t in range(group)])
        for r, piece in zip(range(1, group), [inner[1]] + pieces)
    ]
    convolved = lax.all_to_all(convolved, "ctx", split_axis=0, concat_axis=0, tiled=True).reshape(
        channels_here, tokens_here
    )
    mixed = gate(post_gate, signal, pre_gate, convolved, skip_gain, pieces[1:] + pieces[:1])
    gathered = lax.all_gather(mixed, GROUP, axis=0, tiled=True)
    shares = project(place, gathered, [own] + pieces, width)
    received = [send_to_target(shares[step], step, quads) for step in range(TARGETS - 1)]
    return finish(received + [shares[-1]])


def solution(mesh):
    ctx, tp = mesh.devices.shape
    fine = Mesh(mesh.devices.reshape(ctx, tp // 4, 2, 2), ("ctx",) + TP_AXES)
    return jax.shard_map(
        per_device,
        mesh=fine,
        in_specs=(
            P(TP_AXES, "ctx"),
            P(TP_AXES, "ctx"),
            P(TP_AXES, "ctx"),
            P(TP_AXES, "ctx"),
            P(TP_AXES),
            P(TP_AXES, None),
        ),
        out_specs=P(TP_AXES, "ctx"),
        check_vma=False,
    )
```

```python
import math

import jax
import jax.numpy as jnp
import numpy as np
from jax import lax
from jax.experimental import pallas as pl
from jax.experimental.pallas import tpu as pltpu
from jax.sharding import Mesh
from jax.sharding import PartitionSpec as P

TP_AXES = ("quad", "pair", "core")
GROUP = ("pair", "core")
MIB = 1 << 20


def targets_of(quad, pair, core, quads):
    onward = 2 * pair - 1
    far = lax.rem(quad + 2 * onward + quads, quads)
    near = lax.rem(quad + onward + quads, quads)
    chips = [(far, 1 - pair), (near, pair), (near, 1 - pair), (quad, pair)]
    return [(q * 2 + p) * 2 + core for q, p in chips]


def send_to_target(share, step, quads):
    pairs = []
    for quad in range(quads):
        for pair in range(2):
            onward = 1 if pair == 1 else -1
            q = (quad + (2 * onward if step == 0 else onward)) % quads
            p = pair if step == 1 else 1 - pair
            pairs += [((quad * 2 + pair) * 2 + c, (q * 2 + p) * 2 + c) for c in range(2)]
    return lax.ppermute(share, TP_AXES, pairs)


def arrange_kernel(group, quads, width, members, place_ref, weight_ref, *refs):
    count = len(members) * group
    out_refs, done_ref, blocks, in_sems, out_sems = refs[: len(members)], *refs[-4:]
    tp = place_ref[0]
    quad, place = tp // group, lax.rem(tp, group)
    loads, stores = [], []
    for n, r in enumerate(members):
        other = place ^ r
        for i, target in enumerate(targets_of(quad, other // 2, lax.rem(other, 2), quads)):
            k = n * group + i
            start = pl.multiple_of(target * width, width)
            loads.append(
                pltpu.make_async_copy(
                    weight_ref.at[:, pl.ds(start, width)], blocks.at[k], in_sems.at[k]
                )
            )
            stores.append(
                pltpu.make_async_copy(
                    blocks.at[k], out_refs[n].at[:, pl.ds(i * width, width)], out_sems.at[k]
                )
            )
    for load in loads:
        load.start()
    for k in range(count):
        loads[k].wait()
        stores[k].start()
    for store in stores:
        store.wait()
    done_ref[0] = tp


def arrange(out_weight, place, group, quads, width, members):
    rows = out_weight.shape[0]
    count = len(members) * group
    piece = jax.ShapeDtypeStruct((rows, group * width), out_weight.dtype)
    *pieces, done = pl.pallas_call(
        lambda *refs: arrange_kernel(group, quads, width, members, *refs),
        out_shape=[piece] * len(members) + [jax.ShapeDtypeStruct((1,), jnp.int32)],
        in_specs=[
            pl.BlockSpec(memory_space=pltpu.SMEM),
            pl.BlockSpec(memory_space=pltpu.HBM),
        ],
        out_specs=[pl.BlockSpec(memory_space=pltpu.HBM)] * len(members)
        + [pl.BlockSpec(memory_space=pltpu.SMEM)],
        scratch_shapes=[
            pltpu.VMEM((count, rows, width), out_weight.dtype),
            pltpu.SemaphoreType.DMA((count,)),
            pltpu.SemaphoreType.DMA((count,)),
        ],
        compiler_params=pltpu.CompilerParams(vmem_limit_bytes=60 * MIB),
        cost_estimate=pl.CostEstimate(
            flops=0, bytes_accessed=4 * rows * count * width, transcendentals=0
        ),
    )(place, out_weight)
    return pieces, done


def own_columns_kernel(group, quads, width, place_ref, weight_ref, out_ref, sems):
    tp = place_ref[0]
    quad, place = tp // group, lax.rem(tp, group)
    copies = []
    for i, target in enumerate(targets_of(quad, place // 2, lax.rem(place, 2), quads)):
        start = pl.multiple_of(target * width, width)
        copies.append(
            pltpu.make_async_copy(
                weight_ref.at[:, pl.ds(start, width)],
                out_ref.at[:, pl.ds(i * width, width)],
                sems.at[i],
            )
        )
    for copy in copies:
        copy.start()
    for copy in copies:
        copy.wait()


def own_columns(out_weight, place, group, quads, width):
    rows = out_weight.shape[0]
    return pl.pallas_call(
        lambda *refs: own_columns_kernel(group, quads, width, *refs),
        out_shape=jax.ShapeDtypeStruct((rows, group * width), out_weight.dtype),
        in_specs=[
            pl.BlockSpec(memory_space=pltpu.SMEM),
            pl.BlockSpec(memory_space=pltpu.HBM),
        ],
        out_specs=pl.BlockSpec(memory_space=pltpu.VMEM),
        scratch_shapes=[pltpu.SemaphoreType.DMA((group,))],
        compiler_params=pltpu.CompilerParams(vmem_limit_bytes=60 * MIB),
        cost_estimate=pl.CostEstimate(
            flops=0, bytes_accessed=4 * rows * group * width, transcendentals=0
        ),
    )(place, out_weight)


def project_kernel(group, place_ref, mixed_ref, own_hbm, *refs):
    out_refs, own_ref, sem = refs[group - 1 : -2], refs[-2], refs[-1]
    load = pltpu.make_async_copy(own_hbm, own_ref, sem)
    load.start()
    weight_refs = (own_ref,) + refs[: group - 1]
    tokens = mixed_ref.shape[0] // group
    width = out_refs[0].shape[1]
    place = lax.rem(place_ref[0], group)
    mixed = [
        mixed_ref[pl.ds(pl.multiple_of((place ^ r) * tokens, tokens), tokens), :]
        for r in range(group)
    ]

    def product(r, i):
        weights = weight_refs[r][:, i * width : (i + 1) * width]
        return jnp.dot(mixed[r], weights, preferred_element_type=jnp.float32)

    totals = [sum(product(r, i) for r in range(1, group)) for i in range(group)]
    load.wait()
    for i in range(group):
        out_refs[i][...] = (totals[i] + product(0, i)).astype(out_refs[i].dtype)


def project(place, mixed, weights, width):
    group = len(weights)
    share = jax.ShapeDtypeStruct((mixed.shape[0] // group, width), mixed.dtype)
    return pl.pallas_call(
        lambda *refs: project_kernel(group, *refs),
        out_shape=[share] * group,
        in_specs=[pl.BlockSpec(memory_space=pltpu.SMEM)]
        + [pl.BlockSpec(memory_space=pltpu.VMEM), pl.BlockSpec(memory_space=pltpu.HBM)]
        + [pl.BlockSpec(memory_space=pltpu.VMEM)] * (group - 1),
        out_specs=[pl.BlockSpec(memory_space=pltpu.VMEM)] * group,
        scratch_shapes=[
            pltpu.VMEM(weights[0].shape, weights[0].dtype),
            pltpu.SemaphoreType.DMA,
        ],
        compiler_params=pltpu.CompilerParams(vmem_limit_bytes=10 * MIB),
        cost_estimate=pl.CostEstimate(
            flops=2 * mixed.size * group * width,
            bytes_accessed=2 * (mixed.size + sum(w.size for w in weights) + group * share.size),
            transcendentals=0,
        ),
    )(place, mixed, pltpu.with_memory_space_constraint(weights[0], pltpu.HBM), *weights[1:])


def finish_kernel(*refs):
    total = refs[0][...].astype(jnp.float32)
    for ref in refs[1:-1]:
        total = total + ref[...].astype(jnp.float32)
    refs[-1][...] = total.astype(refs[-1].dtype).T


def finish(shares):
    tokens, width = shares[0].shape
    return pl.pallas_call(
        finish_kernel,
        out_shape=jax.ShapeDtypeStruct((width, tokens), shares[0].dtype),
        in_specs=[pl.BlockSpec(memory_space=pltpu.VMEM)] * len(shares),
        out_specs=pl.BlockSpec(memory_space=pltpu.VMEM),
        compiler_params=pltpu.CompilerParams(vmem_limit_bytes=6 * MIB),
    )(*shares)


def dft_tables(blocks, tokens, channels):
    period = 2 * blocks
    total = period * tokens
    low = blocks + 1
    k1 = np.arange(low)
    i = np.arange(blocks)
    s = np.arange(tokens)
    first = 2 * np.pi * (np.outer(k1, i) % period) / period
    turn = 2 * np.pi * (np.outer(k1, s) % total) / total
    square = 2 * np.pi * (np.outer(s, s) % tokens) / tokens
    front = np.concatenate([np.cos(first), -np.sin(first)])
    weight = np.where((k1 == 0) | (k1 == blocks), 1.0, 2.0)[:, None] / total
    back = np.concatenate(
        [
            np.kron((weight * np.cos(first)).T, np.eye(channels)),
            np.kron(-(weight * np.sin(first)).T, np.eye(channels)),
        ],
        axis=1,
    )
    matrices = [jnp.asarray(m, jnp.bfloat16) for m in (front, np.cos(square), np.sin(square), back)]
    turns = [jnp.asarray(m, jnp.float32) for m in (np.cos(turn), np.sin(turn))]
    return matrices + turns


def matmul(left, right):
    return jnp.dot(left, right, preferred_element_type=jnp.float32)


def convolve_kernel(
    channels, in_ref, front_ref, square_cos_ref, square_sin_ref, back_ref, cos_ref, sin_ref, after_ref, out_ref, rows_ref
):
    del after_ref
    low, tokens = cos_ref.shape
    both = 2 * channels
    blocks = front_ref.shape[1]
    width = blocks * both
    repeat = lax.broadcasted_iota(jnp.int32, (blocks, width), 1) // both
    repeat = (repeat == lax.broadcasted_iota(jnp.int32, (blocks, width), 0)).astype(jnp.bfloat16)
    agree = lax.broadcasted_iota(jnp.int32, (both, width), 1) % both
    agree = (agree == lax.broadcasted_iota(jnp.int32, (both, width), 0))[None]
    entries = matmul(front_ref[...], repeat)
    turn_cos = cos_ref[...].reshape(low, 1, tokens)
    turn_sin = sin_ref[...].reshape(low, 1, tokens)

    def spread(part):
        part = jnp.where(agree, part.reshape(low, 1, width), 0.0)
        part = part.reshape(low * both, width).astype(jnp.bfloat16)
        return matmul(part, in_ref[...]).reshape(low, both, tokens)

    def flat(array):
        return array.reshape(-1, tokens).astype(jnp.bfloat16)

    real, imag = spread(entries[:low]), spread(entries[low:])
    turned_real = flat(real * turn_cos + imag * turn_sin)
    turned_imag = flat(imag * turn_cos - real * turn_sin)
    square_cos, square_sin = square_cos_ref[...], square_sin_ref[...]
    real = matmul(turned_real, square_cos) + matmul(turned_imag, square_sin)
    imag = matmul(turned_imag, square_cos) - matmul(turned_real, square_sin)
    real, imag = real.reshape(low, both, tokens), imag.reshape(low, both, tokens)
    sig_real, tap_real = real[:, :channels], real[:, channels:]
    sig_imag, tap_imag = imag[:, :channels], imag[:, channels:]
    prod_real = flat(sig_real * tap_real - sig_imag * tap_imag)
    prod_imag = flat(sig_real * tap_imag + sig_imag * tap_real)
    real = matmul(prod_real, square_cos) - matmul(prod_imag, square_sin)
    imag = matmul(prod_imag, square_cos) + matmul(prod_real, square_sin)
    real, imag = real.reshape(low, channels, tokens), imag.reshape(low, channels, tokens)
    half = low * channels
    rows_ref[:half, :] = (real * turn_cos - imag * turn_sin).reshape(half, tokens)
    rows_ref[half:, :] = (real * turn_sin + imag * turn_cos).reshape(half, tokens)
    out_ref[...] = matmul(back_ref[...], rows_ref[...].astype(jnp.bfloat16)).astype(out_ref.dtype)


def convolve(blocks_in, channels, tables, after):
    blocks, both, tokens = blocks_in.shape
    out = pl.pallas_call(
        lambda *refs: convolve_kernel(channels, *refs),
        out_shape=jax.ShapeDtypeStruct((blocks * channels, tokens), jnp.bfloat16),
        in_specs=[pl.BlockSpec(memory_space=pltpu.VMEM)] * (1 + len(tables))
        + [pl.BlockSpec(memory_space=pltpu.SMEM)],
        out_specs=pl.BlockSpec(memory_space=pltpu.VMEM),
        scratch_shapes=[pltpu.VMEM((2 * tables[-1].shape[0] * channels, tokens), jnp.float32)],
        compiler_params=pltpu.CompilerParams(vmem_limit_bytes=32 * MIB),
        cost_estimate=pl.CostEstimate(
            flops=800_000_000, bytes_accessed=3_000_000, transcendentals=0
        ),
    )(blocks_in.reshape(blocks * both, tokens), *tables, after)
    return out.reshape(blocks, channels, tokens)


def outgoing_kernel(devices, signal_hbm, gate_hbm, taps_hbm, out_ref, signal_ref, gate_ref, taps_ref, sems):
    copies = [
        pltpu.make_async_copy(source, target, sems.at[n])
        for n, (source, target) in enumerate(
            [(signal_hbm, signal_ref), (gate_hbm, gate_ref), (taps_hbm, taps_ref)]
        )
    ]
    for copy in copies:
        copy.start()
    for copy in copies:
        copy.wait()
    rows, tokens = signal_ref.shape
    gated = signal_ref[...].astype(jnp.float32) * gate_ref[...].astype(jnp.float32)
    both = jnp.concatenate(
        [
            gated.reshape(devices, rows // devices, tokens),
            taps_ref[...].reshape(devices, rows // devices, tokens),
        ],
        axis=1,
    )
    out_ref[...] = both.reshape(2 * rows, tokens).astype(out_ref.dtype)


def outgoing(signal, pre_gate, filter_taps, devices):
    rows, tokens = signal.shape
    out = pl.pallas_call(
        lambda *refs: outgoing_kernel(devices, *refs),
        out_shape=jax.ShapeDtypeStruct((2 * rows, tokens), jnp.bfloat16),
        in_specs=[pl.BlockSpec(memory_space=pltpu.HBM)] * 3,
        out_specs=pl.BlockSpec(memory_space=pltpu.VMEM),
        scratch_shapes=[
            pltpu.VMEM(signal.shape, signal.dtype),
            pltpu.VMEM(pre_gate.shape, pre_gate.dtype),
            pltpu.VMEM(filter_taps.shape, filter_taps.dtype),
            pltpu.SemaphoreType.DMA((3,)),
        ],
        compiler_params=pltpu.CompilerParams(vmem_limit_bytes=60 * MIB),
    )(signal, pre_gate, filter_taps)
    return out.reshape(devices, 2 * rows // devices, tokens)


def gate_kernel(post_ref, signal_ref, pre_ref, convolved_ref, gain_ref, after_ref, out_ref):
    del after_ref
    gated = signal_ref[...].astype(jnp.float32) * pre_ref[...].astype(jnp.float32)
    inner = convolved_ref[...].astype(jnp.float32) + gain_ref[...] * gated
    out_ref[...] = (post_ref[...].astype(jnp.float32) * inner).astype(out_ref.dtype).T


def gate(post_gate, signal, pre_gate, convolved, skip_gain, after):
    corners = jnp.concatenate([array[:16, :128] for array in after])
    return pl.pallas_call(
        gate_kernel,
        out_shape=jax.ShapeDtypeStruct(post_gate.shape[::-1], post_gate.dtype),
        in_specs=[pl.BlockSpec(memory_space=pltpu.VMEM)] * 6,
        out_specs=pl.BlockSpec(memory_space=pltpu.VMEM),
        compiler_params=pltpu.CompilerParams(vmem_limit_bytes=6 * MIB),
        cost_estimate=pl.CostEstimate(
            flops=5 * post_gate.size, bytes_accessed=10 * post_gate.size, transcendentals=0
        ),
    )(post_gate, signal, pre_gate, convolved, skip_gain[:, None], corners)


def per_device(signal, pre_gate, post_gate, filter_taps, skip_gain, out_weight):
    channels_here, tokens_here = signal.shape
    devices = lax.axis_size("ctx")
    channels = channels_here // devices
    quads = lax.axis_size("quad")
    group = lax.axis_size("pair") * lax.axis_size("core")
    features = out_weight.shape[1]
    width = features // (quads * group)

    send = outgoing(signal, pre_gate, filter_taps, devices)
    blocks = lax.all_to_all(send, "ctx", split_axis=0, concat_axis=0, tiled=True)

    place = lax.axis_index(TP_AXES).astype(jnp.int32).reshape(1)
    members = [2, 3, 1]
    pieces, arranged = arrange(out_weight, place, group, quads, width, members)
    pieces = {
        r: lax.ppermute(piece, GROUP, [(t, t ^ r) for t in range(group)])
        for r, piece in zip(members, pieces)
    }
    pieces = [pieces[r] for r in range(1, group)]
    own = own_columns(out_weight, place, group, quads, width)
    tables = dft_tables(devices, tokens_here, channels)
    convolved = convolve(blocks, channels, tables, arranged)
    inner, _ = arrange(out_weight, place, group, quads, width, [0, 1])
    weights = [inner[0]] + [
        lax.ppermute(piece, GROUP, [(t, t ^ r) for t in range(group)])
        for r, piece in zip(range(1, group), [inner[1]] + pieces)
    ]
    convolved = lax.all_to_all(convolved, "ctx", split_axis=0, concat_axis=0, tiled=True).reshape(
        channels_here, tokens_here
    )
    mixed = gate(post_gate, signal, pre_gate, convolved, skip_gain, pieces)
    gathered = lax.all_gather(mixed, GROUP, axis=0, tiled=True)
    shares = project(place, gathered, [own] + pieces, width)
    return finish([send_to_target(shares[step], step, quads) for step in range(3)] + [shares[3]])


def solution(mesh):
    ctx, tp = mesh.devices.shape
    fine = Mesh(mesh.devices.reshape(ctx, tp // 4, 2, 2), ("ctx",) + TP_AXES)
    return jax.shard_map(
        per_device,
        mesh=fine,
        in_specs=(
            P(TP_AXES, "ctx"),
            P(TP_AXES, "ctx"),
            P(TP_AXES, "ctx"),
            P(TP_AXES, "ctx"),
            P(TP_AXES),
            P(TP_AXES, None),
        ),
        out_specs=P(TP_AXES, "ctx"),
        check_vma=False,
    )
```

```python
import math

import jax
import jax.numpy as jnp
import numpy as np
from jax import lax
from jax.experimental import pallas as pl
from jax.experimental.pallas import tpu as pltpu
from jax.sharding import Mesh
from jax.sharding import PartitionSpec as P

TP_AXES = ("quad", "pair", "core")
GROUP = ("pair", "core")
MIB = 1 << 20


def targets_of(quad, pair, core, quads):
    onward = 2 * pair - 1
    far = lax.rem(quad + 2 * onward + quads, quads)
    near = lax.rem(quad + onward + quads, quads)
    chips = [(far, 1 - pair), (near, pair), (near, 1 - pair), (quad, pair)]
    return [(q * 2 + p) * 2 + core for q, p in chips]


def send_to_target(share, step, quads):
    pairs = []
    for quad in range(quads):
        for pair in range(2):
            onward = 1 if pair == 1 else -1
            q = (quad + (2 * onward if step == 0 else onward)) % quads
            p = pair if step == 1 else 1 - pair
            pairs += [((quad * 2 + pair) * 2 + c, (q * 2 + p) * 2 + c) for c in range(2)]
    return lax.ppermute(share, TP_AXES, pairs)


def arrange_kernel(group, quads, width, members, place_ref, weight_ref, *refs):
    count = len(members) * group
    out_refs, done_ref, blocks, in_sems, out_sems = refs[: len(members)], *refs[-4:]
    tp = place_ref[0]
    quad, place = tp // group, lax.rem(tp, group)
    loads, stores = [], []
    for n, r in enumerate(members):
        other = place ^ r
        for i, target in enumerate(targets_of(quad, other // 2, lax.rem(other, 2), quads)):
            k = n * group + i
            start = pl.multiple_of(target * width, width)
            loads.append(
                pltpu.make_async_copy(
                    weight_ref.at[:, pl.ds(start, width)], blocks.at[k], in_sems.at[k]
                )
            )
            stores.append(
                pltpu.make_async_copy(
                    blocks.at[k], out_refs[n].at[:, pl.ds(i * width, width)], out_sems.at[k]
                )
            )
    for load in loads:
        load.start()
    for k in range(count):
        loads[k].wait()
        stores[k].start()
    for store in stores:
        store.wait()
    done_ref[0] = tp


def arrange(out_weight, place, group, quads, width, members):
    rows = out_weight.shape[0]
    count = len(members) * group
    piece = jax.ShapeDtypeStruct((rows, group * width), out_weight.dtype)
    *pieces, done = pl.pallas_call(
        lambda *refs: arrange_kernel(group, quads, width, members, *refs),
        out_shape=[piece] * len(members) + [jax.ShapeDtypeStruct((1,), jnp.int32)],
        in_specs=[
            pl.BlockSpec(memory_space=pltpu.SMEM),
            pl.BlockSpec(memory_space=pltpu.HBM),
        ],
        out_specs=[pl.BlockSpec(memory_space=pltpu.HBM)] * len(members)
        + [pl.BlockSpec(memory_space=pltpu.SMEM)],
        scratch_shapes=[
            pltpu.VMEM((count, rows, width), out_weight.dtype),
            pltpu.SemaphoreType.DMA((count,)),
            pltpu.SemaphoreType.DMA((count,)),
        ],
        compiler_params=pltpu.CompilerParams(vmem_limit_bytes=60 * MIB),
        cost_estimate=pl.CostEstimate(
            flops=0, bytes_accessed=4 * rows * count * width, transcendentals=0
        ),
    )(place, out_weight)
    return pieces, done


def own_columns_kernel(group, quads, width, place_ref, weight_ref, out_ref, sems):
    tp = place_ref[0]
    quad, place = tp // group, lax.rem(tp, group)
    copies = []
    for i, target in enumerate(targets_of(quad, place // 2, lax.rem(place, 2), quads)):
        start = pl.multiple_of(target * width, width)
        copies.append(
            pltpu.make_async_copy(
                weight_ref.at[:, pl.ds(start, width)],
                out_ref.at[:, pl.ds(i * width, width)],
                sems.at[i],
            )
        )
    for copy in copies:
        copy.start()
    for copy in copies:
        copy.wait()


def own_columns(out_weight, place, group, quads, width):
    rows = out_weight.shape[0]
    return pl.pallas_call(
        lambda *refs: own_columns_kernel(group, quads, width, *refs),
        out_shape=jax.ShapeDtypeStruct((rows, group * width), out_weight.dtype),
        in_specs=[
            pl.BlockSpec(memory_space=pltpu.SMEM),
            pl.BlockSpec(memory_space=pltpu.HBM),
        ],
        out_specs=pl.BlockSpec(memory_space=pltpu.VMEM),
        scratch_shapes=[pltpu.SemaphoreType.DMA((group,))],
        compiler_params=pltpu.CompilerParams(vmem_limit_bytes=60 * MIB),
        cost_estimate=pl.CostEstimate(
            flops=0, bytes_accessed=4 * rows * group * width, transcendentals=0
        ),
    )(place, out_weight)


def project_kernel(group, place_ref, mixed_ref, own_hbm, *refs):
    out_refs, own_ref, sem = refs[group - 1 : -2], refs[-2], refs[-1]
    load = pltpu.make_async_copy(own_hbm, own_ref, sem)
    load.start()
    weight_refs = (own_ref,) + refs[: group - 1]
    tokens = mixed_ref.shape[0] // group
    width = out_refs[0].shape[1]
    place = lax.rem(place_ref[0], group)
    mixed = [
        mixed_ref[pl.ds(pl.multiple_of((place ^ r) * tokens, tokens), tokens), :]
        for r in range(group)
    ]

    def product(r, i):
        weights = weight_refs[r][:, i * width : (i + 1) * width]
        return jnp.dot(mixed[r], weights, preferred_element_type=jnp.float32)

    totals = [sum(product(r, i) for r in range(1, group)) for i in range(group)]
    load.wait()
    for i in range(group):
        out_refs[i][...] = (totals[i] + product(0, i)).astype(out_refs[i].dtype)


def project(place, mixed, weights, width):
    group = len(weights)
    share = jax.ShapeDtypeStruct((mixed.shape[0] // group, width), mixed.dtype)
    return pl.pallas_call(
        lambda *refs: project_kernel(group, *refs),
        out_shape=[share] * group,
        in_specs=[pl.BlockSpec(memory_space=pltpu.SMEM)]
        + [pl.BlockSpec(memory_space=pltpu.VMEM), pl.BlockSpec(memory_space=pltpu.HBM)]
        + [pl.BlockSpec(memory_space=pltpu.VMEM)] * (group - 1),
        out_specs=[pl.BlockSpec(memory_space=pltpu.VMEM)] * group,
        scratch_shapes=[
            pltpu.VMEM(weights[0].shape, weights[0].dtype),
            pltpu.SemaphoreType.DMA,
        ],
        compiler_params=pltpu.CompilerParams(vmem_limit_bytes=10 * MIB),
        cost_estimate=pl.CostEstimate(
            flops=2 * mixed.size * group * width,
            bytes_accessed=2 * (mixed.size + sum(w.size for w in weights) + group * share.size),
            transcendentals=0,
        ),
    )(place, mixed, pltpu.with_memory_space_constraint(weights[0], pltpu.HBM), *weights[1:])


def finish_kernel(*refs):
    total = refs[0][...].astype(jnp.float32)
    for ref in refs[1:-1]:
        total = total + ref[...].astype(jnp.float32)
    refs[-1][...] = total.astype(refs[-1].dtype).T


def finish(shares):
    tokens, width = shares[0].shape
    return pl.pallas_call(
        finish_kernel,
        out_shape=jax.ShapeDtypeStruct((width, tokens), shares[0].dtype),
        in_specs=[pl.BlockSpec(memory_space=pltpu.VMEM)] * len(shares),
        out_specs=pl.BlockSpec(memory_space=pltpu.VMEM),
        compiler_params=pltpu.CompilerParams(vmem_limit_bytes=6 * MIB),
    )(*shares)


def dft_tables(blocks, tokens, channels):
    period = 2 * blocks
    total = period * tokens
    low = blocks + 1
    k1 = np.arange(low)
    i = np.arange(blocks)[::-1]
    s = np.arange(tokens)
    first = 2 * np.pi * (np.outer(k1, i) % period) / period
    turn = 2 * np.pi * (np.outer(k1, s) % total) / total
    square = 2 * np.pi * (np.outer(s, s) % tokens) / tokens
    front = np.concatenate([np.cos(first), -np.sin(first)])
    weight = np.where((k1 == 0) | (k1 == blocks), 1.0, 2.0)[:, None] / total
    back = np.concatenate(
        [
            np.kron((weight * np.cos(first)).T, np.eye(channels)),
            np.kron(-(weight * np.sin(first)).T, np.eye(channels)),
        ],
        axis=1,
    )
    matrices = [jnp.asarray(m, jnp.bfloat16) for m in (front, np.cos(square), np.sin(square), back)]
    turns = [jnp.asarray(m, jnp.float32) for m in (np.cos(turn), np.sin(turn))]
    return matrices + turns


def matmul(left, right):
    return jnp.dot(left, right, preferred_element_type=jnp.float32)


def convolve_kernel(
    channels, in_ref, front_ref, square_cos_ref, square_sin_ref, back_ref, cos_ref, sin_ref, after_ref, out_ref, rows_ref
):
    del after_ref
    low, tokens = cos_ref.shape
    both = 2 * channels
    blocks = front_ref.shape[1]
    width = blocks * both
    repeat = lax.broadcasted_iota(jnp.int32, (blocks, width), 1) // both
    repeat = (repeat == lax.broadcasted_iota(jnp.int32, (blocks, width), 0)).astype(jnp.bfloat16)
    agree = lax.broadcasted_iota(jnp.int32, (both, width), 1) % both
    agree = (agree == lax.broadcasted_iota(jnp.int32, (both, width), 0))[None]
    entries = matmul(front_ref[...], repeat)
    turn_cos = cos_ref[...].reshape(low, 1, tokens)
    turn_sin = sin_ref[...].reshape(low, 1, tokens)

    def spread(part):
        part = jnp.where(agree, part.reshape(low, 1, width), 0.0)
        part = part.reshape(low * both, width).astype(jnp.bfloat16)
        return matmul(part, in_ref[...]).reshape(low, both, tokens)

    def flat(array):
        return array.reshape(-1, tokens).astype(jnp.bfloat16)

    real, imag = spread(entries[:low]), spread(entries[low:])
    turned_real = flat(real * turn_cos + imag * turn_sin)
    turned_imag = flat(imag * turn_cos - real * turn_sin)
    square_cos, square_sin = square_cos_ref[...], square_sin_ref[...]
    real = matmul(turned_real, square_cos) + matmul(turned_imag, square_sin)
    imag = matmul(turned_imag, square_cos) - matmul(turned_real, square_sin)
    real, imag = real.reshape(low, both, tokens), imag.reshape(low, both, tokens)
    sig_real, tap_real = real[:, :channels], real[:, channels:]
    sig_imag, tap_imag = imag[:, :channels], imag[:, channels:]
    prod_real = flat(sig_real * tap_real - sig_imag * tap_imag)
    prod_imag = flat(sig_real * tap_imag + sig_imag * tap_real)
    real = matmul(prod_real, square_cos) - matmul(prod_imag, square_sin)
    imag = matmul(prod_imag, square_cos) + matmul(prod_real, square_sin)
    real, imag = real.reshape(low, channels, tokens), imag.reshape(low, channels, tokens)
    half = low * channels
    rows_ref[:half, :] = (real * turn_cos - imag * turn_sin).reshape(half, tokens)
    rows_ref[half:, :] = (real * turn_sin + imag * turn_cos).reshape(half, tokens)
    out_ref[...] = matmul(back_ref[...], rows_ref[...].astype(jnp.bfloat16)).astype(out_ref.dtype)


def convolve(blocks_in, channels, tables, after):
    blocks, both, tokens = blocks_in.shape
    out = pl.pallas_call(
        lambda *refs: convolve_kernel(channels, *refs),
        out_shape=jax.ShapeDtypeStruct((blocks * channels, tokens), jnp.bfloat16),
        in_specs=[pl.BlockSpec(memory_space=pltpu.VMEM)] * (1 + len(tables))
        + [pl.BlockSpec(memory_space=pltpu.SMEM)],
        out_specs=pl.BlockSpec(memory_space=pltpu.VMEM),
        scratch_shapes=[pltpu.VMEM((2 * tables[-1].shape[0] * channels, tokens), jnp.float32)],
        compiler_params=pltpu.CompilerParams(vmem_limit_bytes=32 * MIB),
        cost_estimate=pl.CostEstimate(
            flops=800_000_000, bytes_accessed=3_000_000, transcendentals=0
        ),
    )(blocks_in.reshape(blocks * both, tokens), *tables, after)
    return out.reshape(blocks, channels, tokens)


def outgoing_kernel(devices, signal_hbm, gate_hbm, taps_hbm, out_ref, signal_ref, gate_ref, taps_ref, sems):
    copies = [
        pltpu.make_async_copy(source, target, sems.at[n])
        for n, (source, target) in enumerate(
            [(signal_hbm, signal_ref), (gate_hbm, gate_ref), (taps_hbm, taps_ref)]
        )
    ]
    for copy in copies:
        copy.start()
    for copy in copies:
        copy.wait()
    rows, tokens = signal_ref.shape
    gated = signal_ref[...].astype(jnp.float32) * gate_ref[...].astype(jnp.float32)
    both = jnp.concatenate(
        [
            gated.reshape(devices, rows // devices, tokens),
            taps_ref[...].reshape(devices, rows // devices, tokens),
        ],
        axis=1,
    )
    out_ref[...] = both.reshape(2 * rows, tokens).astype(out_ref.dtype)


def outgoing(signal, pre_gate, filter_taps, devices):
    rows, tokens = signal.shape
    out = pl.pallas_call(
        lambda *refs: outgoing_kernel(devices, *refs),
        out_shape=jax.ShapeDtypeStruct((2 * rows, tokens), jnp.bfloat16),
        in_specs=[pl.BlockSpec(memory_space=pltpu.HBM)] * 3,
        out_specs=pl.BlockSpec(memory_space=pltpu.VMEM),
        scratch_shapes=[
            pltpu.VMEM(signal.shape, signal.dtype),
            pltpu.VMEM(pre_gate.shape, pre_gate.dtype),
            pltpu.VMEM(filter_taps.shape, filter_taps.dtype),
            pltpu.SemaphoreType.DMA((3,)),
        ],
        compiler_params=pltpu.CompilerParams(vmem_limit_bytes=60 * MIB),
    )(signal, pre_gate, filter_taps)
    return out.reshape(devices, 2 * rows // devices, tokens)


def gate_kernel(post_ref, signal_ref, pre_ref, convolved_ref, gain_ref, after_ref, out_ref):
    del after_ref
    gated = signal_ref[...].astype(jnp.float32) * pre_ref[...].astype(jnp.float32)
    inner = convolved_ref[...].astype(jnp.float32) + gain_ref[...] * gated
    out_ref[...] = (post_ref[...].astype(jnp.float32) * inner).astype(out_ref.dtype).T


def gate(post_gate, signal, pre_gate, convolved, skip_gain, after):
    corners = jnp.concatenate([array[:16, :128] for array in after])
    return pl.pallas_call(
        gate_kernel,
        out_shape=jax.ShapeDtypeStruct(post_gate.shape[::-1], post_gate.dtype),
        in_specs=[pl.BlockSpec(memory_space=pltpu.VMEM)] * 6,
        out_specs=pl.BlockSpec(memory_space=pltpu.VMEM),
        compiler_params=pltpu.CompilerParams(vmem_limit_bytes=6 * MIB),
        cost_estimate=pl.CostEstimate(
            flops=5 * post_gate.size, bytes_accessed=10 * post_gate.size, transcendentals=0
        ),
    )(post_gate, signal, pre_gate, convolved, skip_gain[:, None], corners)


def exchange(parts, devices):
    backwards = [list(range(devices))[::-1]]
    return lax.all_to_all(
        parts, "ctx", split_axis=0, concat_axis=0, axis_index_groups=backwards, tiled=True
    )


def per_device(signal, pre_gate, post_gate, filter_taps, skip_gain, out_weight):
    channels_here, tokens_here = signal.shape
    devices = lax.axis_size("ctx")
    channels = channels_here // devices
    quads = lax.axis_size("quad")
    group = lax.axis_size("pair") * lax.axis_size("core")
    features = out_weight.shape[1]
    width = features // (quads * group)

    send = outgoing(signal, pre_gate, filter_taps, devices)
    blocks = exchange(send, devices)

    place = lax.axis_index(TP_AXES).astype(jnp.int32).reshape(1)
    members = [2, 3, 1]
    pieces, arranged = arrange(out_weight, place, group, quads, width, members)
    pieces = {
        r: lax.ppermute(piece, GROUP, [(t, t ^ r) for t in range(group)])
        for r, piece in zip(members, pieces)
    }
    pieces = [pieces[r] for r in range(1, group)]
    own = own_columns(out_weight, place, group, quads, width)
    tables = dft_tables(devices, tokens_here, channels)
    convolved = convolve(blocks, channels, tables, arranged)
    convolved = exchange(convolved, devices).reshape(channels_here, tokens_here)
    mixed = gate(post_gate, signal, pre_gate, convolved, skip_gain, pieces)
    gathered = lax.all_gather(mixed, GROUP, axis=0, tiled=True)
    shares = project(place, gathered, [own] + pieces, width)
    return finish([send_to_target(shares[step], step, quads) for step in range(3)] + [shares[3]])


def solution(mesh):
    ctx, tp = mesh.devices.shape
    fine = Mesh(mesh.devices.reshape(ctx, tp // 4, 2, 2), ("ctx",) + TP_AXES)
    return jax.shard_map(
        per_device,
        mesh=fine,
        in_specs=(
            P(TP_AXES, "ctx"),
            P(TP_AXES, "ctx"),
            P(TP_AXES, "ctx"),
            P(TP_AXES, "ctx"),
            P(TP_AXES),
            P(TP_AXES, None),
        ),
        out_specs=P(TP_AXES, "ctx"),
        check_vma=False,
    )
```

```python
import math

import jax
import jax.numpy as jnp
import numpy as np
from jax import lax
from jax.experimental import pallas as pl
from jax.experimental.pallas import tpu as pltpu
from jax.sharding import Mesh
from jax.sharding import PartitionSpec as P

TP_AXES = ("quad", "pair", "core")
GROUP = ("pair", "core")
MIB = 1 << 20


def targets_of(quad, pair, core, quads):
    onward = 2 * pair - 1
    far = lax.rem(quad + 2 * onward + quads, quads)
    near = lax.rem(quad + onward + quads, quads)
    chips = [(far, 1 - pair), (near, pair), (near, 1 - pair), (quad, pair)]
    return [(q * 2 + p) * 2 + core for q, p in chips]


def send_to_target(share, step, quads):
    pairs = []
    for quad in range(quads):
        for pair in range(2):
            onward = 1 if pair == 1 else -1
            q = (quad + (2 * onward if step == 0 else onward)) % quads
            p = pair if step == 1 else 1 - pair
            pairs += [((quad * 2 + pair) * 2 + c, (q * 2 + p) * 2 + c) for c in range(2)]
    return lax.ppermute(share, TP_AXES, pairs)


def arrange_kernel(group, quads, width, members, place_ref, weight_ref, *refs):
    count = len(members) * group
    out_refs, done_ref, blocks, in_sems, out_sems = refs[: len(members)], *refs[-4:]
    tp = place_ref[0]
    quad, place = tp // group, lax.rem(tp, group)
    loads, stores = [], []
    for n, r in enumerate(members):
        other = place ^ r
        for i, target in enumerate(targets_of(quad, other // 2, lax.rem(other, 2), quads)):
            k = n * group + i
            start = pl.multiple_of(target * width, width)
            loads.append(
                pltpu.make_async_copy(
                    weight_ref.at[:, pl.ds(start, width)], blocks.at[k], in_sems.at[k]
                )
            )
            stores.append(
                pltpu.make_async_copy(
                    blocks.at[k], out_refs[n].at[:, pl.ds(i * width, width)], out_sems.at[k]
                )
            )
    for load in loads:
        load.start()
    for k in range(count):
        loads[k].wait()
        stores[k].start()
    for store in stores:
        store.wait()
    done_ref[0] = tp


def arrange(out_weight, place, group, quads, width, members):
    rows = out_weight.shape[0]
    count = len(members) * group
    piece = jax.ShapeDtypeStruct((rows, group * width), out_weight.dtype)
    *pieces, done = pl.pallas_call(
        lambda *refs: arrange_kernel(group, quads, width, members, *refs),
        out_shape=[piece] * len(members) + [jax.ShapeDtypeStruct((1,), jnp.int32)],
        in_specs=[
            pl.BlockSpec(memory_space=pltpu.SMEM),
            pl.BlockSpec(memory_space=pltpu.HBM),
        ],
        out_specs=[pl.BlockSpec(memory_space=pltpu.HBM)] * len(members)
        + [pl.BlockSpec(memory_space=pltpu.SMEM)],
        scratch_shapes=[
            pltpu.VMEM((count, rows, width), out_weight.dtype),
            pltpu.SemaphoreType.DMA((count,)),
            pltpu.SemaphoreType.DMA((count,)),
        ],
        compiler_params=pltpu.CompilerParams(vmem_limit_bytes=60 * MIB),
        cost_estimate=pl.CostEstimate(
            flops=0, bytes_accessed=4 * rows * count * width, transcendentals=0
        ),
    )(place, out_weight)
    return pieces, done


def own_columns_kernel(group, quads, width, place_ref, weight_ref, out_ref, sems):
    tp = place_ref[0]
    quad, place = tp // group, lax.rem(tp, group)
    copies = []
    for i, target in enumerate(targets_of(quad, place // 2, lax.rem(place, 2), quads)):
        start = pl.multiple_of(target * width, width)
        copies.append(
            pltpu.make_async_copy(
                weight_ref.at[:, pl.ds(start, width)],
                out_ref.at[:, pl.ds(i * width, width)],
                sems.at[i],
            )
        )
    for copy in copies:
        copy.start()
    for copy in copies:
        copy.wait()


def own_columns(out_weight, place, group, quads, width):
    rows = out_weight.shape[0]
    return pl.pallas_call(
        lambda *refs: own_columns_kernel(group, quads, width, *refs),
        out_shape=jax.ShapeDtypeStruct((rows, group * width), out_weight.dtype),
        in_specs=[
            pl.BlockSpec(memory_space=pltpu.SMEM),
            pl.BlockSpec(memory_space=pltpu.HBM),
        ],
        out_specs=pl.BlockSpec(memory_space=pltpu.VMEM),
        scratch_shapes=[pltpu.SemaphoreType.DMA((group,))],
        compiler_params=pltpu.CompilerParams(vmem_limit_bytes=60 * MIB),
        cost_estimate=pl.CostEstimate(
            flops=0, bytes_accessed=4 * rows * group * width, transcendentals=0
        ),
    )(place, out_weight)


def project_kernel(group, place_ref, mixed_ref, own_hbm, *refs):
    out_refs, own_ref, sem = refs[group - 1 : -2], refs[-2], refs[-1]
    load = pltpu.make_async_copy(own_hbm, own_ref, sem)
    load.start()
    weight_refs = (own_ref,) + refs[: group - 1]
    tokens = mixed_ref.shape[0] // group
    width = out_refs[0].shape[1]
    place = lax.rem(place_ref[0], group)
    mixed = [
        mixed_ref[pl.ds(pl.multiple_of((place ^ r) * tokens, tokens), tokens), :]
        for r in range(group)
    ]

    def product(r, i):
        weights = weight_refs[r][:, i * width : (i + 1) * width]
        return jnp.dot(mixed[r], weights, preferred_element_type=jnp.float32)

    totals = [sum(product(r, i) for r in range(1, group)) for i in range(group)]
    load.wait()
    for i in range(group):
        out_refs[i][...] = (totals[i] + product(0, i)).astype(out_refs[i].dtype)


def project(place, mixed, weights, width):
    group = len(weights)
    share = jax.ShapeDtypeStruct((mixed.shape[0] // group, width), mixed.dtype)
    return pl.pallas_call(
        lambda *refs: project_kernel(group, *refs),
        out_shape=[share] * group,
        in_specs=[pl.BlockSpec(memory_space=pltpu.SMEM)]
        + [pl.BlockSpec(memory_space=pltpu.VMEM), pl.BlockSpec(memory_space=pltpu.HBM)]
        + [pl.BlockSpec(memory_space=pltpu.VMEM)] * (group - 1),
        out_specs=[pl.BlockSpec(memory_space=pltpu.VMEM)] * group,
        scratch_shapes=[
            pltpu.VMEM(weights[0].shape, weights[0].dtype),
            pltpu.SemaphoreType.DMA,
        ],
        compiler_params=pltpu.CompilerParams(vmem_limit_bytes=10 * MIB),
        cost_estimate=pl.CostEstimate(
            flops=2 * mixed.size * group * width,
            bytes_accessed=2 * (mixed.size + sum(w.size for w in weights) + group * share.size),
            transcendentals=0,
        ),
    )(place, mixed, pltpu.with_memory_space_constraint(weights[0], pltpu.HBM), *weights[1:])


def finish_kernel(*refs):
    total = refs[0][...].astype(jnp.float32)
    for ref in refs[1:-1]:
        total = total + ref[...].astype(jnp.float32)
    refs[-1][...] = total.astype(refs[-1].dtype).T


def finish(shares):
    tokens, width = shares[0].shape
    return pl.pallas_call(
        finish_kernel,
        out_shape=jax.ShapeDtypeStruct((width, tokens), shares[0].dtype),
        in_specs=[pl.BlockSpec(memory_space=pltpu.VMEM)] * len(shares),
        out_specs=pl.BlockSpec(memory_space=pltpu.VMEM),
        compiler_params=pltpu.CompilerParams(vmem_limit_bytes=6 * MIB),
    )(*shares)


def dft_tables(blocks, tokens, channels):
    period = 2 * blocks
    total = period * tokens
    low = blocks + 1
    k1 = np.arange(low)
    i = np.arange(blocks)[::-1]
    s = np.arange(tokens)
    first = 2 * np.pi * (np.outer(k1, i) % period) / period
    turn = 2 * np.pi * (np.outer(k1, s) % total) / total
    square = 2 * np.pi * (np.outer(s, s) % tokens) / tokens
    front = np.concatenate([np.cos(first), -np.sin(first)])
    weight = np.where((k1 == 0) | (k1 == blocks), 1.0, 2.0)[:, None] / total
    back = np.concatenate(
        [
            np.kron((weight * np.cos(first)).T, np.eye(channels)),
            np.kron(-(weight * np.sin(first)).T, np.eye(channels)),
        ],
        axis=1,
    )
    matrices = [jnp.asarray(m, jnp.bfloat16) for m in (front, np.cos(square), np.sin(square), back)]
    turns = [jnp.asarray(m, jnp.float32) for m in (np.cos(turn), np.sin(turn))]
    return matrices + turns


def matmul(left, right):
    return jnp.dot(left, right, preferred_element_type=jnp.float32)


def convolve_kernel(
    channels, in_ref, front_ref, square_cos_ref, square_sin_ref, back_ref, cos_ref, sin_ref, after_ref, out_ref, rows_ref
):
    del after_ref
    low, tokens = cos_ref.shape
    both = 2 * channels
    blocks = front_ref.shape[1]
    width = blocks * both
    repeat = lax.broadcasted_iota(jnp.int32, (blocks, width), 1) // both
    repeat = (repeat == lax.broadcasted_iota(jnp.int32, (blocks, width), 0)).astype(jnp.bfloat16)
    agree = lax.broadcasted_iota(jnp.int32, (both, width), 1) % both
    agree = (agree == lax.broadcasted_iota(jnp.int32, (both, width), 0))[None]
    entries = matmul(front_ref[...], repeat)
    turn_cos = cos_ref[...].reshape(low, 1, tokens)
    turn_sin = sin_ref[...].reshape(low, 1, tokens)

    def spread(part):
        part = jnp.where(agree, part.reshape(low, 1, width), 0.0)
        part = part.reshape(low * both, width).astype(jnp.bfloat16)
        return matmul(part, in_ref[...]).reshape(low, both, tokens)

    def flat(array):
        return array.reshape(-1, tokens).astype(jnp.bfloat16)

    real, imag = spread(entries[:low]), spread(entries[low:])
    turned_real = flat(real * turn_cos + imag * turn_sin)
    turned_imag = flat(imag * turn_cos - real * turn_sin)
    square_cos, square_sin = square_cos_ref[...], square_sin_ref[...]
    real = matmul(turned_real, square_cos) + matmul(turned_imag, square_sin)
    imag = matmul(turned_imag, square_cos) - matmul(turned_real, square_sin)
    real, imag = real.reshape(low, both, tokens), imag.reshape(low, both, tokens)
    sig_real, tap_real = real[:, :channels], real[:, channels:]
    sig_imag, tap_imag = imag[:, :channels], imag[:, channels:]
    prod_real = flat(sig_real * tap_real - sig_imag * tap_imag)
    prod_imag = flat(sig_real * tap_imag + sig_imag * tap_real)
    real = matmul(prod_real, square_cos) - matmul(prod_imag, square_sin)
    imag = matmul(prod_imag, square_cos) + matmul(prod_real, square_sin)
    real, imag = real.reshape(low, channels, tokens), imag.reshape(low, channels, tokens)
    half = low * channels
    rows_ref[:half, :] = (real * turn_cos - imag * turn_sin).reshape(half, tokens)
    rows_ref[half:, :] = (real * turn_sin + imag * turn_cos).reshape(half, tokens)
    out_ref[...] = matmul(back_ref[...], rows_ref[...].astype(jnp.bfloat16)).astype(out_ref.dtype)


def convolve(blocks_in, channels, tables, after):
    blocks, both, tokens = blocks_in.shape
    out = pl.pallas_call(
        lambda *refs: convolve_kernel(channels, *refs),
        out_shape=jax.ShapeDtypeStruct((blocks * channels, tokens), jnp.bfloat16),
        in_specs=[pl.BlockSpec(memory_space=pltpu.VMEM)] * (1 + len(tables))
        + [pl.BlockSpec(memory_space=pltpu.SMEM)],
        out_specs=pl.BlockSpec(memory_space=pltpu.VMEM),
        scratch_shapes=[pltpu.VMEM((2 * tables[-1].shape[0] * channels, tokens), jnp.float32)],
        compiler_params=pltpu.CompilerParams(vmem_limit_bytes=32 * MIB),
        cost_estimate=pl.CostEstimate(
            flops=800_000_000, bytes_accessed=3_000_000, transcendentals=0
        ),
    )(blocks_in.reshape(blocks * both, tokens), *tables, after)
    return out.reshape(blocks, channels, tokens)


def outgoing_kernel(devices, signal_hbm, gate_hbm, taps_hbm, out_ref, signal_ref, gate_ref, taps_ref, sems):
    copies = [
        pltpu.make_async_copy(source, target, sems.at[n])
        for n, (source, target) in enumerate(
            [(signal_hbm, signal_ref), (gate_hbm, gate_ref), (taps_hbm, taps_ref)]
        )
    ]
    for copy in copies:
        copy.start()
    for copy in copies:
        copy.wait()
    rows, tokens = signal_ref.shape
    gated = signal_ref[...].astype(jnp.float32) * gate_ref[...].astype(jnp.float32)
    both = jnp.concatenate(
        [
            gated.reshape(devices, rows // devices, tokens),
            taps_ref[...].reshape(devices, rows // devices, tokens),
        ],
        axis=1,
    )
    out_ref[...] = both.reshape(2 * rows, tokens).astype(out_ref.dtype)


def outgoing(signal, pre_gate, filter_taps, devices):
    rows, tokens = signal.shape
    out = pl.pallas_call(
        lambda *refs: outgoing_kernel(devices, *refs),
        out_shape=jax.ShapeDtypeStruct((2 * rows, tokens), jnp.bfloat16),
        in_specs=[pl.BlockSpec(memory_space=pltpu.HBM)] * 3,
        out_specs=pl.BlockSpec(memory_space=pltpu.VMEM),
        scratch_shapes=[
            pltpu.VMEM(signal.shape, signal.dtype),
            pltpu.VMEM(pre_gate.shape, pre_gate.dtype),
            pltpu.VMEM(filter_taps.shape, filter_taps.dtype),
            pltpu.SemaphoreType.DMA((3,)),
        ],
        compiler_params=pltpu.CompilerParams(vmem_limit_bytes=60 * MIB),
    )(signal, pre_gate, filter_taps)
    return out.reshape(devices, 2 * rows // devices, tokens)


def gate_kernel(post_ref, signal_ref, pre_ref, convolved_ref, gain_ref, after_ref, out_ref):
    del after_ref
    gated = signal_ref[...].astype(jnp.float32) * pre_ref[...].astype(jnp.float32)
    inner = convolved_ref[...].astype(jnp.float32) + gain_ref[...] * gated
    out_ref[...] = (post_ref[...].astype(jnp.float32) * inner).astype(out_ref.dtype).T


def gate(post_gate, signal, pre_gate, convolved, skip_gain, after):
    corners = jnp.concatenate([array[:16, :128] for array in after])
    return pl.pallas_call(
        gate_kernel,
        out_shape=jax.ShapeDtypeStruct(post_gate.shape[::-1], post_gate.dtype),
        in_specs=[pl.BlockSpec(memory_space=pltpu.VMEM)] * 6,
        out_specs=pl.BlockSpec(memory_space=pltpu.VMEM),
        compiler_params=pltpu.CompilerParams(vmem_limit_bytes=6 * MIB),
        cost_estimate=pl.CostEstimate(
            flops=5 * post_gate.size, bytes_accessed=10 * post_gate.size, transcendentals=0
        ),
    )(post_gate, signal, pre_gate, convolved, skip_gain[:, None], corners)


def exchange(parts, devices):
    backwards = [list(range(devices))[::-1]]
    return lax.all_to_all(
        parts, "ctx", split_axis=0, concat_axis=0, axis_index_groups=backwards, tiled=True
    )


def per_device(signal, pre_gate, post_gate, filter_taps, skip_gain, out_weight):
    channels_here, tokens_here = signal.shape
    devices = lax.axis_size("ctx")
    channels = channels_here // devices
    quads = lax.axis_size("quad")
    group = lax.axis_size("pair") * lax.axis_size("core")
    features = out_weight.shape[1]
    width = features // (quads * group)

    send = outgoing(signal, pre_gate, filter_taps, devices)
    blocks = exchange(send, devices)

    place = lax.axis_index(TP_AXES).astype(jnp.int32).reshape(1)
    members = [2, 3, 1]
    pieces, arranged = arrange(out_weight, place, group, quads, width, members)
    pieces = {
        r: lax.ppermute(piece, GROUP, [(t, t ^ r) for t in range(group)])
        for r, piece in zip(members, pieces)
    }
    pieces = [pieces[r] for r in range(1, group)]
    own = own_columns(out_weight, place, group, quads, width)
    tables = dft_tables(devices, tokens_here, channels)
    convolved = convolve(blocks, channels, tables, arranged)
    convolved = exchange(convolved, devices).reshape(channels_here, tokens_here)
    mixed = gate(post_gate, signal, pre_gate, convolved, skip_gain, pieces[1:] + pieces[:1])
    gathered = lax.all_gather(mixed, GROUP, axis=0, tiled=True)
    shares = project(place, gathered, [own] + pieces, width)
    return finish([send_to_target(shares[step], step, quads) for step in range(3)] + [shares[3]])


def solution(mesh):
    ctx, tp = mesh.devices.shape
    fine = Mesh(mesh.devices.reshape(ctx, tp // 4, 2, 2), ("ctx",) + TP_AXES)
    return jax.shard_map(
        per_device,
        mesh=fine,
        in_specs=(
            P(TP_AXES, "ctx"),
            P(TP_AXES, "ctx"),
            P(TP_AXES, "ctx"),
            P(TP_AXES, "ctx"),
            P(TP_AXES),
            P(TP_AXES, None),
        ),
        out_specs=P(TP_AXES, "ctx"),
        check_vma=False,
    )
```

```python
import math

import jax
import jax.numpy as jnp
import numpy as np
from jax import lax
from jax.experimental import pallas as pl
from jax.experimental.pallas import tpu as pltpu
from jax.sharding import Mesh
from jax.sharding import PartitionSpec as P

TP_AXES = ("quad", "pair", "core")
GROUP = ("pair", "core")
MIB = 1 << 20


def targets_of(quad, pair, core, quads):
    onward = 2 * pair - 1
    far = lax.rem(quad + 2 * onward + quads, quads)
    near = lax.rem(quad + onward + quads, quads)
    chips = [(far, 1 - pair), (near, pair), (near, 1 - pair), (quad, pair)]
    return [(q * 2 + p) * 2 + core for q, p in chips]


def send_to_target(share, step, quads):
    pairs = []
    for quad in range(quads):
        for pair in range(2):
            onward = 1 if pair == 1 else -1
            q = (quad + (2 * onward if step == 0 else onward)) % quads
            p = pair if step == 1 else 1 - pair
            pairs += [((quad * 2 + pair) * 2 + c, (q * 2 + p) * 2 + c) for c in range(2)]
    return lax.ppermute(share, TP_AXES, pairs)


def arrange_kernel(group, quads, width, members, place_ref, weight_ref, *refs):
    count = len(members) * group
    out_refs, done_ref, blocks, in_sems, out_sems = refs[: len(members)], *refs[-4:]
    tp = place_ref[0]
    quad, place = tp // group, lax.rem(tp, group)
    loads, stores = [], []
    for n, r in enumerate(members):
        other = place ^ r
        for i, target in enumerate(targets_of(quad, other // 2, lax.rem(other, 2), quads)):
            k = n * group + i
            start = pl.multiple_of(target * width, width)
            loads.append(
                pltpu.make_async_copy(
                    weight_ref.at[:, pl.ds(start, width)], blocks.at[k], in_sems.at[k]
                )
            )
            stores.append(
                pltpu.make_async_copy(
                    blocks.at[k], out_refs[n].at[:, pl.ds(i * width, width)], out_sems.at[k]
                )
            )
    for load in loads:
        load.start()
    for k in range(count):
        loads[k].wait()
        stores[k].start()
    for store in stores:
        store.wait()
    done_ref[0] = tp


def arrange(out_weight, place, group, quads, width, members):
    rows = out_weight.shape[0]
    count = len(members) * group
    piece = jax.ShapeDtypeStruct((rows, group * width), out_weight.dtype)
    *pieces, done = pl.pallas_call(
        lambda *refs: arrange_kernel(group, quads, width, members, *refs),
        out_shape=[piece] * len(members) + [jax.ShapeDtypeStruct((1,), jnp.int32)],
        in_specs=[
            pl.BlockSpec(memory_space=pltpu.SMEM),
            pl.BlockSpec(memory_space=pltpu.HBM),
        ],
        out_specs=[pl.BlockSpec(memory_space=pltpu.HBM)] * len(members)
        + [pl.BlockSpec(memory_space=pltpu.SMEM)],
        scratch_shapes=[
            pltpu.VMEM((count, rows, width), out_weight.dtype),
            pltpu.SemaphoreType.DMA((count,)),
            pltpu.SemaphoreType.DMA((count,)),
        ],
        compiler_params=pltpu.CompilerParams(vmem_limit_bytes=60 * MIB),
        cost_estimate=pl.CostEstimate(
            flops=0, bytes_accessed=4 * rows * count * width, transcendentals=0
        ),
    )(place, out_weight)
    return pieces, done


def own_columns_kernel(group, quads, width, place_ref, weight_ref, out_ref, sems):
    tp = place_ref[0]
    quad, place = tp // group, lax.rem(tp, group)
    copies = []
    for i, target in enumerate(targets_of(quad, place // 2, lax.rem(place, 2), quads)):
        start = pl.multiple_of(target * width, width)
        copies.append(
            pltpu.make_async_copy(
                weight_ref.at[:, pl.ds(start, width)],
                out_ref.at[:, pl.ds(i * width, width)],
                sems.at[i],
            )
        )
    for copy in copies:
        copy.start()
    for copy in copies:
        copy.wait()


def own_columns(out_weight, place, group, quads, width):
    rows = out_weight.shape[0]
    return pl.pallas_call(
        lambda *refs: own_columns_kernel(group, quads, width, *refs),
        out_shape=jax.ShapeDtypeStruct((rows, group * width), out_weight.dtype),
        in_specs=[
            pl.BlockSpec(memory_space=pltpu.SMEM),
            pl.BlockSpec(memory_space=pltpu.HBM),
        ],
        out_specs=pl.BlockSpec(memory_space=pltpu.VMEM),
        scratch_shapes=[pltpu.SemaphoreType.DMA((group,))],
        compiler_params=pltpu.CompilerParams(vmem_limit_bytes=60 * MIB),
        cost_estimate=pl.CostEstimate(
            flops=0, bytes_accessed=4 * rows * group * width, transcendentals=0
        ),
    )(place, out_weight)


def project_kernel(group, place_ref, mixed_ref, own_hbm, *refs):
    out_refs, own_ref, sem = refs[group - 1 : -2], refs[-2], refs[-1]
    load = pltpu.make_async_copy(own_hbm, own_ref, sem)
    load.start()
    weight_refs = (own_ref,) + refs[: group - 1]
    tokens = mixed_ref.shape[0] // group
    width = out_refs[0].shape[1]
    place = lax.rem(place_ref[0], group)
    mixed = [
        mixed_ref[pl.ds(pl.multiple_of((place ^ r) * tokens, tokens), tokens), :]
        for r in range(group)
    ]

    def product(r, i):
        weights = weight_refs[r][:, i * width : (i + 1) * width]
        return jnp.dot(mixed[r], weights, preferred_element_type=jnp.float32)

    totals = [sum(product(r, i) for r in range(1, group)) for i in range(group)]
    load.wait()
    for i in range(group):
        out_refs[i][...] = (totals[i] + product(0, i)).astype(out_refs[i].dtype)


def project(place, mixed, weights, width):
    group = len(weights)
    share = jax.ShapeDtypeStruct((mixed.shape[0] // group, width), mixed.dtype)
    return pl.pallas_call(
        lambda *refs: project_kernel(group, *refs),
        out_shape=[share] * group,
        in_specs=[pl.BlockSpec(memory_space=pltpu.SMEM)]
        + [pl.BlockSpec(memory_space=pltpu.VMEM), pl.BlockSpec(memory_space=pltpu.HBM)]
        + [pl.BlockSpec(memory_space=pltpu.VMEM)] * (group - 1),
        out_specs=[pl.BlockSpec(memory_space=pltpu.VMEM)] * group,
        scratch_shapes=[
            pltpu.VMEM(weights[0].shape, weights[0].dtype),
            pltpu.SemaphoreType.DMA,
        ],
        compiler_params=pltpu.CompilerParams(vmem_limit_bytes=10 * MIB),
        cost_estimate=pl.CostEstimate(
            flops=2 * mixed.size * group * width,
            bytes_accessed=2 * (mixed.size + sum(w.size for w in weights) + group * share.size),
            transcendentals=0,
        ),
    )(place, mixed, pltpu.with_memory_space_constraint(weights[0], pltpu.HBM), *weights[1:])


def finish_kernel(*refs):
    total = refs[0][...].astype(jnp.float32)
    for ref in refs[1:-1]:
        total = total + ref[...].astype(jnp.float32)
    refs[-1][...] = total.astype(refs[-1].dtype).T


def finish(shares):
    tokens, width = shares[0].shape
    return pl.pallas_call(
        finish_kernel,
        out_shape=jax.ShapeDtypeStruct((width, tokens), shares[0].dtype),
        in_specs=[pl.BlockSpec(memory_space=pltpu.VMEM)] * len(shares),
        out_specs=pl.BlockSpec(memory_space=pltpu.VMEM),
        compiler_params=pltpu.CompilerParams(vmem_limit_bytes=6 * MIB),
    )(*shares)


def exchange_order(devices):
    return [(2 * devices // 3 - n) % devices for n in range(devices)]


def dft_tables(blocks, tokens, channels):
    period = 2 * blocks
    total = period * tokens
    low = blocks + 1
    k1 = np.arange(low)
    i = np.array(exchange_order(blocks))
    s = np.arange(tokens)
    first = 2 * np.pi * (np.outer(k1, i) % period) / period
    turn = 2 * np.pi * (np.outer(k1, s) % total) / total
    square = 2 * np.pi * (np.outer(s, s) % tokens) / tokens
    front = np.concatenate([np.cos(first), -np.sin(first)])
    weight = np.where((k1 == 0) | (k1 == blocks), 1.0, 2.0)[:, None] / total
    back = np.concatenate(
        [
            np.kron((weight * np.cos(first)).T, np.eye(channels)),
            np.kron(-(weight * np.sin(first)).T, np.eye(channels)),
        ],
        axis=1,
    )
    matrices = [jnp.asarray(m, jnp.bfloat16) for m in (front, np.cos(square), np.sin(square), back)]
    turns = [jnp.asarray(m, jnp.float32) for m in (np.cos(turn), np.sin(turn))]
    return matrices + turns


def matmul(left, right):
    return jnp.dot(left, right, preferred_element_type=jnp.float32)


def convolve_kernel(
    channels, in_ref, front_ref, square_cos_ref, square_sin_ref, back_ref, cos_ref, sin_ref, after_ref, out_ref, rows_ref
):
    del after_ref
    low, tokens = cos_ref.shape
    both = 2 * channels
    blocks = front_ref.shape[1]
    width = blocks * both
    repeat = lax.broadcasted_iota(jnp.int32, (blocks, width), 1) // both
    repeat = (repeat == lax.broadcasted_iota(jnp.int32, (blocks, width), 0)).astype(jnp.bfloat16)
    agree = lax.broadcasted_iota(jnp.int32, (both, width), 1) % both
    agree = (agree == lax.broadcasted_iota(jnp.int32, (both, width), 0))[None]
    entries = matmul(front_ref[...], repeat)
    turn_cos = cos_ref[...].reshape(low, 1, tokens)
    turn_sin = sin_ref[...].reshape(low, 1, tokens)

    def spread(part):
        part = jnp.where(agree, part.reshape(low, 1, width), 0.0)
        part = part.reshape(low * both, width).astype(jnp.bfloat16)
        return matmul(part, in_ref[...]).reshape(low, both, tokens)

    def flat(array):
        return array.reshape(-1, tokens).astype(jnp.bfloat16)

    real, imag = spread(entries[:low]), spread(entries[low:])
    turned_real = flat(real * turn_cos + imag * turn_sin)
    turned_imag = flat(imag * turn_cos - real * turn_sin)
    square_cos, square_sin = square_cos_ref[...], square_sin_ref[...]
    real = matmul(turned_real, square_cos) + matmul(turned_imag, square_sin)
    imag = matmul(turned_imag, square_cos) - matmul(turned_real, square_sin)
    real, imag = real.reshape(low, both, tokens), imag.reshape(low, both, tokens)
    sig_real, tap_real = real[:, :channels], real[:, channels:]
    sig_imag, tap_imag = imag[:, :channels], imag[:, channels:]
    prod_real = flat(sig_real * tap_real - sig_imag * tap_imag)
    prod_imag = flat(sig_real * tap_imag + sig_imag * tap_real)
    real = matmul(prod_real, square_cos) - matmul(prod_imag, square_sin)
    imag = matmul(prod_imag, square_cos) + matmul(prod_real, square_sin)
    real, imag = real.reshape(low, channels, tokens), imag.reshape(low, channels, tokens)
    half = low * channels
    rows_ref[:half, :] = (real * turn_cos - imag * turn_sin).reshape(half, tokens)
    rows_ref[half:, :] = (real * turn_sin + imag * turn_cos).reshape(half, tokens)
    out_ref[...] = matmul(back_ref[...], rows_ref[...].astype(jnp.bfloat16)).astype(out_ref.dtype)


def convolve(blocks_in, channels, tables, after):
    blocks, both, tokens = blocks_in.shape
    out = pl.pallas_call(
        lambda *refs: convolve_kernel(channels, *refs),
        out_shape=jax.ShapeDtypeStruct((blocks * channels, tokens), jnp.bfloat16),
        in_specs=[pl.BlockSpec(memory_space=pltpu.VMEM)] * (1 + len(tables))
        + [pl.BlockSpec(memory_space=pltpu.SMEM)],
        out_specs=pl.BlockSpec(memory_space=pltpu.VMEM),
        scratch_shapes=[pltpu.VMEM((2 * tables[-1].shape[0] * channels, tokens), jnp.float32)],
        compiler_params=pltpu.CompilerParams(vmem_limit_bytes=32 * MIB),
        cost_estimate=pl.CostEstimate(
            flops=800_000_000, bytes_accessed=3_000_000, transcendentals=0
        ),
    )(blocks_in.reshape(blocks * both, tokens), *tables, after)
    return out.reshape(blocks, channels, tokens)


def outgoing_kernel(devices, signal_hbm, gate_hbm, taps_hbm, out_ref, signal_ref, gate_ref, taps_ref, sems):
    copies = [
        pltpu.make_async_copy(source, target, sems.at[n])
        for n, (source, target) in enumerate(
            [(signal_hbm, signal_ref), (gate_hbm, gate_ref), (taps_hbm, taps_ref)]
        )
    ]
    for copy in copies:
        copy.start()
    for copy in copies:
        copy.wait()
    rows, tokens = signal_ref.shape
    gated = signal_ref[...].astype(jnp.float32) * gate_ref[...].astype(jnp.float32)
    both = jnp.concatenate(
        [
            gated.reshape(devices, rows // devices, tokens),
            taps_ref[...].reshape(devices, rows // devices, tokens),
        ],
        axis=1,
    )
    out_ref[...] = both.reshape(2 * rows, tokens).astype(out_ref.dtype)


def outgoing(signal, pre_gate, filter_taps, devices):
    rows, tokens = signal.shape
    out = pl.pallas_call(
        lambda *refs: outgoing_kernel(devices, *refs),
        out_shape=jax.ShapeDtypeStruct((2 * rows, tokens), jnp.bfloat16),
        in_specs=[pl.BlockSpec(memory_space=pltpu.HBM)] * 3,
        out_specs=pl.BlockSpec(memory_space=pltpu.VMEM),
        scratch_shapes=[
            pltpu.VMEM(signal.shape, signal.dtype),
            pltpu.VMEM(pre_gate.shape, pre_gate.dtype),
            pltpu.VMEM(filter_taps.shape, filter_taps.dtype),
            pltpu.SemaphoreType.DMA((3,)),
        ],
        compiler_params=pltpu.CompilerParams(vmem_limit_bytes=60 * MIB),
    )(signal, pre_gate, filter_taps)
    return out.reshape(devices, 2 * rows // devices, tokens)


def gate_kernel(post_ref, signal_ref, pre_ref, convolved_ref, gain_ref, after_ref, out_ref):
    del after_ref
    gated = signal_ref[...].astype(jnp.float32) * pre_ref[...].astype(jnp.float32)
    inner = convolved_ref[...].astype(jnp.float32) + gain_ref[...] * gated
    out_ref[...] = (post_ref[...].astype(jnp.float32) * inner).astype(out_ref.dtype).T


def gate(post_gate, signal, pre_gate, convolved, skip_gain, after):
    corners = jnp.concatenate([array[:16, :128] for array in after])
    return pl.pallas_call(
        gate_kernel,
        out_shape=jax.ShapeDtypeStruct(post_gate.shape[::-1], post_gate.dtype),
        in_specs=[pl.BlockSpec(memory_space=pltpu.VMEM)] * 6,
        out_specs=pl.BlockSpec(memory_space=pltpu.VMEM),
        compiler_params=pltpu.CompilerParams(vmem_limit_bytes=6 * MIB),
        cost_estimate=pl.CostEstimate(
            flops=5 * post_gate.size, bytes_accessed=10 * post_gate.size, transcendentals=0
        ),
    )(post_gate, signal, pre_gate, convolved, skip_gain[:, None], corners)


def exchange(parts, devices):
    return lax.all_to_all(
        parts,
        "ctx",
        split_axis=0,
        concat_axis=0,
        axis_index_groups=[exchange_order(devices)],
        tiled=True,
    )


def per_device(signal, pre_gate, post_gate, filter_taps, skip_gain, out_weight):
    channels_here, tokens_here = signal.shape
    devices = lax.axis_size("ctx")
    channels = channels_here // devices
    quads = lax.axis_size("quad")
    group = lax.axis_size("pair") * lax.axis_size("core")
    features = out_weight.shape[1]
    width = features // (quads * group)

    send = outgoing(signal, pre_gate, filter_taps, devices)
    blocks = exchange(send, devices)

    place = lax.axis_index(TP_AXES).astype(jnp.int32).reshape(1)
    members = [2, 3, 1]
    pieces, arranged = arrange(out_weight, place, group, quads, width, members)
    pieces = {
        r: lax.ppermute(piece, GROUP, [(t, t ^ r) for t in range(group)])
        for r, piece in zip(members, pieces)
    }
    pieces = [pieces[r] for r in range(1, group)]
    own = own_columns(out_weight, place, group, quads, width)
    tables = dft_tables(devices, tokens_here, channels)
    convolved = convolve(blocks, channels, tables, arranged)
    convolved = exchange(convolved, devices).reshape(channels_here, tokens_here)
    mixed = gate(post_gate, signal, pre_gate, convolved, skip_gain, pieces[1:] + pieces[:1])
    gathered = lax.all_gather(mixed, GROUP, axis=0, tiled=True)
    shares = project(place, gathered, [own] + pieces, width)
    return finish([send_to_target(shares[step], step, quads) for step in range(3)] + [shares[3]])


def solution(mesh):
    ctx, tp = mesh.devices.shape
    fine = Mesh(mesh.devices.reshape(ctx, tp // 4, 2, 2), ("ctx",) + TP_AXES)
    return jax.shard_map(
        per_device,
        mesh=fine,
        in_specs=(
            P(TP_AXES, "ctx"),
            P(TP_AXES, "ctx"),
            P(TP_AXES, "ctx"),
            P(TP_AXES, "ctx"),
            P(TP_AXES),
            P(TP_AXES, None),
        ),
        out_specs=P(TP_AXES, "ctx"),
        check_vma=False,
    )
```

```python
import math

import jax
import jax.numpy as jnp
import numpy as np
from jax import lax
from jax.experimental import pallas as pl
from jax.experimental.pallas import tpu as pltpu
from jax.sharding import Mesh
from jax.sharding import PartitionSpec as P

TP_AXES = ("quad", "pair", "core")
GROUP = ("pair", "core")
MIB = 1 << 20


def targets_of(quad, pair, core, quads):
    onward = 2 * pair - 1
    far = lax.rem(quad + 2 * onward + quads, quads)
    near = lax.rem(quad + onward + quads, quads)
    chips = [(far, 1 - pair), (near, pair), (near, 1 - pair), (quad, pair)]
    return [(q * 2 + p) * 2 + core for q, p in chips]


def send_to_target(share, step, quads):
    pairs = []
    for quad in range(quads):
        for pair in range(2):
            onward = 1 if pair == 1 else -1
            q = (quad + (2 * onward if step == 0 else onward)) % quads
            p = pair if step == 1 else 1 - pair
            pairs += [((quad * 2 + pair) * 2 + c, (q * 2 + p) * 2 + c) for c in range(2)]
    return lax.ppermute(share, TP_AXES, pairs)


def arrange_kernel(group, quads, width, members, place_ref, weight_ref, *refs):
    count = len(members) * group
    out_refs, done_ref, blocks, in_sems, out_sems = refs[: len(members)], *refs[-4:]
    tp = place_ref[0]
    quad, place = tp // group, lax.rem(tp, group)
    loads, stores = [], []
    for n, r in enumerate(members):
        other = place ^ r
        for i, target in enumerate(targets_of(quad, other // 2, lax.rem(other, 2), quads)):
            k = n * group + i
            start = pl.multiple_of(target * width, width)
            loads.append(
                pltpu.make_async_copy(
                    weight_ref.at[:, pl.ds(start, width)], blocks.at[k], in_sems.at[k]
                )
            )
            stores.append(
                pltpu.make_async_copy(
                    blocks.at[k], out_refs[n].at[:, pl.ds(i * width, width)], out_sems.at[k]
                )
            )
    for load in loads:
        load.start()
    for k in range(count):
        loads[k].wait()
        stores[k].start()
    for store in stores:
        store.wait()
    done_ref[0] = tp


def arrange(out_weight, place, group, quads, width, members):
    rows = out_weight.shape[0]
    count = len(members) * group
    piece = jax.ShapeDtypeStruct((rows, group * width), out_weight.dtype)
    *pieces, done = pl.pallas_call(
        lambda *refs: arrange_kernel(group, quads, width, members, *refs),
        out_shape=[piece] * len(members) + [jax.ShapeDtypeStruct((1,), jnp.int32)],
        in_specs=[
            pl.BlockSpec(memory_space=pltpu.SMEM),
            pl.BlockSpec(memory_space=pltpu.HBM),
        ],
        out_specs=[pl.BlockSpec(memory_space=pltpu.HBM)] * len(members)
        + [pl.BlockSpec(memory_space=pltpu.SMEM)],
        scratch_shapes=[
            pltpu.VMEM((count, rows, width), out_weight.dtype),
            pltpu.SemaphoreType.DMA((count,)),
            pltpu.SemaphoreType.DMA((count,)),
        ],
        compiler_params=pltpu.CompilerParams(vmem_limit_bytes=60 * MIB),
        cost_estimate=pl.CostEstimate(
            flops=0, bytes_accessed=4 * rows * count * width, transcendentals=0
        ),
    )(place, out_weight)
    return pieces, done


def own_columns_kernel(group, quads, width, place_ref, weight_ref, out_ref, sems):
    tp = place_ref[0]
    quad, place = tp // group, lax.rem(tp, group)
    copies = []
    for i, target in enumerate(targets_of(quad, place // 2, lax.rem(place, 2), quads)):
        start = pl.multiple_of(target * width, width)
        copies.append(
            pltpu.make_async_copy(
                weight_ref.at[:, pl.ds(start, width)],
                out_ref.at[:, pl.ds(i * width, width)],
                sems.at[i],
            )
        )
    for copy in copies:
        copy.start()
    for copy in copies:
        copy.wait()


def own_columns(out_weight, place, group, quads, width):
    rows = out_weight.shape[0]
    return pl.pallas_call(
        lambda *refs: own_columns_kernel(group, quads, width, *refs),
        out_shape=jax.ShapeDtypeStruct((rows, group * width), out_weight.dtype),
        in_specs=[
            pl.BlockSpec(memory_space=pltpu.SMEM),
            pl.BlockSpec(memory_space=pltpu.HBM),
        ],
        out_specs=pl.BlockSpec(memory_space=pltpu.VMEM),
        scratch_shapes=[pltpu.SemaphoreType.DMA((group,))],
        compiler_params=pltpu.CompilerParams(vmem_limit_bytes=60 * MIB),
        cost_estimate=pl.CostEstimate(
            flops=0, bytes_accessed=4 * rows * group * width, transcendentals=0
        ),
    )(place, out_weight)


def project_kernel(group, place_ref, mixed_ref, own_hbm, *refs):
    out_refs, own_ref, sems = refs[group - 1 : -2], refs[-2], refs[-1]
    step = own_ref.shape[1] // group
    loads = [
        pltpu.make_async_copy(
            own_hbm.at[:, pl.ds(i * step, step)], own_ref.at[:, pl.ds(i * step, step)], sems.at[i]
        )
        for i in range(group)
    ]
    for load in loads:
        load.start()
    weight_refs = (own_ref,) + refs[: group - 1]
    tokens = mixed_ref.shape[0] // group
    width = out_refs[0].shape[1]
    place = lax.rem(place_ref[0], group)
    mixed = [
        mixed_ref[pl.ds(pl.multiple_of((place ^ r) * tokens, tokens), tokens), :]
        for r in range(group)
    ]

    def product(r, i):
        weights = weight_refs[r][:, i * width : (i + 1) * width]
        return jnp.dot(mixed[r], weights, preferred_element_type=jnp.float32)

    totals = {}
    for i in range(group + 2):
        if i < group:
            totals[i] = sum(product(r, i) for r in range(1, group))
        if i >= 2:
            loads[i - 2].wait()
            total = totals.pop(i - 2) + product(0, i - 2)
            out_refs[i - 2][...] = total.astype(out_refs[i - 2].dtype)


def project(place, mixed, weights, width):
    group = len(weights)
    share = jax.ShapeDtypeStruct((mixed.shape[0] // group, width), mixed.dtype)
    return pl.pallas_call(
        lambda *refs: project_kernel(group, *refs),
        out_shape=[share] * group,
        in_specs=[pl.BlockSpec(memory_space=pltpu.SMEM)]
        + [pl.BlockSpec(memory_space=pltpu.VMEM), pl.BlockSpec(memory_space=pltpu.HBM)]
        + [pl.BlockSpec(memory_space=pltpu.VMEM)] * (group - 1),
        out_specs=[pl.BlockSpec(memory_space=pltpu.VMEM)] * group,
        scratch_shapes=[
            pltpu.VMEM(weights[0].shape, weights[0].dtype),
            pltpu.SemaphoreType.DMA((group,)),
        ],
        compiler_params=pltpu.CompilerParams(vmem_limit_bytes=10 * MIB),
        cost_estimate=pl.CostEstimate(
            flops=2 * mixed.size * group * width,
            bytes_accessed=2 * (mixed.size + sum(w.size for w in weights) + group * share.size),
            transcendentals=0,
        ),
    )(place, mixed, pltpu.with_memory_space_constraint(weights[0], pltpu.HBM), *weights[1:])


def finish_kernel(*refs):
    total = refs[0][...].astype(jnp.float32)
    for ref in refs[1:-1]:
        total = total + ref[...].astype(jnp.float32)
    refs[-1][...] = total.astype(refs[-1].dtype).T


def finish(shares):
    tokens, width = shares[0].shape
    return pl.pallas_call(
        finish_kernel,
        out_shape=jax.ShapeDtypeStruct((width, tokens), shares[0].dtype),
        in_specs=[pl.BlockSpec(memory_space=pltpu.VMEM)] * len(shares),
        out_specs=pl.BlockSpec(memory_space=pltpu.VMEM),
        compiler_params=pltpu.CompilerParams(vmem_limit_bytes=6 * MIB),
    )(*shares)


def dft_tables(blocks, tokens, channels):
    period = 2 * blocks
    total = period * tokens
    low = blocks + 1
    k1 = np.arange(low)
    i = np.arange(blocks)[::-1]
    s = np.arange(tokens)
    first = 2 * np.pi * (np.outer(k1, i) % period) / period
    turn = 2 * np.pi * (np.outer(k1, s) % total) / total
    square = 2 * np.pi * (np.outer(s, s) % tokens) / tokens
    front = np.concatenate([np.cos(first), -np.sin(first)])
    weight = np.where((k1 == 0) | (k1 == blocks), 1.0, 2.0)[:, None] / total
    back = np.concatenate(
        [
            np.kron((weight * np.cos(first)).T, np.eye(channels)),
            np.kron(-(weight * np.sin(first)).T, np.eye(channels)),
        ],
        axis=1,
    )
    matrices = [jnp.asarray(m, jnp.bfloat16) for m in (front, np.cos(square), np.sin(square), back)]
    turns = [jnp.asarray(m, jnp.float32) for m in (np.cos(turn), np.sin(turn))]
    return matrices + turns


def matmul(left, right):
    return jnp.dot(left, right, preferred_element_type=jnp.float32)


def convolve_kernel(
    channels, in_ref, front_ref, square_cos_ref, square_sin_ref, back_ref, cos_ref, sin_ref, after_ref, out_ref, rows_ref
):
    del after_ref
    low, tokens = cos_ref.shape
    both = 2 * channels
    blocks = front_ref.shape[1]
    width = blocks * both
    repeat = lax.broadcasted_iota(jnp.int32, (blocks, width), 1) // both
    repeat = (repeat == lax.broadcasted_iota(jnp.int32, (blocks, width), 0)).astype(jnp.bfloat16)
    agree = lax.broadcasted_iota(jnp.int32, (both, width), 1) % both
    agree = (agree == lax.broadcasted_iota(jnp.int32, (both, width), 0))[None]
    entries = matmul(front_ref[...], repeat)
    turn_cos = cos_ref[...].reshape(low, 1, tokens)
    turn_sin = sin_ref[...].reshape(low, 1, tokens)

    def spread(part):
        part = jnp.where(agree, part.reshape(low, 1, width), 0.0)
        part = part.reshape(low * both, width).astype(jnp.bfloat16)
        return matmul(part, in_ref[...]).reshape(low, both, tokens)

    def flat(array):
        return array.reshape(-1, tokens).astype(jnp.bfloat16)

    real, imag = spread(entries[:low]), spread(entries[low:])
    turned_real = flat(real * turn_cos + imag * turn_sin)
    turned_imag = flat(imag * turn_cos - real * turn_sin)
    square_cos, square_sin = square_cos_ref[...], square_sin_ref[...]
    real = matmul(turned_real, square_cos) + matmul(turned_imag, square_sin)
    imag = matmul(turned_imag, square_cos) - matmul(turned_real, square_sin)
    real, imag = real.reshape(low, both, tokens), imag.reshape(low, both, tokens)
    sig_real, tap_real = real[:, :channels], real[:, channels:]
    sig_imag, tap_imag = imag[:, :channels], imag[:, channels:]
    prod_real = flat(sig_real * tap_real - sig_imag * tap_imag)
    prod_imag = flat(sig_real * tap_imag + sig_imag * tap_real)
    real = matmul(prod_real, square_cos) - matmul(prod_imag, square_sin)
    imag = matmul(prod_imag, square_cos) + matmul(prod_real, square_sin)
    real, imag = real.reshape(low, channels, tokens), imag.reshape(low, channels, tokens)
    half = low * channels
    rows_ref[:half, :] = (real * turn_cos - imag * turn_sin).reshape(half, tokens)
    rows_ref[half:, :] = (real * turn_sin + imag * turn_cos).reshape(half, tokens)
    out_ref[...] = matmul(back_ref[...], rows_ref[...].astype(jnp.bfloat16)).astype(out_ref.dtype)


def convolve(blocks_in, channels, tables, after):
    blocks, both, tokens = blocks_in.shape
    out = pl.pallas_call(
        lambda *refs: convolve_kernel(channels, *refs),
        out_shape=jax.ShapeDtypeStruct((blocks * channels, tokens), jnp.bfloat16),
        in_specs=[pl.BlockSpec(memory_space=pltpu.VMEM)] * (1 + len(tables))
        + [pl.BlockSpec(memory_space=pltpu.SMEM)],
        out_specs=pl.BlockSpec(memory_space=pltpu.VMEM),
        scratch_shapes=[pltpu.VMEM((2 * tables[-1].shape[0] * channels, tokens), jnp.float32)],
        compiler_params=pltpu.CompilerParams(vmem_limit_bytes=32 * MIB),
        cost_estimate=pl.CostEstimate(
            flops=800_000_000, bytes_accessed=3_000_000, transcendentals=0
        ),
    )(blocks_in.reshape(blocks * both, tokens), *tables, after)
    return out.reshape(blocks, channels, tokens)


def outgoing_kernel(devices, signal_hbm, gate_hbm, taps_hbm, out_ref, signal_ref, gate_ref, taps_ref, sems):
    copies = [
        pltpu.make_async_copy(source, target, sems.at[n])
        for n, (source, target) in enumerate(
            [(signal_hbm, signal_ref), (gate_hbm, gate_ref), (taps_hbm, taps_ref)]
        )
    ]
    for copy in copies:
        copy.start()
    for copy in copies:
        copy.wait()
    rows, tokens = signal_ref.shape
    gated = signal_ref[...].astype(jnp.float32) * gate_ref[...].astype(jnp.float32)
    both = jnp.concatenate(
        [
            gated.reshape(devices, rows // devices, tokens),
            taps_ref[...].reshape(devices, rows // devices, tokens),
        ],
        axis=1,
    )
    out_ref[...] = both.reshape(2 * rows, tokens).astype(out_ref.dtype)


def outgoing(signal, pre_gate, filter_taps, devices):
    rows, tokens = signal.shape
    out = pl.pallas_call(
        lambda *refs: outgoing_kernel(devices, *refs),
        out_shape=jax.ShapeDtypeStruct((2 * rows, tokens), jnp.bfloat16),
        in_specs=[pl.BlockSpec(memory_space=pltpu.HBM)] * 3,
        out_specs=pl.BlockSpec(memory_space=pltpu.VMEM),
        scratch_shapes=[
            pltpu.VMEM(signal.shape, signal.dtype),
            pltpu.VMEM(pre_gate.shape, pre_gate.dtype),
            pltpu.VMEM(filter_taps.shape, filter_taps.dtype),
            pltpu.SemaphoreType.DMA((3,)),
        ],
        compiler_params=pltpu.CompilerParams(vmem_limit_bytes=60 * MIB),
    )(signal, pre_gate, filter_taps)
    return out.reshape(devices, 2 * rows // devices, tokens)


def gate_kernel(post_ref, signal_ref, pre_ref, convolved_ref, gain_ref, after_ref, out_ref):
    del after_ref
    gated = signal_ref[...].astype(jnp.float32) * pre_ref[...].astype(jnp.float32)
    inner = convolved_ref[...].astype(jnp.float32) + gain_ref[...] * gated
    out_ref[...] = (post_ref[...].astype(jnp.float32) * inner).astype(out_ref.dtype).T


def gate(post_gate, signal, pre_gate, convolved, skip_gain, after):
    corners = jnp.concatenate([array[:16, :128] for array in after])
    return pl.pallas_call(
        gate_kernel,
        out_shape=jax.ShapeDtypeStruct(post_gate.shape[::-1], post_gate.dtype),
        in_specs=[pl.BlockSpec(memory_space=pltpu.VMEM)] * 6,
        out_specs=pl.BlockSpec(memory_space=pltpu.VMEM),
        compiler_params=pltpu.CompilerParams(vmem_limit_bytes=6 * MIB),
        cost_estimate=pl.CostEstimate(
            flops=5 * post_gate.size, bytes_accessed=10 * post_gate.size, transcendentals=0
        ),
    )(post_gate, signal, pre_gate, convolved, skip_gain[:, None], corners)


def exchange(parts, devices):
    backwards = [list(range(devices))[::-1]]
    return lax.all_to_all(
        parts, "ctx", split_axis=0, concat_axis=0, axis_index_groups=backwards, tiled=True
    )


def per_device(signal, pre_gate, post_gate, filter_taps, skip_gain, out_weight):
    channels_here, tokens_here = signal.shape
    devices = lax.axis_size("ctx")
    channels = channels_here // devices
    quads = lax.axis_size("quad")
    group = lax.axis_size("pair") * lax.axis_size("core")
    features = out_weight.shape[1]
    width = features // (quads * group)

    send = outgoing(signal, pre_gate, filter_taps, devices)
    blocks = exchange(send, devices)

    place = lax.axis_index(TP_AXES).astype(jnp.int32).reshape(1)
    members = [2, 3, 1]
    pieces, arranged = arrange(out_weight, place, group, quads, width, members)
    pieces = {
        r: lax.ppermute(piece, GROUP, [(t, t ^ r) for t in range(group)])
        for r, piece in zip(members, pieces)
    }
    pieces = [pieces[r] for r in range(1, group)]
    own = own_columns(out_weight, place, group, quads, width)
    tables = dft_tables(devices, tokens_here, channels)
    convolved = convolve(blocks, channels, tables, arranged)
    convolved = exchange(convolved, devices).reshape(channels_here, tokens_here)
    mixed = gate(post_gate, signal, pre_gate, convolved, skip_gain, pieces[1:] + pieces[:1])
    gathered = lax.all_gather(mixed, GROUP, axis=0, tiled=True)
    shares = project(place, gathered, [own] + pieces, width)
    return finish([send_to_target(shares[step], step, quads) for step in range(3)] + [shares[3]])


def solution(mesh):
    ctx, tp = mesh.devices.shape
    fine = Mesh(mesh.devices.reshape(ctx, tp // 4, 2, 2), ("ctx",) + TP_AXES)
    return jax.shard_map(
        per_device,
        mesh=fine,
        in_specs=(
            P(TP_AXES, "ctx"),
            P(TP_AXES, "ctx"),
            P(TP_AXES, "ctx"),
            P(TP_AXES, "ctx"),
            P(TP_AXES),
            P(TP_AXES, None),
        ),
        out_specs=P(TP_AXES, "ctx"),
        check_vma=False,
    )
```
